32 devices in a mesh: wide: 8 (over z, x), narrow: 4 (over y, core).
Axes of the slice: x: 2, y: 2, z: 4, core: 2. Of those that a mesh axis runs over, the one named last changes fastest.
Arguments:
- tokens: bfloat16 [16384, 1024], P(('wide', 'narrow')), may hold values from -20 to 20
- lengths: int32 [16], P('wide'), may hold values from 128 to 1024, as said below
- norm_gain: float32 [1024], replicated, may hold values from 0.25 to 1.75
- w_query: bfloat16 [1024, 1024], P(None, 'narrow'), may hold values from -0.1875 to 0.1875
- w_key: bfloat16 [1024, 512], P(None, 'narrow'), may hold values from -0.1875 to 0.1875
- w_value: bfloat16 [1024, 512], P(None, 'narrow'), may hold values from -0.1875 to 0.1875
- query_scale: float32 [64], replicated, may hold values from 0.8 to 1.8
- key_scale: float32 [64], replicated, may hold values from 0.8 to 1.8
- w_out: bfloat16 [1024, 1024], P('narrow'), may hold values from -1.5 to 1.5
- ffn_gain: float32 [1024], replicated, may hold values from 0.25 to 1.75
- w_gate: bfloat16 [1024, 4608], P(None, 'narrow'), may hold values from -0.1875 to 0.1875
- w_up: bfloat16 [1024, 4608], P(None, 'narrow'), may hold values from -0.1875 to 0.1875
- w_down: bfloat16 [4608, 1024], P('narrow'), may hold values from -0.09375 to 0.09375
- cotangent: bfloat16 [16384, 1024], P(('wide', 'narrow')), may hold values from -6 to 6
Outputs:
- output: bfloat16 [16384, 1024], P(('wide', 'narrow'))
- tokens_grad: float32 [16384, 1024], P(('wide', 'narrow'))
- norm_gain_grad: float32 [1024], replicated
- query_grad: float32 [1024, 1024], P(None, 'narrow')
- key_grad: float32 [1024, 512], P(None, 'narrow')
- value_grad: float32 [1024, 512], P(None, 'narrow')
- query_scale_grad: float32 [64], replicated
- key_scale_grad: float32 [64], replicated
- out_grad: float32 [1024, 1024], P('narrow')
- ffn_gain_grad: float32 [1024], replicated
- gate_grad: float32 [1024, 4608], P(None, 'narrow')
- up_grad: float32 [1024, 4608], P(None, 'narrow')
- down_grad: float32 [4608, 1024], P('narrow')
The draws below stay inside these ranges and needn't reach their ends.
Inputs may be any that keep to these rules, and one draw needn't show every extreme that they name: `lengths`: slots of a sequence at or past its length are padding. Some sequence has exactly 1024 in every draw.
All inputs are finite; a program needn't handle non-finite values.
Results may differ from the reference program's by a relative error of at most 0.02.
Values may be sent and summed in bfloat16 or wider, within the bound.
A program may use at most 192 MiB of HBM per device.

```python
import math
import jax
import jax.numpy as jnp
from jax import lax

D = 1024
H = 16
KV = 8
HD = 64
FF = 4608
LEN = 1024
SEQ_DEV = 2
SEQS = 16
TOKENS = 16384
N_WIDE = 8


def draw_tokens(key, part):
    key = jax.random.fold_in(key, 11)
    base_key, scale_key = jax.random.split(key)
    base = jnp.clip(jax.random.normal(base_key, (TOKENS, D), jnp.float32), -5.0, 5.0)
    scales = jnp.exp(jax.random.uniform(scale_key, (TOKENS, 1), jnp.float32, math.log(0.5), math.log(4.0)))
    return (base * scales).astype(jnp.bfloat16)


def draw_lengths(key, part):
    key = jax.random.fold_in(key, 23)
    length_key, pick_key = jax.random.split(key)
    drawn = jax.random.randint(length_key, (SEQS,), LEN // 8, LEN + 1)
    chosen = jax.random.randint(pick_key, (), 0, SEQS)
    return jnp.where(jnp.arange(SEQS) == chosen, LEN, drawn).astype(jnp.int32)


def level_of(stream_key, extent, pieces, smallest, high):
    def one(dim, blocks):
        heights = jax.random.uniform(jax.random.fold_in(jax.random.fold_in(stream_key, 6), dim), (blocks,), jnp.float32, smallest / len(pieces), high / len(pieces))
        return jnp.repeat(jnp.exp(heights), extent[dim] // blocks).reshape((-1,) + (1,) * (len(extent) - dim - 1))

    loudness = one(*pieces[0])
    for cut in pieces[1:]:
        loudness = loudness * one(*cut)
    return loudness


def normal_values(own_key, dims, spread, limit, cuts=(), kind=jnp.bfloat16):
    level = level_of(own_key, dims, cuts, -0.22, 0.18) if cuts else 1.0
    array = jax.random.normal(own_key, dims, jnp.float32) * spread * level
    return jnp.minimum(jnp.maximum(array, -limit), limit).astype(kind)


def setup_inputs(seed: int = 0) -> dict:
    seeds = jax.random.split(jax.random.key(seed), 15)
    return {
        "tokens": draw_tokens(jax.random.fold_in(seeds[14], 71), 0),
        "lengths": draw_lengths(jax.random.fold_in(seeds[14], 71), 0),
        "norm_gain": jnp.clip(1.0 + 0.15 * jax.random.normal(seeds[2], (D,), jnp.float32), 0.25, 1.75),
        "w_query": normal_values(seeds[3], (D, H * HD), D ** -0.5, 0.1875, ((1, 4),)),
        "w_key": normal_values(seeds[4], (D, KV * HD), D ** -0.5, 0.1875, ((1, 4),)),
        "w_value": normal_values(seeds[5], (D, KV * HD), D ** -0.5, 0.1875, ((1, 4),)),
        "query_scale": jnp.clip(jax.random.uniform(seeds[6], (HD,), jnp.float32, 0.8, 1.8), 0.8, 1.8),
        "key_scale": jnp.clip(jax.random.uniform(seeds[7], (HD,), jnp.float32, 0.8, 1.8), 0.8, 1.8),
        "w_out": normal_values(seeds[8], (H * HD, D), (max(H * HD // 64, 16)) ** -0.5, 1.5, ((0, 4),)),
        "ffn_gain": jnp.clip(1.0 + 0.15 * jax.random.normal(seeds[9], (D,), jnp.float32), 0.25, 1.75),
        "w_gate": normal_values(seeds[10], (D, FF), D ** -0.5, 0.1875, ((1, 4),)),
        "w_up": normal_values(seeds[11], (D, FF), D ** -0.5, 0.1875, ((1, 4),)),
        "w_down": normal_values(seeds[12], (FF, D), FF ** -0.5, 0.09375, ((0, 4),)),
        "cotangent": normal_values(seeds[13], (TOKENS, D), 1.0, 6.0, ((0, 32),)),
    }


EPSILON = 1e-05
ROPE_BASE = 1000000.0

@jax.custom_vjp
def low(v):
    return lax.optimization_barrier(v.astype(jnp.bfloat16)).astype(jnp.float32)

@jax.custom_vjp
def low_back(v):
    return v

def low_keep(v):
    return (low(v), None)

def low_pass(kept, grad):
    return (grad,)

def back_keep(v):
    return (v, None)

def back_low(kept, grad):
    return (low(grad),)
low.defvjp(low_keep, low_pass)
low_back.defvjp(back_keep, back_low)

def rope_tables(length, width):
    half_width = width // 2
    frequency = ROPE_BASE ** (-(2.0 * jnp.arange(half_width, dtype=jnp.float32)) / width)
    angles = jnp.arange(length, dtype=jnp.float32)[:, None] * frequency[None, :]
    return (jnp.cos(angles), jnp.sin(angles))

def rotate(values_in, cosine, sine):
    half_width = values_in.shape[-1] // 2
    front_half = values_in[..., :half_width]
    back_half = values_in[..., half_width:]
    cos_b = cosine[:, None, :]
    sin_b = sine[:, None, :]
    return jnp.concatenate([front_half * cos_b - back_half * sin_b, back_half * cos_b + front_half * sin_b], axis=-1)

def row_norm(values_in, gain_vec):
    inv_rms = lax.rsqrt(lax.optimization_barrier(jnp.mean(values_in * values_in, axis=-1, keepdims=True)) + EPSILON)
    return (values_in * inv_rms * gain_vec, inv_rms)

def causal_allowed(row_count, length):
    row_ids = jnp.arange(row_count)[:, None]
    col_ids = jnp.arange(row_count)[None, :]
    return (col_ids <= row_ids) & (col_ids < length)

def attend_seq(entries):
    queries, keys, values, length = entries
    highest_prec = lax.Precision.HIGHEST
    row_count = queries.shape[0]
    kv_count = keys.shape[1]
    grouped = queries.reshape(row_count, kv_count, -1, HD)
    scores = jnp.einsum('qkgd,skd->kgqs', grouped, keys, precision=highest_prec)
    scores = low_back(scores * (1.0 / math.sqrt(HD)))
    scores = jnp.where(causal_allowed(row_count, length), scores, -1e+30)
    highest = lax.optimization_barrier(jnp.max(scores, axis=-1, keepdims=True))
    exponent = jnp.exp(scores - highest)
    probabilities = low(exponent / lax.optimization_barrier(jnp.sum(exponent, axis=-1, keepdims=True)))
    mixed_rows = jnp.einsum('kgqs,skd->qkgd', probabilities, values, precision=highest_prec)
    return low(low_back(mixed_rows.reshape(row_count, -1, HD)))

def block_layer(field_in, weights, seq_lengths):
    norm_gain, w_query, w_key, w_value, query_scale, key_scale, w_out, ffn_gain, w_gate, w_up, w_down = weights
    highest_prec = lax.Precision.HIGHEST
    cosine, sine = rope_tables(LEN, HD)
    seq_count = seq_lengths.shape[0]
    normed_one = low(row_norm(field_in, norm_gain)[0])
    query_raw = low_back(jnp.dot(normed_one, w_query, precision=highest_prec))
    key_raw = low_back(jnp.dot(normed_one, w_key, precision=highest_prec))
    value_low = low(low_back(jnp.dot(normed_one, w_value, precision=highest_prec)))
    queries = low(rotate(row_norm(query_raw.reshape(seq_count, LEN, H, HD), query_scale)[0], cosine, sine))
    keys = low(rotate(row_norm(key_raw.reshape(seq_count, LEN, KV, HD), key_scale)[0], cosine, sine))
    value_heads = value_low.reshape(seq_count, LEN, KV, HD)
    attended = lax.map(jax.checkpoint(attend_seq), (queries, keys, value_heads, seq_lengths))
    mixed_heads = attended.reshape(seq_count * LEN, H * HD)
    residual_mid = field_in + low_back(jnp.dot(mixed_heads, w_out, precision=highest_prec))
    normed_two = low(row_norm(residual_mid, ffn_gain)[0])
    gate_pre = low_back(jnp.dot(normed_two, w_gate, precision=highest_prec))
    up_pre = low_back(jnp.dot(normed_two, w_up, precision=highest_prec))
    hidden = low(jax.nn.silu(gate_pre) * up_pre)
    return residual_mid + low_back(jnp.dot(hidden, w_down, precision=highest_prec))

def reference(tokens, lengths, norm_gain, w_query, w_key, w_value, query_scale, key_scale, w_out, ffn_gain, w_gate, w_up, w_down, cotangent):
    params = (norm_gain, w_query, w_key, w_value, query_scale, key_scale, w_out, ffn_gain, w_gate, w_up, w_down)
    params = tuple((entry.astype(jnp.float32) for entry in params))
    group_rows = SEQ_DEV * LEN
    blocks = tokens.astype(jnp.float32).reshape(N_WIDE, group_rows, D)
    cotan_blocks = cotangent.astype(jnp.float32).reshape(N_WIDE, group_rows, D)
    length_blocks = lengths.reshape(N_WIDE, SEQ_DEV)

    def scan_step(totals, entries):
        block_in, cotan_block, seq_lengths = entries

        def forward(field_in, *weights):
            return block_layer(field_in, weights, seq_lengths)
        result, pullback = jax.vjp(forward, block_in, *params)
        gradients = pullback(cotan_block)
        totals = tuple((left + right for left, right in zip(totals, gradients[1:])))
        return (totals, (result.astype(jnp.bfloat16), gradients[0]))
    starts = tuple((jnp.zeros_like(entry) for entry in params))
    totals, (results, input_grads) = lax.scan(scan_step, starts, (blocks, cotan_blocks, length_blocks))
    return (results.reshape(TOKENS, D), input_grads.reshape(TOKENS, D), totals[0], totals[1], totals[2], totals[3], totals[4], totals[5], totals[6], totals[7], totals[8], totals[9], totals[10])
```

```python
import functools
import math

import jax
import jax.numpy as jnp
from jax import lax
from jax.experimental import pallas as pl
from jax.experimental.pallas import tpu as pltpu
from jax.sharding import PartitionSpec as P

HD = 64
LEN = 1024
BLK = 256
TILE = 2 * HD

EPSILON = 1e-05
ROPE_BASE = 1000000.0
F32 = jnp.float32
BF16 = jnp.bfloat16
VMEM_LIMIT = 48 * 1024 * 1024


def rope_tables(length, width):
    half_width = width // 2
    frequency = ROPE_BASE ** (-(2.0 * jnp.arange(half_width, dtype=jnp.float32)) / width)
    angles = jnp.arange(length, dtype=jnp.float32)[:, None] * frequency[None, :]
    return (jnp.cos(angles), jnp.sin(angles))


def row_norm(values_in, gain_vec):
    inv_rms = lax.rsqrt(jnp.mean(values_in * values_in, axis=-1, keepdims=True) + EPSILON)
    return (values_in * inv_rms * gain_vec, inv_rms)


def row_norm_back(values_in, inv_rms, gain_vec, grad_in):
    scaled = grad_in * gain_vec
    back_part = inv_rms * scaled - values_in * (inv_rms * inv_rms * inv_rms) * jnp.mean(
        values_in * scaled, axis=-1, keepdims=True
    )
    gain_part = jnp.sum((grad_in * values_in * inv_rms).reshape(-1, values_in.shape[-1]), axis=0)
    return (back_part, gain_part)


def contract(left_side, right_side, left_dim, right_dim):
    return lax.dot_general(
        left_side,
        right_side,
        (((left_dim,), (right_dim,)), ((), ())),
        preferred_element_type=F32,
    )


def lanes(shape):
    return lax.broadcasted_iota(jnp.int32, shape, 1)


def group_ones():
    rows = lax.broadcasted_iota(jnp.int32, (TILE, TILE), 0) // HD
    cols = lax.broadcasted_iota(jnp.int32, (TILE, TILE), 1) // HD
    return jnp.where(rows == cols, 1.0, 0.0).astype(BF16)


def group_sum(values_in, ones):
    high = values_in.astype(BF16)
    rest = (values_in - high.astype(F32)).astype(BF16)
    return contract(high, ones, 1, 0) + contract(rest, ones, 1, 0)


def swap_halves(values_in):
    half = HD // 2
    front = lax.rem(lanes(values_in.shape), HD) < half
    return jnp.where(
        front, pltpu.roll(values_in, TILE - half, 1), pltpu.roll(values_in, half, 1)
    )


def attention_forward(
    len_ref, x_ref, wq_ref, wk_ref, wv_ref, qs_ref, ks_ref, cos_ref, sin_ref,
    att_ref, q_ref, k_ref, v_ref, qraw_ref, kraw_ref, rinv_ref,
    vaug_ref,
):
    length = len_ref[0]
    heads = wk_ref.shape[1] // HD
    ones = group_ones()

    def norm_rope(raw, scale, cosine, sine):
        inv = lax.rsqrt(group_sum(raw * raw, ones) * (1.0 / HD) + EPSILON)
        scaled = raw * inv * scale
        return scaled * cosine + swap_halves(scaled) * sine

    for start in range(0, LEN, BLK):
        rows = slice(start, start + BLK)
        x = x_ref[rows, :]
        cosine, sine = cos_ref[rows, :], sin_ref[rows, :]
        real = (lax.broadcasted_iota(jnp.int32, (BLK, TILE), 0) + start) < length
        q_raw = contract(x, wq_ref[...], 1, 0)
        qraw_ref[rows, :] = q_raw
        for t in range(heads):
            cols = slice(t * TILE, (t + 1) * TILE)
            turned = norm_rope(q_raw[:, cols], qs_ref[...], cosine, sine)
            q_ref[rows, cols] = (turned * (1.0 / math.sqrt(HD))).astype(BF16)
        k_raw = contract(x, wk_ref[...], 1, 0)
        kraw_ref[rows, :] = k_raw
        v_raw = contract(x, wv_ref[...], 1, 0)
        for t in range(heads // 2):
            cols = slice(t * TILE, (t + 1) * TILE)
            turned = norm_rope(k_raw[:, cols], ks_ref[...], cosine, sine)
            k_ref[rows, cols] = jnp.where(real, turned, 0.0).astype(BF16)
            v_pair = jnp.where(real, v_raw[:, cols], 0.0)
            v_ref[rows, cols] = v_pair.astype(BF16)
            lane = lanes((BLK, TILE))
            mark = jnp.where(real & (lane == HD), 1.0, 0.0)
            vaug_ref[2 * t, rows, :] = jnp.where(lane < HD, v_pair, mark).astype(BF16)
            vaug_ref[2 * t + 1, rows, :] = jnp.where(
                lane < HD, pltpu.roll(v_pair, HD, 1), mark
            ).astype(BF16)

    row_ids = lax.rem(lax.broadcasted_iota(jnp.int32, (2 * BLK, BLK), 0), BLK)
    causal = lax.broadcasted_iota(jnp.int32, (2 * BLK, BLK), 1) <= row_ids
    for h in range(heads):
        for i in range(LEN // BLK):
            rows = slice(i * BLK, (i + 1) * BLK)
            low = h * TILE
            q_two = jnp.concatenate(
                [q_ref[rows, low : low + HD], q_ref[rows, low + HD : low + TILE]], axis=0
            )
            total = jnp.zeros((2 * BLK, TILE), F32)
            for j in range(i + 1):
                keys = slice(j * BLK, (j + 1) * BLK)
                scores = contract(q_two, k_ref[keys, h * HD : (h + 1) * HD], 1, 1)
                weight = jnp.exp(scores)
                if i == j:
                    weight = jnp.where(causal, weight, 0.0)
                total += contract(weight.astype(BF16), vaug_ref[h, keys, :], 1, 0)
            inv = 1.0 / total[:, HD : HD + 1]
            mixed = total[:, :HD] * inv
            att_ref[rows, low : low + HD] = mixed[:BLK].astype(BF16)
            att_ref[rows, low + HD : low + TILE] = mixed[BLK:].astype(BF16)
            rinv_ref[rows, low : low + HD] = jnp.broadcast_to(inv[:BLK], (BLK, HD))
            rinv_ref[rows, low + HD : low + TILE] = jnp.broadcast_to(inv[BLK:], (BLK, HD))


def attention_backward(
    len_ref, g_ref, wo_ref, q_ref, k_ref, v_ref, att_ref, qraw_ref, kraw_ref, rinv_ref,
    qs_ref, ks_ref, cos_ref, sin_ref,
    gq_ref, gk_ref, gv_ref, qsg_ref, ksg_ref,
    vaug_ref, aug_ref, dk_ref, dv_ref,
):
    length = len_ref[0]
    heads = k_ref.shape[1] // HD
    ones = group_ones()
    lane = lanes((BLK, TILE))

    for start in range(0, LEN, BLK):
        rows = slice(start, start + BLK)
        grad = contract(g_ref[rows, :], wo_ref[...], 1, 1).astype(BF16).astype(F32)
        for t in range(heads):
            cols = slice(t * TILE, (t + 1) * TILE)
            part = (grad[:, cols] * rinv_ref[rows, cols]).astype(BF16).astype(F32)
            inner = group_sum(part * att_ref[rows, cols].astype(F32), ones)
            for which in range(2):
                mine = part if which == 0 else pltpu.roll(part, HD, 1)
                sums = pltpu.roll(inner, HD, 1) if which == 0 else inner
                high = sums.astype(BF16).astype(F32)
                tail = jnp.where(
                    lane == HD, -high, jnp.where(lane == HD + 1, high - sums, 0.0)
                )
                aug_ref[2 * t + which, rows, :] = jnp.where(lane < HD, mine, tail).astype(BF16)
        for t in range(heads // 2):
            v_pair = v_ref[rows, t * TILE : (t + 1) * TILE].astype(F32)
            mark = jnp.where(lane < HD + 2, 1.0, 0.0)
            vaug_ref[2 * t, rows, :] = jnp.where(lane < HD, v_pair, mark).astype(BF16)
            vaug_ref[2 * t + 1, rows, :] = jnp.where(
                lane < HD, pltpu.roll(v_pair, HD, 1), mark
            ).astype(BF16)

    dk_ref[...] = jnp.zeros_like(dk_ref)
    dv_ref[...] = jnp.zeros_like(dv_ref)
    col_ids = lax.rem(lax.broadcasted_iota(jnp.int32, (BLK, 2 * BLK), 1), BLK)
    causal = lax.broadcasted_iota(jnp.int32, (BLK, 2 * BLK), 0) <= col_ids

    def turn_back(grad, cosine, sine):
        return grad * cosine - swap_halves(grad) * sine

    def norm_back(raw, turned, scale):
        inv = lax.rsqrt(group_sum(raw * raw, ones) * (1.0 / HD) + EPSILON)
        scaled = turned * scale
        unit = raw * inv
        inner = group_sum(unit * scaled, ones) * (1.0 / HD)
        gain = jnp.sum(turned * unit, axis=0, keepdims=True)
        return inv * (scaled - unit * inner), gain

    q_gain = jnp.zeros((1, TILE), F32)
    for h in range(heads):
        keys_turned = jnp.transpose(
            k_ref[:, (h // 2) * TILE : (h // 2 + 1) * TILE].astype(F32)
        )[(h % 2) * HD : (h % 2 + 1) * HD].astype(BF16)
        for i in range(LEN // BLK):
            rows = slice(i * BLK, (i + 1) * BLK)
            low = h * TILE
            q_two = jnp.concatenate(
                [q_ref[rows, low : low + HD], q_ref[rows, low + HD : low + TILE]], axis=0
            )
            aug = jnp.concatenate([aug_ref[2 * h, rows, :], aug_ref[2 * h + 1, rows, :]], axis=0)
            dq = jnp.zeros((HD, 2 * BLK), F32)
            for j in range(i + 1):
                keys = slice(j * BLK, (j + 1) * BLK)
                weight = jnp.exp(contract(k_ref[keys, h * HD : (h + 1) * HD], q_two, 1, 1))
                if i == j:
                    weight = jnp.where(causal, weight, 0.0)
                slope = (weight * contract(vaug_ref[h, keys, :], aug, 1, 1)).astype(BF16)
                dv_ref[h, keys, :] += contract(weight.astype(BF16), aug, 1, 0)
                dk_ref[h, keys, :] += contract(slope, q_two, 1, 0)
                dq += contract(keys_turned[:, keys], slope, 1, 0)
            both = jnp.concatenate([dq[:, :BLK], dq[:, BLK:]], axis=0)
            grad = jnp.transpose(both) * (1.0 / math.sqrt(HD))
            cols = slice(low, low + TILE)
            turned = turn_back(grad, cos_ref[rows, :], sin_ref[rows, :])
            out, gain = norm_back(qraw_ref[rows, cols], turned, qs_ref[...])
            gq_ref[rows, cols] = out.astype(BF16)
            q_gain += gain
    qsg_ref[...] = q_gain

    k_gain = jnp.zeros((1, TILE), F32)
    for start in range(0, LEN, BLK):
        rows = slice(start, start + BLK)
        real = (lax.broadcasted_iota(jnp.int32, (BLK, TILE), 0) + start) < length
        for t in range(heads // 2):
            cols = slice(t * TILE, (t + 1) * TILE)
            grad = jnp.concatenate([dk_ref[2 * t, rows, :], dk_ref[2 * t + 1, rows, :]], axis=1)
            grad = jnp.where(real, grad, 0.0)
            turned = turn_back(grad, cos_ref[rows, :], sin_ref[rows, :])
            out, gain = norm_back(kraw_ref[rows, cols], turned, ks_ref[...])
            gk_ref[rows, cols] = out.astype(BF16)
            k_gain += gain
            values = jnp.where(
                lane < HD, dv_ref[2 * t, rows, :], pltpu.roll(dv_ref[2 * t + 1, rows, :], HD, 1)
            )
            gv_ref[rows, cols] = jnp.where(real, values, 0.0).astype(BF16)
    ksg_ref[...] = k_gain


VM = pl.BlockSpec(memory_space=pltpu.VMEM)
SM = pl.BlockSpec(memory_space=pltpu.SMEM)


def run_forward(length, rows, wq, wk, wv, qs, ks, cosine, sine):
    nq, nk = wq.shape[1], wk.shape[1]
    shape = jax.ShapeDtypeStruct
    return pl.pallas_call(
        attention_forward,
        out_shape=(
            shape((LEN, nq), BF16),
            shape((LEN, nq), BF16),
            shape((LEN, nk), BF16),
            shape((LEN, nk), BF16),
            shape((LEN, nq), F32),
            shape((LEN, nk), F32),
            shape((LEN, nq), F32),
        ),
        in_specs=[SM] + [VM] * 8,
        out_specs=[VM] * 7,
        scratch_shapes=[pltpu.VMEM((nk // HD, LEN, TILE), BF16)],
        compiler_params=pltpu.CompilerParams(vmem_limit_bytes=VMEM_LIMIT),
        cost_estimate=pl.CostEstimate(
            flops=2 * LEN * rows.shape[1] * 2 * nq + 8 * LEN * LEN * nq,
            bytes_accessed=8 * 1024 * 1024,
            transcendentals=0,
        ),
        name="attention_forward",
    )(length, rows, wq, wk, wv, qs, ks, cosine, sine)


def run_backward(length, grads, wo, q, k, v, att, q_raw, k_raw, rinv, qs, ks, cosine, sine):
    nq, nk = q.shape[1], k.shape[1]
    heads = nk // HD
    shape = jax.ShapeDtypeStruct
    return pl.pallas_call(
        attention_backward,
        out_shape=(
            shape((LEN, nq), BF16),
            shape((LEN, nk), BF16),
            shape((LEN, nk), BF16),
            shape((1, TILE), F32),
            shape((1, TILE), F32),
        ),
        in_specs=[SM] + [VM] * 13,
        out_specs=[VM] * 5,
        scratch_shapes=[
            pltpu.VMEM((heads, LEN, TILE), BF16),
            pltpu.VMEM((2 * heads, LEN, TILE), BF16),
            pltpu.VMEM((heads, LEN, HD), F32),
            pltpu.VMEM((heads, LEN, TILE), F32),
        ],
        compiler_params=pltpu.CompilerParams(vmem_limit_bytes=VMEM_LIMIT),
        cost_estimate=pl.CostEstimate(
            flops=2 * LEN * grads.shape[1] * nq + 24 * LEN * LEN * nq,
            bytes_accessed=8 * 1024 * 1024,
            transcendentals=0,
        ),
        name="attention_backward",
    )(length, grads, wo, q, k, v, att, q_raw, k_raw, rinv, qs, ks, cosine, sine)


def ring_order(count):
    side = 2 ** (int(math.log2(count)) // 2) if count > 1 else 1
    tall = count // side
    order = [0]
    for col in range(tall):
        steps = range(1, side) if col % 2 == 0 else range(side - 1, 0, -1)
        order += [col * side + s for s in steps]
    order += [col * side for col in range(tall - 1, 0, -1)]
    return order


def on_device(
    wide, narrow,
    tokens, lengths, norm_gain, w_query, w_key, w_value, query_scale, key_scale, w_out,
    ffn_gain, w_gate, w_up, w_down, cotangent,
):
    sequences = lengths.shape[0]
    side = narrow // sequences
    own = tokens.shape[0]
    me = lax.axis_index("narrow")
    place, mine = lax.rem(me, side), me // side

    def across(array, turn=1):
        return lax.ppermute(
            array, "narrow", [(i, (i + turn * side) % narrow) for i in range(narrow)]
        )

    def within(array, turn):
        return lax.ppermute(
            array,
            "narrow",
            [(i, (i // side) * side + (i % side + turn) % side) for i in range(narrow)],
        )

    def gather(array):
        size = array.shape[0]
        whole = jnp.zeros((side * size,) + array.shape[1:], array.dtype)
        whole = lax.dynamic_update_slice(whole, array, (place * size, 0))
        for turn in range(1, side):
            source = lax.rem(place + side - turn, side)
            whole = lax.dynamic_update_slice(whole, within(array, turn), (source * size, 0))
        return whole

    def scatter(parts):
        size = parts.shape[0] // side
        total = lax.dynamic_slice_in_dim(parts, place * size, size).astype(F32)
        for turn in range(1, side):
            target = lax.rem(place + turn, side)
            total += within(
                lax.dynamic_slice_in_dim(parts, target * size, size).astype(BF16), turn
            ).astype(F32)
        return total

    cosine, sine = rope_tables(LEN, HD)
    cosine = jnp.concatenate([cosine] * 4, axis=1)
    sine = jnp.concatenate([-sine, sine, -sine, sine], axis=1)
    qs = jnp.concatenate([query_scale] * 2)[None, :]
    ks = jnp.concatenate([key_scale] * 2)[None, :]
    length = lax.dynamic_slice_in_dim(lengths, mine, 1)

    weights = [(w_query, w_key, w_value, w_out)]
    weights += [tuple(across(w, t) for w in weights[0]) for t in range(1, sequences)]
    joined = w_key.shape[1] % TILE != 0
    if joined:
        weights = [
            tuple(jnp.concatenate(ws, axis=1 if n < 3 else 0) for n, ws in enumerate(zip(*weights)))
        ]

    residual = tokens.astype(F32)
    normed_one, inv_one = row_norm(residual, norm_gain)
    rows_one = gather(normed_one.astype(BF16))
    saved = [run_forward(length, rows_one, *w[:3], qs, ks, cosine, sine) for w in weights]
    mixed = contract(saved[0][0], weights[0][3], 1, 0)
    for s, w in zip(saved[1:], weights[1:]):
        mixed += contract(s[0], w[3], 1, 0)
    middle = residual + scatter(mixed)

    normed_two, inv_two = row_norm(middle, ffn_gain)
    low_two = normed_two.astype(BF16)

    blocks = []
    for turn in range(sequences):
        rows = gather(across(low_two, turn) if turn else low_two)
        grads = gather(across(cotangent, turn) if turn else cotangent)
        gate_pre = contract(rows, w_gate, 1, 0)
        up_pre = contract(rows, w_up, 1, 0)
        sigmoid_gate = jax.nn.sigmoid(gate_pre)
        hidden = (gate_pre * sigmoid_gate * up_pre).astype(BF16)
        grad_hidden = contract(grads, w_down, 1, 1)
        grad_gate = (
            grad_hidden * up_pre * sigmoid_gate * (1.0 + gate_pre * (1.0 - sigmoid_gate))
        ).astype(BF16)
        grad_up = (grad_hidden * gate_pre * sigmoid_gate).astype(BF16)
        back = contract(grad_gate, w_gate, 1, 1) + contract(grad_up, w_up, 1, 1)
        blocks.append((rows, grads, hidden, grad_gate, grad_up, back))

    def to_owners(parts):
        total = scatter(parts[0])
        for turn in range(1, sequences):
            total += across(scatter(parts[turn]).astype(BF16), sequences - turn).astype(F32)
        return total

    grad_normed_two = to_owners([b[5] for b in blocks])
    rows_two, grad_rows, hidden, grad_gate, grad_up = (
        jnp.concatenate([b[n] for b in blocks], axis=0) for n in range(5)
    )
    output = middle + to_owners([contract(b[2], w_down, 1, 0) for b in blocks])
    grad_down = contract(hidden, grad_rows, 0, 0).astype(BF16)
    grad_w_gate = contract(rows_two, grad_gate, 0, 0).astype(BF16)
    grad_w_up = contract(rows_two, grad_up, 0, 0).astype(BF16)

    back_two, gain_two = row_norm_back(middle, inv_two, ffn_gain, grad_normed_two)
    grad_middle = cotangent.astype(F32) + back_two
    branch = gather(grad_middle.astype(BF16))

    q_gain, k_gain = 0.0, 0.0
    back_one = 0.0
    weight_grads = []
    for s, (wq, wk, wv, wo) in zip(saved, weights):
        att, q, k, v, q_raw, k_raw, rinv = s
        gq, gk, gv, qg, kg = run_backward(
            length, branch, wo, q, k, v, att, q_raw, k_raw, rinv, qs, ks, cosine, sine
        )
        q_gain += qg[0, :HD] + qg[0, HD:]
        k_gain += kg[0, :HD] + kg[0, HD:]
        back_one += contract(gq, wq, 1, 1) + contract(gk, wk, 1, 1) + contract(gv, wv, 1, 1)
        weight_grads.append(
            (
                contract(rows_one, gq, 0, 0),
                contract(rows_one, gk, 0, 0),
                contract(rows_one, gv, 0, 0),
                contract(att, branch, 0, 0),
            )
        )
    if joined:
        weight_grads = [
            tuple(
                jnp.split(w, sequences, axis=1 if n < 3 else 0)[p]
                for n, w in enumerate(weight_grads[0])
            )
            for p in range(sequences)
        ]
    own_grads = list(weight_grads[0])
    for turn in range(1, sequences):
        for n in range(4):
            own_grads[n] += across(weight_grads[turn][n].astype(BF16), sequences - turn).astype(F32)
    grad_normed_one = scatter(back_one)
    back_one, gain_one = row_norm_back(residual, inv_one, norm_gain, grad_normed_one)
    grad_tokens = grad_middle + back_one

    grad_down, grad_w_gate, grad_w_up = lax.psum((grad_down, grad_w_gate, grad_w_up), "wide")
    grad_down, grad_w_gate, grad_w_up, *own_grads = lax.optimization_barrier(
        (grad_down, grad_w_gate, grad_w_up, *own_grads)
    )
    summed = lax.psum(tuple(g.astype(BF16) for g in own_grads), "wide")
    gain_summed = lax.psum((gain_one, gain_two, q_gain, k_gain), ("wide", "narrow"))
    return (
        output.astype(BF16),
        grad_tokens,
        gain_summed[0],
        summed[0].astype(F32),
        summed[1].astype(F32),
        summed[2].astype(F32),
        gain_summed[2],
        gain_summed[3],
        summed[3].astype(F32),
        gain_summed[1],
        grad_w_gate.astype(F32),
        grad_w_up.astype(F32),
        grad_down.astype(F32),
    )


def solution(mesh):
    rows = P(("wide", "narrow"), None)
    columns, depth, copied = P(None, "narrow"), P("narrow", None), P()
    return jax.shard_map(
        functools.partial(on_device, mesh.shape["wide"], mesh.shape["narrow"]),
        mesh=mesh,
        in_specs=(
            rows, P("wide"), copied, columns, columns, columns, copied, copied, depth,
            copied, columns, columns, depth, rows,
        ),
        out_specs=(
            rows, rows, copied, columns, columns, columns, copied, copied, depth,
            copied, columns, columns, depth,
        ),
        check_vma=False,
    )
```

```python
import functools
import math

import jax
import jax.numpy as jnp
from jax import lax
from jax.experimental import pallas as pl
from jax.experimental.pallas import tpu as pltpu
from jax.sharding import PartitionSpec as P

HD = 64
LEN = 1024
BLK = 256
TILE = 2 * HD

EPSILON = 1e-05
ROPE_BASE = 1000000.0
F32 = jnp.float32
BF16 = jnp.bfloat16
VMEM_LIMIT = 48 * 1024 * 1024
BACK_LIMIT = 60 * 1024 * 1024


def rope_tables(length, width):
    half_width = width // 2
    frequency = ROPE_BASE ** (-(2.0 * jnp.arange(half_width, dtype=jnp.float32)) / width)
    angles = jnp.arange(length, dtype=jnp.float32)[:, None] * frequency[None, :]
    return (jnp.cos(angles), jnp.sin(angles))


def row_norm(values_in, gain_vec):
    inv_rms = lax.rsqrt(jnp.mean(values_in * values_in, axis=-1, keepdims=True) + EPSILON)
    return (values_in * inv_rms * gain_vec, inv_rms)


def row_norm_back(values_in, inv_rms, gain_vec, grad_in):
    scaled = grad_in * gain_vec
    back_part = inv_rms * scaled - values_in * (inv_rms * inv_rms * inv_rms) * jnp.mean(
        values_in * scaled, axis=-1, keepdims=True
    )
    gain_part = jnp.sum((grad_in * values_in * inv_rms).reshape(-1, values_in.shape[-1]), axis=0)
    return (back_part, gain_part)


def contract(left_side, right_side, left_dim, right_dim):
    return lax.dot_general(
        left_side,
        right_side,
        (((left_dim,), (right_dim,)), ((), ())),
        preferred_element_type=F32,
    )


def lanes(shape):
    return lax.broadcasted_iota(jnp.int32, shape, 1)


def group_ones():
    rows = lax.broadcasted_iota(jnp.int32, (TILE, TILE), 0) // HD
    cols = lax.broadcasted_iota(jnp.int32, (TILE, TILE), 1) // HD
    return jnp.where(rows == cols, 1.0, 0.0).astype(BF16)


def group_sum(values_in, ones):
    high = values_in.astype(BF16)
    rest = (values_in - high.astype(F32)).astype(BF16)
    return contract(high, ones, 1, 0) + contract(rest, ones, 1, 0)


def swap_halves(values_in):
    half = HD // 2
    front = lax.rem(lanes(values_in.shape), HD) < half
    return jnp.where(
        front, pltpu.roll(values_in, TILE - half, 1), pltpu.roll(values_in, half, 1)
    )


def attention_forward(
    len_ref, x_ref, wq_ref, wk_ref, wv_ref, qs_ref, ks_ref, cos_ref, sin_ref,
    att_ref, q_ref, k_ref, v_ref, qraw_ref, kraw_ref, rinv_ref,
    vaug_ref,
):
    length = len_ref[0]
    heads = wk_ref.shape[1] // HD
    ones = group_ones()

    def norm_rope(raw, scale, cosine, sine):
        inv = lax.rsqrt(group_sum(raw * raw, ones) * (1.0 / HD) + EPSILON)
        scaled = raw * inv * scale
        return scaled * cosine + swap_halves(scaled) * sine

    for start in range(0, LEN, BLK):
        rows = slice(start, start + BLK)
        x = x_ref[rows, :]
        cosine, sine = cos_ref[rows, :], sin_ref[rows, :]
        real = (lax.broadcasted_iota(jnp.int32, (BLK, TILE), 0) + start) < length
        q_raw = contract(x, wq_ref[...], 1, 0)
        qraw_ref[rows, :] = q_raw
        for t in range(heads):
            cols = slice(t * TILE, (t + 1) * TILE)
            turned = norm_rope(q_raw[:, cols], qs_ref[...], cosine, sine)
            q_ref[rows, cols] = (turned * (1.0 / math.sqrt(HD))).astype(BF16)
        k_raw = contract(x, wk_ref[...], 1, 0)
        kraw_ref[rows, :] = k_raw
        v_raw = contract(x, wv_ref[...], 1, 0)
        for t in range(heads // 2):
            cols = slice(t * TILE, (t + 1) * TILE)
            turned = norm_rope(k_raw[:, cols], ks_ref[...], cosine, sine)
            k_ref[rows, cols] = jnp.where(real, turned, 0.0).astype(BF16)
            v_pair = jnp.where(real, v_raw[:, cols], 0.0)
            v_ref[rows, cols] = v_pair.astype(BF16)
            lane = lanes((BLK, TILE))
            mark = jnp.where(real & (lane == HD), 1.0, 0.0)
            vaug_ref[2 * t, rows, :] = jnp.where(lane < HD, v_pair, mark).astype(BF16)
            vaug_ref[2 * t + 1, rows, :] = jnp.where(
                lane < HD, pltpu.roll(v_pair, HD, 1), mark
            ).astype(BF16)

    row_ids = lax.rem(lax.broadcasted_iota(jnp.int32, (2 * BLK, BLK), 0), BLK)
    causal = lax.broadcasted_iota(jnp.int32, (2 * BLK, BLK), 1) <= row_ids
    for h in range(heads):
        for i in range(LEN // BLK):
            rows = slice(i * BLK, (i + 1) * BLK)
            low = h * TILE
            q_two = jnp.concatenate(
                [q_ref[rows, low : low + HD], q_ref[rows, low + HD : low + TILE]], axis=0
            )
            total = jnp.zeros((2 * BLK, TILE), F32)
            for j in range(i + 1):
                keys = slice(j * BLK, (j + 1) * BLK)
                scores = contract(q_two, k_ref[keys, h * HD : (h + 1) * HD], 1, 1)
                weight = jnp.exp(scores)
                if i == j:
                    weight = jnp.where(causal, weight, 0.0)
                total += contract(weight.astype(BF16), vaug_ref[h, keys, :], 1, 0)
            inv = 1.0 / total[:, HD : HD + 1]
            mixed = total[:, :HD] * inv
            att_ref[rows, low : low + HD] = mixed[:BLK].astype(BF16)
            att_ref[rows, low + HD : low + TILE] = mixed[BLK:].astype(BF16)
            rinv_ref[rows, low : low + HD] = jnp.broadcast_to(inv[:BLK], (BLK, HD))
            rinv_ref[rows, low + HD : low + TILE] = jnp.broadcast_to(inv[BLK:], (BLK, HD))


class Ring:
    def __init__(self, count, place, target, turn, chunk, first, rows, own, source, out, land, sends, recvs):
        self.count, self.place, self.target, self.turn = count, place, target, turn
        self.chunk, self.first, self.rows = chunk, first, rows
        self.own, self.source, self.out, self.land = own, source, out, land
        self.sends, self.recvs = sends, recvs
        self.done = 0

    def index(self, steps):
        return lax.rem(self.place + self.turn * steps + 2 * self.count, self.count)

    def part(self, ref, steps):
        start = pl.multiple_of(self.index(steps) * self.chunk + self.first, 16)
        return ref.at[pl.ds(start, self.rows), :]

    def copy(self, step, source, target):
        return pltpu.make_async_remote_copy(
            src_ref=source,
            dst_ref=target,
            send_sem=self.sends.at[step],
            recv_sem=self.recvs.at[step],
            device_id={"wide": self.target},
            device_id_type=pl.DeviceIdType.MESH,
        )

    def copy_of(self, step):
        last = self.count - 1
        if step == 0:
            return self.copy(0, self.part(self.source, 0), self.land.at[0])
        if step < last:
            return self.copy(step, self.land.at[step - 1], self.land.at[step])
        steps = last - step + 1
        where = self.part(self.out, steps)
        return self.copy(step, self.land.at[last - 1] if step == last else where, where)

    def begin(self):
        self.copy_of(0).start()

    @property
    def left(self):
        return 2 * (self.count - 1) - self.done

    def tick(self, keep):
        step, last = self.done, self.count - 1
        self.done += 1
        if step < last:
            slot = self.land.at[step]
            self.copy(step, slot, slot).wait_recv()
            start = pl.multiple_of(self.index(-step - 1) * self.chunk + self.first, 16)

            @pl.loop(0, self.rows // 16)
            def _(r):
                at = pl.multiple_of(r * 16, 16)
                mine = self.own[pl.ds(pl.multiple_of(start + at, 16), 16), :].astype(F32)
                slot[pl.ds(at, 16), :] = (slot[pl.ds(at, 16), :].astype(F32) + mine).astype(BF16)

            if step == last - 1:
                kept = pltpu.make_async_copy(slot, self.part(self.out, 1), keep)
                kept.start()
                self.copy_of(last).start()
                kept.wait()
            else:
                self.copy_of(step + 1).start()
        else:
            where = self.part(self.out, last - step)
            self.copy(step, where, where).wait_recv()
            if self.left:
                self.copy_of(step + 1).start()

    def finish(self):
        for step in range(2 * (self.count - 1)):
            self.copy_of(step).wait_send()


def ring_rows(rows, count):
    chunk = -(-rows // (count * 16)) * 16
    forward = -(-chunk // 32) * 16
    return chunk, forward, chunk - forward


def backward_kernel(plan, *refs):
    count, narrow, side = plan["wide"], plan["narrow"], plan["side"]
    groups, own_rows = plan["groups"], plan["own"]
    taken = 0

    def take(number):
        nonlocal taken
        taken += number
        return refs[taken - number : taken]

    len_ref, qs_ref, ks_ref, ng_ref, g2_ref = take(5)
    loads_from = take(plan["loads"])
    outs = take(4)
    gt_ref, gains_ref = take(2)
    loaded = take(plan["loads"])
    lands = take(plan["lands"])
    all_ref, vaug_ref, aug_ref, dk_ref, dv_ref = take(5)
    px1, px2, rx1, rx2, own1, own2 = take(6)
    gn_send, gn_recv, gn_own = take(3)
    gain_mine, gain_in = take(2)
    load_sems, ring_sends, ring_recvs, keep_sem, y_sends, y_recvs, gn_sends, gn_recvs, gain_sends, gain_recvs = take(10)

    branch, rows_turned, w_all, tok, gmid, cos_ref, sin_ref, gu_own, gd_own = loaded[:9]
    group_refs = [loaded[9 + 9 * g : 18 + 9 * g] for g in range(groups)]
    gu_src, gd_src = loads_from[7], loads_from[8]

    w = lax.axis_index("wide")
    n = lax.axis_index("narrow")
    half = count // 2
    place_ring = lax.rem((1 - w % 2) * (count - w // 2) + (w % 2) * (w // 2 + 1), count)

    def at_place(p):
        far = lax.rem(p + count - 1, count) // half
        z = (1 - far) * (p - 1) + far * lax.rem(count - p, count)
        return 2 * z + 1 - far

    onward = at_place(lax.rem(place_ring + 1, count))
    behind = at_place(lax.rem(place_ring + count - 1, count))
    across = lax.rem(n + side, narrow)
    place = lax.rem(n, side)

    def mate(turn):
        return n - place + lax.rem(place + turn, side)

    def flip(value, bit):
        return value + bit - 2 * bit * lax.rem(value // bit, 2)

    doubling = [("narrow", 2**e) for e in range(int(math.log2(narrow)))]
    doubling += [("wide", 2**e) for e in range(int(math.log2(count)))]
    partners = [{axis: flip(n if axis == "narrow" else w, bit)} for axis, bit in doubling]
    peers = [{"wide": onward}, {"wide": behind}, {"narrow": across}]
    peers += [{"narrow": mate(t)} for t in range(1, side)] + partners

    loads = [
        pltpu.make_async_copy(s, d, load_sems.at[i])
        for i, (s, d) in enumerate(zip(loads_from, loaded))
    ]
    for load in loads:
        load.start()
    waited = set()

    def need(*which):
        for i in which:
            if i not in waited:
                waited.add(i)
                loads[i].wait()

    barrier = pltpu.get_barrier_semaphore()
    for peer in peers:
        pl.semaphore_signal(barrier, inc=1, device_id=peer, device_id_type=pl.DeviceIdType.MESH)
    pl.semaphore_wait(barrier, len(peers))

    rings = []
    used = 0
    for a, (own, source, out, rows) in enumerate(
        [
            (gu_own, gu_src, outs[0], plan["rows"][0]),
            (gd_own, gd_src, outs[1], plan["rows"][1]),
            (own1, own1, outs[2], plan["rows"][2]),
            (own2, own2, outs[3], plan["rows"][3]),
        ]
    ):
        chunk, forward, backward = ring_rows(rows, count)
        pair = []
        for turn, target, first, size in ((1, onward, 0, forward), (-1, behind, forward, backward)):
            if size:
                pair.append(
                    Ring(
                        count, place_ring, target, turn, chunk, first, size, own, source, out,
                        lands[used], ring_sends.at[used], ring_recvs.at[used],
                    )
                )
                used += 1
        rings.append(pair)

    for pair in rings[:2]:
        for ring in pair:
            ring.begin()

    def tick(pair):
        for ring in pair:
            if ring.left:
                ring.tick(keep_sem)

    length = len_ref[0]
    ones = group_ones()
    lane = lanes((BLK, TILE))
    width = w_all.shape[1] // groups
    gains = {"q": jnp.zeros((1, TILE), F32), "k": jnp.zeros((1, TILE), F32)}
    col_ids = lax.rem(lax.broadcasted_iota(jnp.int32, (BLK, 2 * BLK), 1), BLK)
    causal = lax.broadcasted_iota(jnp.int32, (BLK, 2 * BLK), 0) <= col_ids

    def turn_back(grad, cosine, sine):
        return grad * cosine - swap_halves(grad) * sine

    def norm_back(raw, turned, scale):
        inv = lax.rsqrt(group_sum(raw * raw, ones) * (1.0 / HD) + EPSILON)
        scaled = turned * scale
        unit = raw * inv
        inner = group_sum(unit * scaled, ones) * (1.0 / HD)
        gain = jnp.sum(turned * unit, axis=0, keepdims=True)
        return inv * (scaled - unit * inner), gain

    def attention_pieces(g):
        q_ref, k_ref, v_ref, att_ref, qraw_ref, kraw_ref, rinv_ref, wo_ref, _ = group_refs[g]
        heads = k_ref.shape[1] // HD
        base, nq, nk = g * width, q_ref.shape[1], k_ref.shape[1]
        for start in range(0, LEN, BLK):
            rows = slice(start, start + BLK)
            grad = contract(branch[rows, :], wo_ref[...], 1, 1).astype(BF16).astype(F32)
            for t in range(heads):
                cols = slice(t * TILE, (t + 1) * TILE)
                part = (grad[:, cols] * rinv_ref[rows, cols]).astype(BF16).astype(F32)
                inner = group_sum(part * att_ref[rows, cols].astype(F32), ones)
                for which in range(2):
                    mine = part if which == 0 else pltpu.roll(part, HD, 1)
                    sums = pltpu.roll(inner, HD, 1) if which == 0 else inner
                    high = sums.astype(BF16).astype(F32)
                    tail = jnp.where(
                        lane == HD, -high, jnp.where(lane == HD + 1, high - sums, 0.0)
                    )
                    aug_ref[2 * t + which, rows, :] = jnp.where(lane < HD, mine, tail).astype(BF16)
            for t in range(heads // 2):
                v_pair = v_ref[rows, t * TILE : (t + 1) * TILE].astype(F32)
                mark = jnp.where(lane < HD + 2, 1.0, 0.0)
                vaug_ref[2 * t, rows, :] = jnp.where(lane < HD, v_pair, mark).astype(BF16)
                vaug_ref[2 * t + 1, rows, :] = jnp.where(
                    lane < HD, pltpu.roll(v_pair, HD, 1), mark
                ).astype(BF16)
            dk_ref[:, rows, :] = jnp.zeros((heads, BLK, HD), F32)
            dv_ref[:, rows, :] = jnp.zeros((heads, BLK, TILE), F32)
            yield

        for h in range(heads):
            keys_turned = jnp.transpose(
                k_ref[:, (h // 2) * TILE : (h // 2 + 1) * TILE].astype(F32)
            )[(h % 2) * HD : (h % 2 + 1) * HD].astype(BF16)
            for i in range(LEN // BLK):
                rows = slice(i * BLK, (i + 1) * BLK)
                low = h * TILE
                q_two = jnp.concatenate(
                    [q_ref[rows, low : low + HD], q_ref[rows, low + HD : low + TILE]], axis=0
                )
                aug = jnp.concatenate(
                    [aug_ref[2 * h, rows, :], aug_ref[2 * h + 1, rows, :]], axis=0
                )
                dq = jnp.zeros((HD, 2 * BLK), F32)
                for j in range(i + 1):
                    keys = slice(j * BLK, (j + 1) * BLK)
                    weight = jnp.exp(contract(k_ref[keys, h * HD : (h + 1) * HD], q_two, 1, 1))
                    if i == j:
                        weight = jnp.where(causal, weight, 0.0)
                    slope = (weight * contract(vaug_ref[h, keys, :], aug, 1, 1)).astype(BF16)
                    dv_ref[h, keys, :] += contract(weight.astype(BF16), aug, 1, 0)
                    dk_ref[h, keys, :] += contract(slope, q_two, 1, 0)
                    dq += contract(keys_turned[:, keys], slope, 1, 0)
                both = jnp.concatenate([dq[:, :BLK], dq[:, BLK:]], axis=0)
                grad = jnp.transpose(both) * (1.0 / math.sqrt(HD))
                turned = turn_back(grad, cos_ref[rows, :], sin_ref[rows, :])
                out, gain = norm_back(qraw_ref[rows, low : low + TILE], turned, qs_ref[...])
                all_ref[rows, base + low : base + low + TILE] = out.astype(BF16)
                gains["q"] += gain
                yield

        for start in range(0, LEN, BLK):
            rows = slice(start, start + BLK)
            real = (lax.broadcasted_iota(jnp.int32, (BLK, TILE), 0) + start) < length
            for t in range(heads // 2):
                low = base + nq + t * TILE
                grad = jnp.concatenate(
                    [dk_ref[2 * t, rows, :], dk_ref[2 * t + 1, rows, :]], axis=1
                )
                grad = jnp.where(real, grad, 0.0)
                turned = turn_back(grad, cos_ref[rows, :], sin_ref[rows, :])
                out, gain = norm_back(
                    kraw_ref[rows, t * TILE : (t + 1) * TILE], turned, ks_ref[...]
                )
                all_ref[rows, low : low + TILE] = out.astype(BF16)
                gains["k"] += gain
                values = jnp.where(
                    lane < HD,
                    dv_ref[2 * t, rows, :],
                    pltpu.roll(dv_ref[2 * t + 1, rows, :], HD, 1),
                )
                all_ref[rows, low + nk : low + nk + TILE] = jnp.where(real, values, 0.0).astype(
                    BF16
                )
            yield

    def wide_copy(source, target, which):
        return pltpu.make_async_remote_copy(
            src_ref=source,
            dst_ref=target,
            send_sem=y_sends.at[which],
            recv_sem=y_recvs.at[which],
            device_id={"narrow": across},
            device_id_type=pl.DeviceIdType.MESH,
        )

    y_out = wide_copy(px2, rx2, 0)
    y_qkv = wide_copy(px1, rx1, 1)

    def out_grads(which, target):
        g, first, size = plan["out_parts"][which]
        target[:size, :] = contract(
            group_refs[g][8][first : first + size, :], branch[...], 1, 0
        ).astype(BF16)

    def qkv_grads(which, target):
        for start in range(0, rows_turned.shape[0], BLK):
            rows = slice(start, start + BLK)
            for source, size, to in plan["qkv_parts"][which]:
                target[rows, to : to + size] = contract(
                    rows_turned[rows, :], all_ref[:, source : source + size], 1, 0
                ).astype(BF16)
            yield

    def gn_copy(turn):
        return pltpu.make_async_remote_copy(
            src_ref=gn_send.at[turn - 1],
            dst_ref=gn_recv.at[turn - 1],
            send_sem=gn_sends.at[turn - 1],
            recv_sem=gn_recvs.at[turn - 1],
            device_id={"narrow": mate(turn)},
            device_id_type=pl.DeviceIdType.MESH,
        )

    def gain_copy(step):
        return pltpu.make_async_remote_copy(
            src_ref=gain_mine.at[step],
            dst_ref=gain_in.at[step],
            send_sem=gain_sends.at[step],
            recv_sem=gain_recvs.at[step],
            device_id=partners[step],
            device_id_type=pl.DeviceIdType.MESH,
        )

    def compute():
        first_group = list(range(9, 18))
        need(0, 5, 6, *first_group)
        out_grads("partner", px2)
        if groups > 1:
            y_out.start()
            yield
        yield from attention_pieces(0)
        need(1)
        if groups == 1:
            y_out.start()
        yield from qkv_grads("partner", px1)
        y_qkv.start()
        if groups > 1:
            need(*range(18, 27))
            yield from attention_pieces(1)
        yield from qkv_grads("own", own1)
        out_grads("own", own2)
        yield
        need(2)
        for turn in [*range(1, side), 0]:
            for start in range(0, own_rows, BLK):
                at = pl.multiple_of(lax.rem(place + turn, side) * own_rows + start, BLK)
                grad = contract(all_ref[pl.ds(at, BLK), :], w_all[...], 1, 1)
                if turn:
                    gn_send[turn - 1, start : start + BLK, :] = grad.astype(BF16)
                else:
                    gn_own[start : start + BLK, :] = grad
                yield
            if turn:
                gn_copy(turn).start()
        need(3, 4)
        for turn in range(1, side):
            gn_copy(turn).wait_recv()
        gain_one = jnp.zeros((1, ng_ref.shape[1]), F32)
        for start in range(0, own_rows, 64):
            rows = slice(start, start + 64)
            grad = gn_own[rows, :]
            for turn in range(1, side):
                grad += gn_recv[turn - 1, rows, :].astype(F32)
            values = tok[rows, :].astype(F32)
            inv = lax.rsqrt(jnp.mean(values * values, axis=1, keepdims=True) + EPSILON)
            unit = values * inv
            scaled = grad * ng_ref[...]
            inner = jnp.mean(unit * scaled, axis=1, keepdims=True)
            gt_ref[rows, :] = gmid[rows, :] + inv * (scaled - unit * inner)
            gain_one += jnp.sum(grad * unit, axis=0, keepdims=True)
        gain_mine[0, 0:1, :] = gain_one
        gain_mine[0, 1:2, :] = g2_ref[...]
        spare = jnp.zeros((1, gain_one.shape[1] - TILE), F32)
        gain_mine[0, 2:3, :] = jnp.concatenate([gains["q"], spare], axis=1)
        gain_mine[0, 3:4, :] = jnp.concatenate([gains["k"], spare], axis=1)
        gain_mine[0, 4:8, :] = jnp.zeros((4, gain_one.shape[1]), F32)
        gain_copy(0).start()
        yield
        y_out.wait_recv()
        y_qkv.wait_recv()
        for mine, theirs in ((own1, rx1), (own2, rx2)):
            tall = mine.shape[0] // 16

            @pl.loop(0, tall)
            def _(r):
                at = pl.ds(pl.multiple_of(r * 16, 16), 16)
                mine[at, :] = (mine[at, :].astype(F32) + theirs[at, :].astype(F32)).astype(BF16)

    need(7, 8)
    turn = 0
    order = [0, 1]
    for number, _ in enumerate(compute()):
        if number % 4 == 3:
            tick(rings[order[turn % 2]])
            turn += 1
    for pair in rings[2:]:
        for ring in pair:
            ring.begin()
    step = 0
    while any(ring.left for pair in rings for ring in pair):
        tick(rings[order[turn % 2]])
        turn += 1
        tick(rings[2])
        tick(rings[3])
        if step < len(doubling):
            gain_copy(step).wait_recv()
            total = gain_mine[step] + gain_in[step]
            if step + 1 < len(doubling):
                gain_mine[step + 1] = total
                gain_copy(step + 1).start()
            else:
                gains_ref[...] = total
        step += 1
    for pair in rings:
        for ring in pair:
            ring.finish()
    y_out.wait_send()
    y_qkv.wait_send()
    for turn in range(1, side):
        gn_copy(turn).wait_send()
    for step in range(len(doubling)):
        gain_copy(step).wait_send()


VM = pl.BlockSpec(memory_space=pltpu.VMEM)
ANY = pl.BlockSpec(memory_space=pl.ANY)
SM = pl.BlockSpec(memory_space=pltpu.SMEM)


def run_forward(length, rows, wq, wk, wv, qs, ks, cosine, sine):
    nq, nk = wq.shape[1], wk.shape[1]
    shape = jax.ShapeDtypeStruct
    return pl.pallas_call(
        attention_forward,
        out_shape=(
            shape((LEN, nq), BF16),
            shape((LEN, nq), BF16),
            shape((LEN, nk), BF16),
            shape((LEN, nk), BF16),
            shape((LEN, nq), F32),
            shape((LEN, nk), F32),
            shape((LEN, nq), F32),
        ),
        in_specs=[SM] + [VM] * 8,
        out_specs=[VM] * 7,
        scratch_shapes=[pltpu.VMEM((nk // HD, LEN, TILE), BF16)],
        compiler_params=pltpu.CompilerParams(vmem_limit_bytes=VMEM_LIMIT),
        cost_estimate=pl.CostEstimate(
            flops=2 * LEN * rows.shape[1] * 2 * nq + 8 * LEN * LEN * nq,
            bytes_accessed=8 * 1024 * 1024,
            transcendentals=0,
        ),
        name="attention_forward",
    )(length, rows, wq, wk, wv, qs, ks, cosine, sine)


def padded(array, count):
    chunk = ring_rows(array.shape[0], count)[0]
    extra = chunk * count - array.shape[0]
    return jnp.pad(array, ((0, extra), (0, 0))) if extra else array


def run_backward(plan, small, big, group_arrays, grads_gu, grads_d):
    count, narrow, side = plan["wide"], plan["narrow"], plan["side"]
    shape = jax.ShapeDtypeStruct
    depth = big[0].shape[1]
    loads = list(big) + [padded(grads_gu, count), padded(grads_d, count)]
    for arrays in group_arrays:
        loads += list(arrays)
    q, k = group_arrays[0][0], group_arrays[0][1]
    heads = k.shape[1] // HD
    qkv, outs = plan["qkv_width"], plan["out_rows"]
    sizes = [grads_gu.shape, grads_d.shape, (depth, qkv), (outs, depth)]
    plan = dict(plan, loads=len(loads), rows=[s[0] for s in sizes], groups=len(group_arrays))
    full, lands = [], []
    for rows, cols in sizes:
        chunk, forward, backward = ring_rows(rows, count)
        full.append((chunk * count, cols))
        lands += [pltpu.VMEM((count - 1, r, cols), BF16) for r in (forward, backward) if r]
    plan["lands"] = len(lands)
    steps = 2 * (count - 1)
    doubling = int(math.log2(narrow)) + int(math.log2(count))
    own = plan["own"]
    dma = pltpu.SemaphoreType.DMA
    results = pl.pallas_call(
        functools.partial(backward_kernel, plan),
        out_shape=tuple(shape(s, BF16) for s in full)
        + (shape((own, depth), F32), shape((8, depth), F32)),
        in_specs=[SM] + [VM] * 4 + [ANY] * len(loads),
        out_specs=[ANY] * 4 + [VM] * 2,
        scratch_shapes=[pltpu.VMEM(a.shape, a.dtype) for a in loads]
        + lands
        + [
            pltpu.VMEM((LEN, big[2].shape[1]), BF16),
            pltpu.VMEM((heads, LEN, TILE), BF16),
            pltpu.VMEM((2 * heads, LEN, TILE), BF16),
            pltpu.VMEM((heads, LEN, HD), F32),
            pltpu.VMEM((heads, LEN, TILE), F32),
            pltpu.VMEM(full[2], BF16),
            pltpu.VMEM(full[3], BF16),
            pltpu.VMEM(full[2], BF16),
            pltpu.VMEM(full[3], BF16),
            pltpu.VMEM(full[2], BF16),
            pltpu.VMEM(full[3], BF16),
            pltpu.VMEM((side - 1, own, depth), BF16),
            pltpu.VMEM((side - 1, own, depth), BF16),
            pltpu.VMEM((own, depth), F32),
            pltpu.VMEM((doubling, 8, depth), F32),
            pltpu.VMEM((doubling, 8, depth), F32),
            dma((len(loads),)),
            dma((len(lands), steps)),
            dma((len(lands), steps)),
            dma,
            dma((2,)),
            dma((2,)),
            dma((side - 1,)),
            dma((side - 1,)),
            dma((doubling,)),
            dma((doubling,)),
        ],
        compiler_params=pltpu.CompilerParams(
            vmem_limit_bytes=BACK_LIMIT, collective_id=1, has_side_effects=True
        ),
        cost_estimate=pl.CostEstimate(
            flops=20 * 10**9, bytes_accessed=64 * 1024 * 1024, transcendentals=0
        ),
        name="backward_and_sums",
    )(*small, *loads)
    return [r[: s[0]] for r, s in zip(results[:4], sizes)] + list(results[4:])


def on_device(
    wide, narrow,
    tokens, lengths, norm_gain, w_query, w_key, w_value, query_scale, key_scale, w_out,
    ffn_gain, w_gate, w_up, w_down, cotangent,
):
    sequences = lengths.shape[0]
    side = narrow // sequences
    own = tokens.shape[0]
    me = lax.axis_index("narrow")
    place, mine = lax.rem(me, side), me // side

    def across(array, turn=1):
        return lax.ppermute(
            array, "narrow", [(i, (i + turn * side) % narrow) for i in range(narrow)]
        )

    def within(array, turn):
        return lax.ppermute(
            array,
            "narrow",
            [(i, (i // side) * side + (i % side + turn) % side) for i in range(narrow)],
        )

    def gather(array):
        size = array.shape[0]
        whole = jnp.zeros((side * size,) + array.shape[1:], array.dtype)
        whole = lax.dynamic_update_slice(whole, array, (place * size, 0))
        for turn in range(1, side):
            source = lax.rem(place + side - turn, side)
            whole = lax.dynamic_update_slice(whole, within(array, turn), (source * size, 0))
        return whole

    def scatter(parts):
        size = parts.shape[0] // side
        total = lax.dynamic_slice_in_dim(parts, place * size, size).astype(F32)
        for turn in range(1, side):
            target = lax.rem(place + turn, side)
            total += within(
                lax.dynamic_slice_in_dim(parts, target * size, size).astype(BF16), turn
            ).astype(F32)
        return total

    cosine, sine = rope_tables(LEN, HD)
    cosine = jnp.concatenate([cosine] * 4, axis=1)
    sine = jnp.concatenate([-sine, sine, -sine, sine], axis=1)
    qs = jnp.concatenate([query_scale] * 2)[None, :]
    ks = jnp.concatenate([key_scale] * 2)[None, :]
    length = lax.dynamic_slice_in_dim(lengths, mine, 1)

    weights = [(w_query, w_key, w_value, w_out)]
    weights += [tuple(across(w, t) for w in weights[0]) for t in range(1, sequences)]
    joined = w_key.shape[1] % TILE != 0
    if joined:
        weights = [
            tuple(jnp.concatenate(ws, axis=1 if n < 3 else 0) for n, ws in enumerate(zip(*weights)))
        ]

    residual = tokens.astype(F32)
    normed_one, inv_one = row_norm(residual, norm_gain)
    rows_one = gather(normed_one.astype(BF16))
    saved = [run_forward(length, rows_one, *w[:3], qs, ks, cosine, sine) for w in weights]
    mixed = contract(saved[0][0], weights[0][3], 1, 0)
    for s, w in zip(saved[1:], weights[1:]):
        mixed += contract(s[0], w[3], 1, 0)
    middle = residual + scatter(mixed)

    normed_two, inv_two = row_norm(middle, ffn_gain)
    low_two = normed_two.astype(BF16)

    blocks = []
    for turn in range(sequences):
        rows = gather(across(low_two, turn) if turn else low_two)
        grads = gather(across(cotangent, turn) if turn else cotangent)
        gate_pre = contract(rows, w_gate, 1, 0)
        up_pre = contract(rows, w_up, 1, 0)
        sigmoid_gate = jax.nn.sigmoid(gate_pre)
        hidden = (gate_pre * sigmoid_gate * up_pre).astype(BF16)
        grad_hidden = contract(grads, w_down, 1, 1)
        grad_gate = (
            grad_hidden * up_pre * sigmoid_gate * (1.0 + gate_pre * (1.0 - sigmoid_gate))
        ).astype(BF16)
        grad_up = (grad_hidden * gate_pre * sigmoid_gate).astype(BF16)
        back = contract(grad_gate, w_gate, 1, 1) + contract(grad_up, w_up, 1, 1)
        blocks.append((rows, grads, hidden, grad_gate, grad_up, back))

    def to_owners(parts):
        total = scatter(parts[0])
        for turn in range(1, sequences):
            total += across(scatter(parts[turn]).astype(BF16), sequences - turn).astype(F32)
        return total

    grad_normed_two = to_owners([b[5] for b in blocks])
    rows_two, grad_rows, hidden, grad_gate, grad_up = (
        jnp.concatenate([b[n] for b in blocks], axis=0) for n in range(5)
    )
    output = middle + to_owners([contract(b[2], w_down, 1, 0) for b in blocks])
    grad_down = contract(hidden, grad_rows, 0, 0).astype(BF16)
    grad_gate_up = contract(
        rows_two, jnp.concatenate([grad_gate, grad_up], axis=1), 0, 0
    ).astype(BF16)

    back_two, gain_two = row_norm_back(middle, inv_two, ffn_gain, grad_normed_two)
    grad_middle = cotangent.astype(F32) + back_two
    branch = gather(grad_middle.astype(BF16))

    nq, nk = w_query.shape[1], w_key.shape[1]
    if joined:
        order = [0]
        qkv_parts = {
            "own": [(0, nq, 0), (2 * nq, nk, nq), (2 * nq + 2 * nk, nk, nq + nk)],
            "partner": [
                (nq, nq, 0), (2 * nq + nk, nk, nq), (2 * nq + 3 * nk, nk, nq + nk)
            ],
        }
        out_parts = {"own": (0, 0, nq), "partner": (0, nq, nq)}
    else:
        order = [1, 0]
        qkv_parts = {
            "partner": [(0, nq + 2 * nk, 0)],
            "own": [(nq + 2 * nk, nq + 2 * nk, 0)],
        }
        out_parts = {"partner": (0, 0, nq), "own": (1, 0, nq)}
    plan = {
        "wide": wide, "narrow": narrow, "side": side, "own": own,
        "qkv_parts": qkv_parts, "out_parts": out_parts,
        "qkv_width": nq + 2 * nk, "out_rows": nq,
    }
    group_arrays = []
    for g in order:
        att, q, k, v, q_raw, k_raw, rinv = saved[g]
        group_arrays.append((q, k, v, att, q_raw, k_raw, rinv, weights[g][3], att.T))
    w_all = jnp.concatenate([w for g in order for w in weights[g][:3]], axis=1)
    sum_gu, sum_down, sum_qkv, sum_out, grad_tokens, gains = run_backward(
        plan,
        (length, qs, ks, norm_gain[None, :], gain_two[None, :]),
        (branch, rows_one.T, w_all, tokens, grad_middle, cosine, sine),
        group_arrays,
        grad_gate_up,
        grad_down,
    )
    hidden_units = w_gate.shape[1]
    return (
        output.astype(BF16),
        grad_tokens,
        gains[0],
        sum_qkv[:, :nq].astype(F32),
        sum_qkv[:, nq : nq + nk].astype(F32),
        sum_qkv[:, nq + nk :].astype(F32),
        gains[2, :HD] + gains[2, HD:TILE],
        gains[3, :HD] + gains[3, HD:TILE],
        sum_out.astype(F32),
        gains[1],
        sum_gu[:, :hidden_units].astype(F32),
        sum_gu[:, hidden_units:].astype(F32),
        sum_down.astype(F32),
    )


def solution(mesh):
    rows = P(("wide", "narrow"), None)
    columns, depth, copied = P(None, "narrow"), P("narrow", None), P()
    return jax.shard_map(
        functools.partial(on_device, mesh.shape["wide"], mesh.shape["narrow"]),
        mesh=mesh,
        in_specs=(
            rows, P("wide"), copied, columns, columns, columns, copied, copied, depth,
            copied, columns, columns, depth, rows,
        ),
        out_specs=(
            rows, rows, copied, columns, columns, columns, copied, copied, depth,
            copied, columns, columns, depth,
        ),
        check_vma=False,
    )
```

```python
import functools
import math

import jax
import jax.numpy as jnp
from jax import lax
from jax.experimental import pallas as pl
from jax.experimental.pallas import tpu as pltpu
from jax.sharding import PartitionSpec as P

HD = 64
LEN = 1024
BLK = 256
TILE = 2 * HD

EPSILON = 1e-05
ROPE_BASE = 1000000.0
F32 = jnp.float32
BF16 = jnp.bfloat16
VMEM_LIMIT = 48 * 1024 * 1024
BACK_LIMIT = 60 * 1024 * 1024


def rope_tables(length, width):
    half_width = width // 2
    frequency = ROPE_BASE ** (-(2.0 * jnp.arange(half_width, dtype=jnp.float32)) / width)
    angles = jnp.arange(length, dtype=jnp.float32)[:, None] * frequency[None, :]
    return (jnp.cos(angles), jnp.sin(angles))


def row_norm(values_in, gain_vec):
    inv_rms = lax.rsqrt(jnp.mean(values_in * values_in, axis=-1, keepdims=True) + EPSILON)
    return (values_in * inv_rms * gain_vec, inv_rms)


def contract(left_side, right_side, left_dim, right_dim):
    return lax.dot_general(
        left_side,
        right_side,
        (((left_dim,), (right_dim,)), ((), ())),
        preferred_element_type=F32,
    )


def lanes(shape):
    return lax.broadcasted_iota(jnp.int32, shape, 1)


def group_ones():
    rows = lax.broadcasted_iota(jnp.int32, (TILE, TILE), 0) // HD
    cols = lax.broadcasted_iota(jnp.int32, (TILE, TILE), 1) // HD
    return jnp.where(rows == cols, 1.0, 0.0).astype(BF16)


def group_sum(values_in, ones):
    high = values_in.astype(BF16)
    rest = (values_in - high.astype(F32)).astype(BF16)
    return contract(high, ones, 1, 0) + contract(rest, ones, 1, 0)


def swap_halves(values_in):
    half = HD // 2
    front = lax.rem(lanes(values_in.shape), HD) < half
    return jnp.where(
        front, pltpu.roll(values_in, TILE - half, 1), pltpu.roll(values_in, half, 1)
    )


def attention_forward(
    len_ref, x_ref, wq_ref, wk_ref, wv_ref, qs_ref, ks_ref, cos_ref, sin_ref,
    att_ref, q_ref, k_ref, v_ref, qraw_ref, kraw_ref, rinv_ref,
    vaug_ref,
):
    length = len_ref[0]
    heads = wk_ref.shape[1] // HD
    ones = group_ones()

    def norm_rope(raw, scale, cosine, sine):
        inv = lax.rsqrt(group_sum(raw * raw, ones) * (1.0 / HD) + EPSILON)
        scaled = raw * inv * scale
        return scaled * cosine + swap_halves(scaled) * sine

    for start in range(0, LEN, BLK):
        rows = slice(start, start + BLK)
        x = x_ref[rows, :]
        cosine, sine = cos_ref[rows, :], sin_ref[rows, :]
        real = (lax.broadcasted_iota(jnp.int32, (BLK, TILE), 0) + start) < length
        q_raw = contract(x, wq_ref[...], 1, 0)
        qraw_ref[rows, :] = q_raw
        for t in range(heads):
            cols = slice(t * TILE, (t + 1) * TILE)
            turned = norm_rope(q_raw[:, cols], qs_ref[...], cosine, sine)
            q_ref[rows, cols] = (turned * (1.0 / math.sqrt(HD))).astype(BF16)
        k_raw = contract(x, wk_ref[...], 1, 0)
        kraw_ref[rows, :] = k_raw
        v_raw = contract(x, wv_ref[...], 1, 0)
        for t in range(heads // 2):
            cols = slice(t * TILE, (t + 1) * TILE)
            turned = norm_rope(k_raw[:, cols], ks_ref[...], cosine, sine)
            k_ref[rows, cols] = jnp.where(real, turned, 0.0).astype(BF16)
            v_pair = jnp.where(real, v_raw[:, cols], 0.0)
            v_ref[rows, cols] = v_pair.astype(BF16)
            lane = lanes((BLK, TILE))
            mark = jnp.where(real & (lane == HD), 1.0, 0.0)
            vaug_ref[2 * t, rows, :] = jnp.where(lane < HD, v_pair, mark).astype(BF16)
            vaug_ref[2 * t + 1, rows, :] = jnp.where(
                lane < HD, pltpu.roll(v_pair, HD, 1), mark
            ).astype(BF16)

    row_ids = lax.rem(lax.broadcasted_iota(jnp.int32, (2 * BLK, BLK), 0), BLK)
    causal = lax.broadcasted_iota(jnp.int32, (2 * BLK, BLK), 1) <= row_ids
    for h in range(heads):
        for i in range(LEN // BLK):
            rows = slice(i * BLK, (i + 1) * BLK)
            low = h * TILE
            q_two = jnp.concatenate(
                [q_ref[rows, low : low + HD], q_ref[rows, low + HD : low + TILE]], axis=0
            )
            total = jnp.zeros((2 * BLK, TILE), F32)
            for j in range(i + 1):
                keys = slice(j * BLK, (j + 1) * BLK)
                scores = contract(q_two, k_ref[keys, h * HD : (h + 1) * HD], 1, 1)
                weight = jnp.exp(scores)
                if i == j:
                    weight = jnp.where(causal, weight, 0.0)
                total += contract(weight.astype(BF16), vaug_ref[h, keys, :], 1, 0)
            inv = 1.0 / total[:, HD : HD + 1]
            mixed = total[:, :HD] * inv
            att_ref[rows, low : low + HD] = mixed[:BLK].astype(BF16)
            att_ref[rows, low + HD : low + TILE] = mixed[BLK:].astype(BF16)
            rinv_ref[rows, low : low + HD] = jnp.broadcast_to(inv[:BLK], (BLK, HD))
            rinv_ref[rows, low + HD : low + TILE] = jnp.broadcast_to(inv[BLK:], (BLK, HD))


class Ring:
    def __init__(self, count, place, target, turn, chunk, first, rows, own, source, out, land, sends, recvs):
        self.count, self.place, self.target, self.turn = count, place, target, turn
        self.chunk, self.first, self.rows = chunk, first, rows
        self.own, self.source, self.out, self.land = own, source, out, land
        self.sends, self.recvs = sends, recvs
        self.done = 0

    def index(self, steps):
        return lax.rem(self.place + self.turn * steps + 2 * self.count, self.count)

    def part(self, ref, steps):
        start = pl.multiple_of(self.index(steps) * self.chunk + self.first, 16)
        return ref.at[pl.ds(start, self.rows), :]

    def copy(self, step, source, target):
        return pltpu.make_async_remote_copy(
            src_ref=source,
            dst_ref=target,
            send_sem=self.sends.at[step],
            recv_sem=self.recvs.at[step],
            device_id={"wide": self.target},
            device_id_type=pl.DeviceIdType.MESH,
        )

    def copy_of(self, step):
        last = self.count - 1
        if step == 0:
            return self.copy(0, self.part(self.source, 0), self.land.at[0])
        if step < last:
            return self.copy(step, self.land.at[step - 1], self.land.at[step])
        steps = last - step + 1
        where = self.part(self.out, steps)
        return self.copy(step, self.land.at[last - 1] if step == last else where, where)

    def begin(self):
        self.copy_of(0).start()

    @property
    def left(self):
        return 2 * (self.count - 1) - self.done

    def tick(self, keep):
        step, last = self.done, self.count - 1
        self.done += 1
        if step < last:
            slot = self.land.at[step]
            self.copy(step, slot, slot).wait_recv()
            start = pl.multiple_of(self.index(-step - 1) * self.chunk + self.first, 16)

            @pl.loop(0, self.rows // 16)
            def _(r):
                at = pl.multiple_of(r * 16, 16)
                mine = self.own[pl.ds(pl.multiple_of(start + at, 16), 16), :].astype(F32)
                slot[pl.ds(at, 16), :] = (slot[pl.ds(at, 16), :].astype(F32) + mine).astype(BF16)

            if step == last - 1:
                kept = pltpu.make_async_copy(slot, self.part(self.out, 1), keep)
                kept.start()
                self.copy_of(last).start()
                kept.wait()
            else:
                self.copy_of(step + 1).start()
        else:
            where = self.part(self.out, last - step)
            self.copy(step, where, where).wait_recv()
            if self.left:
                self.copy_of(step + 1).start()

    def finish(self):
        for step in range(2 * (self.count - 1)):
            self.copy_of(step).wait_send()


def ring_rows(rows, count):
    chunk = -(-rows // (count * 16)) * 16
    forward = -(-chunk // 32) * 16
    return chunk, forward, chunk - forward


def main_kernel(plan, *refs):
    count, narrow, side = plan["wide"], plan["narrow"], plan["side"]
    groups, own_rows = plan["groups"], plan["own"]
    taken = 0

    def take(number):
        nonlocal taken
        taken += number
        return refs[taken - number : taken]

    len_ref, qs_ref, ks_ref, ng_ref, fg_ref = take(5)
    xin, cin, wg_in, wu_in, wd_in, mid_in, tok_in, cos_in, sin_in, turned_in, w_all_in = take(11)
    groups_in = [take(9) for _ in range(groups)]
    gu_out, gd_out, a1_out, a2_out, out_out, gt_out = take(6)
    (gains_ref,) = take(1)
    x_l, x_r, c_l, c_r = take(4)
    gu_own, gd_own, px1, px2, rx1, rx2, own1, own2 = take(8)
    lands = take(plan["lands"])
    send_b, send_o, got_bl, got_ol, got_br, got_or = take(6)
    got_gn = got_br
    far_b, far_o, own_b, own_o, ownr_b, ownr_o = take(6)
    branch = x_r
    gain_mine, gain_in = take(2)
    load_sems, ring_sends, ring_recvs, keep_sem, sends, recvs, free_sem = take(7)

    w = lax.axis_index("wide")
    n = lax.axis_index("narrow")
    half = count // 2
    place_ring = lax.rem((1 - w % 2) * (count - w // 2) + (w % 2) * (w // 2 + 1), count)

    def at_place(p):
        far = lax.rem(p + count - 1, count) // half
        z = (1 - far) * (p - 1) + far * lax.rem(count - p, count)
        return 2 * z + 1 - far

    onward = at_place(lax.rem(place_ring + 1, count))
    behind = at_place(lax.rem(place_ring + count - 1, count))
    across = lax.rem(n + side, narrow)
    place = lax.rem(n, side)
    turns = range(1, side)

    def mate(turn):
        return n - place + lax.rem(place + turn, side)

    def flip(value, bit):
        return value + bit - 2 * bit * lax.rem(value // bit, 2)

    doubling = [("narrow", 2**e) for e in range(int(math.log2(narrow)))]
    doubling += [("wide", 2**e) for e in range(int(math.log2(count)))]
    partners = [{axis: flip(n if axis == "narrow" else w, bit)} for axis, bit in doubling]
    peers = [{"wide": onward}, {"wide": behind}, {"narrow": across}]
    peers += [{"narrow": mate(t)} for t in turns] + partners

    barrier = pltpu.get_barrier_semaphore()
    for peer in peers:
        pl.semaphore_signal(barrier, inc=1, device_id=peer, device_id_type=pl.DeviceIdType.MESH)
    pl.semaphore_wait(barrier, len(peers))

    numbers = {}
    unsent = []

    def remote(name, source, target, device):
        number = numbers.setdefault(name, len(numbers))
        return pltpu.make_async_remote_copy(
            src_ref=source,
            dst_ref=target,
            send_sem=sends.at[number],
            recv_sem=recvs.at[number],
            device_id=device,
            device_id_type=pl.DeviceIdType.MESH,
        )

    def send(name, source, target, device):
        copy = remote(name, source, target, device)
        copy.start()
        unsent.append((name, source, target, device))

    def sent(name):
        for entry in [e for e in unsent if e[0][: len(name)] == name]:
            remote(*entry).wait_send()
            unsent.remove(entry)

    def received(name, target, device):
        remote(name, target, target, device).wait_recv()

    def block(ref, turn):
        start = pl.multiple_of(lax.rem(place + turn, side) * own_rows, BLK)
        return ref.at[pl.ds(start, own_rows), :]

    to_across = {"narrow": across}

    def to_mates(name, source, target):
        for t in turns:
            send(f"{name}{t}", source, target, {"narrow": mate(t)})

    def from_mates(name, ref):
        for t in turns:
            received(f"{name}{t}", block(ref, side - t), {"narrow": mate(t)})

    loading = {}

    def load(name, source, target):
        copy = pltpu.make_async_copy(source, target, load_sems.at[len(loading)])
        loading[name] = [copy]
        copy.start()

    def need(*names):
        for name in names:
            if loading[name]:
                loading[name].pop().wait()

    rings = []
    used = 0
    for own, out, rows in (
        (gu_own, gu_out, plan["rows"][0]),
        (gd_own, gd_out, plan["rows"][1]),
        (own1, a1_out, plan["rows"][2]),
        (own2, a2_out, plan["rows"][3]),
    ):
        chunk, forward, backward = ring_rows(rows, count)
        pair = []
        for turn, target, first, size in ((1, onward, 0, forward), (-1, behind, forward, backward)):
            if size:
                pair.append(
                    Ring(
                        count, place_ring, target, turn, chunk, first, size, own, own, out,
                        lands[used], ring_sends.at[used], ring_recvs.at[used],
                    )
                )
                used += 1
        rings.append(pair)

    def begin(pair):
        for ring in pair:
            ring.begin()

    def tick(pair):
        for ring in pair:
            if ring.left:
                ring.tick(keep_sem)

    units = wg_in.shape[1]

    def feed_forward(wg, wu, wd, hid, gg, gu):
        load("x", xin, block(x_l, 0))
        load("wg", wg_in, wg)
        load("wu", wu_in, wu)
        load("c", cin, block(c_l, 0))
        load("wd", wd_in, wd)
        send("xy", xin, block(x_r, 0), to_across)
        to_mates("xl", xin, block(x_l, 0))
        to_mates("cl", cin, block(c_l, 0))
        send("cy", cin, block(c_r, 0), to_across)

        def rows_pass(x, c, turn, back_to, out_to):
            @pl.loop(0, own_rows // BLK)
            def _(r):
                to = pl.ds(pl.multiple_of(r * BLK, BLK), BLK)
                at = lax.rem(place + turn, side) * own_rows + r * BLK
                rows = pl.ds(pl.multiple_of(at, BLK), BLK)
                gate = contract(x[rows, :], wg[...], 1, 0)
                up = contract(x[rows, :], wu[...], 1, 0)
                grad = contract(c[rows, :], wd[...], 1, 1)
                share = 1.0 / (1.0 + jnp.exp(-gate))
                silu = gate * share
                hid[rows, :] = (silu * up).astype(BF16)
                gg[rows, :] = (grad * up * (share + silu * (1.0 - share))).astype(BF16)
                gu[rows, :] = (grad * silu).astype(BF16)
                back = contract(gg[rows, :], wg[...], 1, 1)
                back += contract(gu[rows, :], wu[...], 1, 1)
                back_to[to, :] = back.astype(BF16)
                out_to[to, :] = contract(hid[rows, :], wd[...], 1, 0).astype(BF16)

        depth = x_l.shape[1]

        def weight_pass(x, c, more):
            step = 384 if units % 384 == 0 else units
            for start in range(0, units, step):
                rows = slice(start, start + step)
                part = contract(hid[:, rows], c[...], 0, 0)
                if more:
                    part += gd_own[rows, :].astype(F32)
                gd_own[rows, :] = part.astype(BF16)
            if more:
                begin(rings[1])
            for start in range(0, depth, BLK):
                rows = slice(start, start + BLK)
                for first, grad in ((0, gg), (units, gu)):
                    part = contract(x[:, rows], grad[...], 0, 0)
                    cols = slice(first, first + units)
                    if more:
                        part += gu_own[rows, cols].astype(F32)
                    gu_own[rows, cols] = part.astype(BF16)

        extra = gd_own.shape[0] - units
        if extra:
            gd_own[units:, :] = jnp.zeros((extra, depth), BF16)
        need("x", "wg", "wu", "c", "wd")
        rows_pass(x_l, c_l, 0, own_b, own_o)
        from_mates("xl", x_l)
        from_mates("cl", c_l)
        for t in turns:
            rows_pass(x_l, c_l, t, send_b.at[t - 1], send_o.at[t - 1])
            send(f"bl{t}", send_b.at[t - 1], got_bl.at[t - 1], {"narrow": mate(t)})
            send(f"ol{t}", send_o.at[t - 1], got_ol.at[t - 1], {"narrow": mate(t)})
        weight_pass(x_l, c_l, False)

        received("xy", block(x_r, 0), to_across)
        to_mates("xr", block(x_r, 0), block(x_r, 0))
        received("cy", block(c_r, 0), to_across)
        to_mates("cr", block(c_r, 0), block(c_r, 0))
        sent("bl")
        sent("ol")
        from_mates("xr", x_r)
        from_mates("cr", c_r)
        for t in turns:
            rows_pass(x_r, c_r, t, send_b.at[t - 1], send_o.at[t - 1])
            send(f"br{t}", send_b.at[t - 1], got_br.at[t - 1], {"narrow": mate(t)})
            send(f"or{t}", send_o.at[t - 1], got_or.at[t - 1], {"narrow": mate(t)})
        rows_pass(x_r, c_r, 0, ownr_b, ownr_o)
        for name, mine, got, far in (("b", ownr_b, got_br, far_b), ("o", ownr_o, got_or, far_o)):
            for t in turns:
                received(f"{name}r{t}", got.at[t - 1], {"narrow": mate(t)})

            @pl.loop(0, own_rows // 32)
            def _(r):
                rows = pl.ds(pl.multiple_of(r * 32, 32), 32)
                total = mine[rows, :].astype(F32)
                for t in turns:
                    total += got[t - 1, rows, :].astype(F32)
                mine[rows, :] = total.astype(BF16)

            send(name + "y", mine, far, to_across)
        weight_pass(x_r, c_r, True)
        begin(rings[0])
        for name in ("xy", "xl", "cl", "cy", "xr", "cr", "br", "or"):
            sent(name)

    weights = [pltpu.VMEM(ref.shape, BF16) for ref in (wg_in, wu_in, wd_in)]
    pl.run_scoped(feed_forward, *weights, *[pltpu.VMEM((LEN, units), BF16) for _ in range(3)])

    for t in turns:
        pl.semaphore_signal(
            free_sem, inc=1, device_id={"narrow": mate(t)}, device_id_type=pl.DeviceIdType.MESH
        )

    def attention(mid, gmid, tok, cos_ref, sin_ref, vaug_ref, aug_ref, dk_ref, dv_ref, *rest):
        group = rest[:9]
        spare = list(rest[9:])
        w_all = c_l if w_all_in.shape == x_r.shape else spare.pop(0)
        all_ref = x_l if w_all_in.shape == x_r.shape else spare.pop(0)
        rows_turned = c_r
        q_ref, k_ref, v_ref, att_ref, qraw_ref, kraw_ref, rinv_ref, wo_ref, attt_ref = group

        load("mid", mid_in, mid)

        def load_group(g):
            for i, (source, target) in enumerate(zip(groups_in[g], group)):
                load(f"group{g}_{i}", source, target)

        def need_group(g):
            need(*[f"group{g}_{i}" for i in range(9)])

        load_group(0)
        load("cos", cos_in, cos_ref)
        load("sin", sin_in, sin_ref)
        load("turned", turned_in, rows_turned)
        load("tok", tok_in, tok)

        length = len_ref[0]
        ones = group_ones()
        lane = lanes((BLK, TILE))
        width = w_all.shape[1] // groups
        heads = k_ref.shape[1] // HD
        nq, nk = q_ref.shape[1], k_ref.shape[1]
        gains = {"q": jnp.zeros((1, TILE), F32), "k": jnp.zeros((1, TILE), F32)}
        col_ids = lax.rem(lax.broadcasted_iota(jnp.int32, (BLK, 2 * BLK), 1), BLK)
        causal = lax.broadcasted_iota(jnp.int32, (BLK, 2 * BLK), 0) <= col_ids

        def turn_back(grad, cosine, sine):
            return grad * cosine - swap_halves(grad) * sine

        def norm_back(raw, turned, scale):
            inv = lax.rsqrt(group_sum(raw * raw, ones) * (1.0 / HD) + EPSILON)
            scaled = turned * scale
            unit = raw * inv
            inner = group_sum(unit * scaled, ones) * (1.0 / HD)
            gain = jnp.sum(turned * unit, axis=0, keepdims=True)
            return inv * (scaled - unit * inner), gain

        def attention_pieces(g):
            base = g * width
            for start in range(0, LEN, BLK):
                rows = slice(start, start + BLK)
                grad = contract(branch[rows, :], wo_ref[...], 1, 1).astype(BF16).astype(F32)
                for t in range(heads):
                    cols = slice(t * TILE, (t + 1) * TILE)
                    part = (grad[:, cols] * rinv_ref[rows, cols]).astype(BF16).astype(F32)
                    inner = group_sum(part * att_ref[rows, cols].astype(F32), ones)
                    for which in range(2):
                        mine = part if which == 0 else pltpu.roll(part, HD, 1)
                        sums = pltpu.roll(inner, HD, 1) if which == 0 else inner
                        high = sums.astype(BF16).astype(F32)
                        tail = jnp.where(
                            lane == HD, -high, jnp.where(lane == HD + 1, high - sums, 0.0)
                        )
                        aug_ref[2 * t + which, rows, :] = jnp.where(lane < HD, mine, tail).astype(
                            BF16
                        )
                for t in range(heads // 2):
                    v_pair = v_ref[rows, t * TILE : (t + 1) * TILE].astype(F32)
                    mark = jnp.where(lane < HD + 2, 1.0, 0.0)
                    vaug_ref[2 * t, rows, :] = jnp.where(lane < HD, v_pair, mark).astype(BF16)
                    vaug_ref[2 * t + 1, rows, :] = jnp.where(
                        lane < HD, pltpu.roll(v_pair, HD, 1), mark
                    ).astype(BF16)
                dk_ref[:, rows, :] = jnp.zeros((heads, BLK, HD), F32)
                dv_ref[:, rows, :] = jnp.zeros((heads, BLK, TILE), F32)
                yield

            for h in range(heads):
                keys_turned = jnp.transpose(
                    k_ref[:, (h // 2) * TILE : (h // 2 + 1) * TILE].astype(F32)
                )[(h % 2) * HD : (h % 2 + 1) * HD].astype(BF16)
                for i in range(LEN // BLK):
                    rows = slice(i * BLK, (i + 1) * BLK)
                    low = h * TILE
                    q_two = jnp.concatenate(
                        [q_ref[rows, low : low + HD], q_ref[rows, low + HD : low + TILE]], axis=0
                    )
                    aug = jnp.concatenate(
                        [aug_ref[2 * h, rows, :], aug_ref[2 * h + 1, rows, :]], axis=0
                    )
                    dq = jnp.zeros((HD, 2 * BLK), F32)
                    for j in range(i + 1):
                        keys = slice(j * BLK, (j + 1) * BLK)
                        weight = jnp.exp(
                            contract(k_ref[keys, h * HD : (h + 1) * HD], q_two, 1, 1)
                        )
                        if i == j:
                            weight = jnp.where(causal, weight, 0.0)
                        slope = (weight * contract(vaug_ref[h, keys, :], aug, 1, 1)).astype(BF16)
                        dv_ref[h, keys, :] += contract(weight.astype(BF16), aug, 1, 0)
                        dk_ref[h, keys, :] += contract(slope, q_two, 1, 0)
                        dq += contract(keys_turned[:, keys], slope, 1, 0)
                    both = jnp.concatenate([dq[:, :BLK], dq[:, BLK:]], axis=0)
                    grad = jnp.transpose(both) * (1.0 / math.sqrt(HD))
                    turned = turn_back(grad, cos_ref[rows, :], sin_ref[rows, :])
                    out, gain = norm_back(qraw_ref[rows, low : low + TILE], turned, qs_ref[...])
                    all_ref[rows, base + low : base + low + TILE] = out.astype(BF16)
                    gains["q"] += gain
                    yield

            for start in range(0, LEN, BLK):
                rows = slice(start, start + BLK)
                real = (lax.broadcasted_iota(jnp.int32, (BLK, TILE), 0) + start) < length
                for t in range(heads // 2):
                    low = base + nq + t * TILE
                    grad = jnp.concatenate(
                        [dk_ref[2 * t, rows, :], dk_ref[2 * t + 1, rows, :]], axis=1
                    )
                    grad = jnp.where(real, grad, 0.0)
                    turned = turn_back(grad, cos_ref[rows, :], sin_ref[rows, :])
                    out, gain = norm_back(
                        kraw_ref[rows, t * TILE : (t + 1) * TILE], turned, ks_ref[...]
                    )
                    all_ref[rows, low : low + TILE] = out.astype(BF16)
                    gains["k"] += gain
                    values = jnp.where(
                        lane < HD,
                        dv_ref[2 * t, rows, :],
                        pltpu.roll(dv_ref[2 * t + 1, rows, :], HD, 1),
                    )
                    all_ref[rows, low + nk : low + nk + TILE] = jnp.where(
                        real, values, 0.0
                    ).astype(BF16)
                yield

        def out_grads(which, target):
            first, size = plan["out_parts"][which]
            target[:size, :] = contract(
                attt_ref[first : first + size, :], branch[...], 1, 0
            ).astype(BF16)
            if target.shape[0] > size:
                target[size:, :] = jnp.zeros((target.shape[0] - size, target.shape[1]), BF16)

        def qkv_grads(which, target):
            for start in range(0, rows_turned.shape[0], BLK):
                rows = slice(start, start + BLK)
                for source, size, to in plan["qkv_parts"][which]:
                    target[rows, to : to + size] = contract(
                        rows_turned[rows, :], all_ref[:, source : source + size], 1, 0
                    ).astype(BF16)
                yield

        def gain_copy(step):
            return (f"gain{step}", gain_mine.at[step], gain_in.at[step], partners[step])

        def compute():
            need("mid")
            for t in turns:
                received(f"bl{t}", got_bl.at[t - 1], {"narrow": mate(t)})
            received("by", far_b, to_across)
            gain_two = jnp.zeros((1, fg_ref.shape[1]), F32)
            own_branch, own_cot = block(branch, 0), block(c_l, 0)
            for start in range(0, own_rows, 64):
                rows = slice(start, start + 64)
                grad = own_b[rows, :].astype(F32) + far_b[rows, :].astype(F32)
                for t in turns:
                    grad += got_bl[t - 1, rows, :].astype(F32)
                values = mid[rows, :]
                inv = lax.rsqrt(jnp.mean(values * values, axis=1, keepdims=True) + EPSILON)
                unit = values * inv
                scaled = grad * fg_ref[...]
                inner = jnp.mean(unit * scaled, axis=1, keepdims=True)
                total = own_cot[rows, :].astype(F32) + inv * (scaled - unit * inner)
                gmid[rows, :] = total
                own_branch[rows, :] = total.astype(BF16)
                gain_two += jnp.sum(grad * unit, axis=0, keepdims=True)
            load("w_all", w_all_in, w_all)
            gain_mine[0, 1:2, :] = gain_two
            pl.semaphore_wait(free_sem, side - 1)
            to_mates("br_", own_branch, own_branch)
            need_group(0)
            need("cos", "sin")
            from_mates("br_", branch)
            yield
            out_grads("partner", px2)
            send("o2", px2, rx2, to_across)
            if groups == 1:
                out_grads("own", own2)
            yield
            yield from attention_pieces(0)
            need("turned")
            yield from qkv_grads("partner", px1)
            send("o1", px1, rx1, to_across)
            if groups > 1:
                load_group(1)
            for t in turns:
                received(f"ol{t}", got_ol.at[t - 1], {"narrow": mate(t)})
            received("oy", far_o, to_across)
            for start in range(0, own_rows, 64):
                rows = slice(start, start + 64)
                total = mid[rows, :] + own_o[rows, :].astype(F32) + far_o[rows, :].astype(F32)
                for t in turns:
                    total += got_ol[t - 1, rows, :].astype(F32)
                own_o[rows, :] = total.astype(BF16)
            load("output", own_o, out_out)
            yield
            if groups > 1:
                need_group(1)
                out_grads("own", own2)
                yield
                yield from attention_pieces(1)
            yield from qkv_grads("own", own1)
            need("w_all", "tok")
            sent("by")
            for turn in [*turns, 0]:
                for start in range(0, own_rows, BLK):
                    at = pl.multiple_of(lax.rem(place + turn, side) * own_rows + start, BLK)
                    grad = contract(all_ref[pl.ds(at, BLK), :], w_all[...], 1, 1).astype(BF16)
                    if turn:
                        send_b[turn - 1, start : start + BLK, :] = grad
                    else:
                        own_b[start : start + BLK, :] = grad
                    yield
                if turn:
                    send(
                        f"gn{turn}", send_b.at[turn - 1], got_gn.at[turn - 1], {"narrow": mate(turn)}
                    )
            for t in turns:
                received(f"gn{t}", got_gn.at[t - 1], {"narrow": mate(t)})
            gain_one = jnp.zeros((1, ng_ref.shape[1]), F32)
            for start in range(0, own_rows, 64):
                rows = slice(start, start + 64)
                grad = own_b[rows, :].astype(F32)
                for t in turns:
                    grad += got_gn[t - 1, rows, :].astype(F32)
                values = tok[rows, :].astype(F32)
                inv = lax.rsqrt(jnp.mean(values * values, axis=1, keepdims=True) + EPSILON)
                unit = values * inv
                scaled = grad * ng_ref[...]
                inner = jnp.mean(unit * scaled, axis=1, keepdims=True)
                gmid[rows, :] += inv * (scaled - unit * inner)
                gain_one += jnp.sum(grad * unit, axis=0, keepdims=True)
            load("grad_tokens", gmid, gt_out)
            gain_mine[0, 0:1, :] = gain_one
            spare = jnp.zeros((1, gain_one.shape[1] - TILE), F32)
            gain_mine[0, 2:3, :] = jnp.concatenate([gains["q"], spare], axis=1)
            gain_mine[0, 3:4, :] = jnp.concatenate([gains["k"], spare], axis=1)
            gain_mine[0, 4:8, :] = jnp.zeros((4, gain_one.shape[1]), F32)
            send(*gain_copy(0))
            yield
            received("o2", rx2, to_across)
            received("o1", rx1, to_across)
            for mine, theirs in ((own1, rx1), (own2, rx2)):
                tall = mine.shape[0] // 16

                @pl.loop(0, tall)
                def _(r):
                    at = pl.ds(pl.multiple_of(r * 16, 16), 16)
                    mine[at, :] = (mine[at, :].astype(F32) + theirs[at, :].astype(F32)).astype(
                        BF16
                    )

        turn = 0
        order = [1, 0]
        for number, _ in enumerate(compute()):
            if number % 4 == 3:
                tick(rings[order[turn % 2]])
                turn += 1
        for pair in rings[2:]:
            begin(pair)
        step = 0
        while any(ring.left for pair in rings for ring in pair):
            tick(rings[order[turn % 2]])
            turn += 1
            tick(rings[2])
            tick(rings[3])
            if step < len(doubling):
                name, mine, other, device = gain_copy(step)
                received(name, other, device)
                total = gain_mine[step] + gain_in[step]
                if step + 1 < len(doubling):
                    gain_mine[step + 1] = total
                    send(*gain_copy(step + 1))
                else:
                    gains_ref[...] = total
            step += 1
        for pair in rings:
            for ring in pair:
                ring.finish()
        sent("")
        need("output", "grad_tokens")

    depth = x_l.shape[1]
    k_shape = groups_in[0][1].shape
    heads = k_shape[1] // HD
    scratch = [
        pltpu.VMEM((own_rows, depth), F32),
        pltpu.VMEM((own_rows, depth), F32),
        pltpu.VMEM((own_rows, depth), BF16),
        pltpu.VMEM((LEN, TILE), F32),
        pltpu.VMEM((LEN, TILE), F32),
        pltpu.VMEM((heads, LEN, TILE), BF16),
        pltpu.VMEM((2 * heads, LEN, TILE), BF16),
        pltpu.VMEM((heads, LEN, HD), F32),
        pltpu.VMEM((heads, LEN, TILE), F32),
    ]
    scratch += [pltpu.VMEM(ref.shape, ref.dtype) for ref in groups_in[0]]
    if w_all_in.shape != x_r.shape:
        scratch += [pltpu.VMEM(w_all_in.shape, BF16), pltpu.VMEM((LEN, w_all_in.shape[1]), BF16)]
    pl.run_scoped(attention, *scratch)


VM = pl.BlockSpec(memory_space=pltpu.VMEM)
ANY = pl.BlockSpec(memory_space=pl.ANY)
SM = pl.BlockSpec(memory_space=pltpu.SMEM)


def run_forward(length, rows, wq, wk, wv, qs, ks, cosine, sine):
    nq, nk = wq.shape[1], wk.shape[1]
    shape = jax.ShapeDtypeStruct
    return pl.pallas_call(
        attention_forward,
        out_shape=(
            shape((LEN, nq), BF16),
            shape((LEN, nq), BF16),
            shape((LEN, nk), BF16),
            shape((LEN, nk), BF16),
            shape((LEN, nq), F32),
            shape((LEN, nk), F32),
            shape((LEN, nq), F32),
        ),
        in_specs=[SM] + [VM] * 8,
        out_specs=[VM] * 7,
        scratch_shapes=[pltpu.VMEM((nk // HD, LEN, TILE), BF16)],
        compiler_params=pltpu.CompilerParams(vmem_limit_bytes=VMEM_LIMIT),
        cost_estimate=pl.CostEstimate(
            flops=2 * LEN * rows.shape[1] * 2 * nq + 8 * LEN * LEN * nq,
            bytes_accessed=8 * 1024 * 1024,
            transcendentals=0,
        ),
        name="attention_forward",
    )(length, rows, wq, wk, wv, qs, ks, cosine, sine)


def run_main(plan, small, big, group_arrays):
    count, narrow, side = plan["wide"], plan["narrow"], plan["side"]
    shape = jax.ShapeDtypeStruct
    own, depth = big[0].shape
    units = big[2].shape[1]
    sizes = [(depth, 2 * units), (units, depth), (depth, plan["qkv_width"]), (plan["out_rows"], depth)]
    plan = dict(plan, rows=[s[0] for s in sizes], groups=len(group_arrays), own=own)
    full, lands = [], []
    for rows, cols in sizes:
        chunk, forward, backward = ring_rows(rows, count)
        full.append((chunk * count, cols))
        lands += [pltpu.VMEM((count - 1, r, cols), BF16) for r in (forward, backward) if r]
    plan["lands"] = len(lands)
    steps = 2 * (count - 1)
    doubling = int(math.log2(narrow)) + int(math.log2(count))
    dma = pltpu.SemaphoreType.DMA
    inputs = [*small, *big, *[a for arrays in group_arrays for a in arrays]]
    rest = (own, depth)
    mates = (side - 1, own, depth)
    scratch = [pltpu.VMEM((LEN, depth), BF16) for _ in range(4)]
    scratch += [pltpu.VMEM(full[i], BF16) for i in (0, 1, 2, 3, 2, 3, 2, 3)]
    scratch += lands
    scratch += [pltpu.VMEM(mates, BF16) for _ in range(6)]
    scratch += [pltpu.VMEM(rest, BF16) for _ in range(6)]
    scratch += [pltpu.VMEM((doubling, 8, depth), F32) for _ in range(2)]
    moves = 6 + 10 * (side - 1) + doubling
    scratch += [
        dma((len(big) + 9 * len(group_arrays) + 2,)),
        dma((len(lands), steps)),
        dma((len(lands), steps)),
        dma,
        dma((moves,)),
        dma((moves,)),
        pltpu.SemaphoreType.REGULAR,
    ]
    results = pl.pallas_call(
        functools.partial(main_kernel, plan),
        out_shape=tuple(shape(s, BF16) for s in full)
        + (shape(rest, BF16), shape(rest, F32), shape((8, depth), F32)),
        in_specs=[SM] + [VM] * 4 + [ANY] * (len(inputs) - 5),
        out_specs=[ANY] * 6 + [VM],
        scratch_shapes=scratch,
        compiler_params=pltpu.CompilerParams(
            vmem_limit_bytes=BACK_LIMIT, collective_id=1, has_side_effects=True
        ),
        cost_estimate=pl.CostEstimate(
            flops=60 * 10**9, bytes_accessed=64 * 1024 * 1024, transcendentals=0
        ),
        name="main",
    )(*inputs)
    return [r[: s[0]] for r, s in zip(results[:4], sizes)] + list(results[4:])


def on_device(
    wide, narrow,
    tokens, lengths, norm_gain, w_query, w_key, w_value, query_scale, key_scale, w_out,
    ffn_gain, w_gate, w_up, w_down, cotangent,
):
    sequences = lengths.shape[0]
    side = narrow // sequences
    own = tokens.shape[0]
    me = lax.axis_index("narrow")
    place, mine = lax.rem(me, side), me // side

    def across(array, turn=1):
        return lax.ppermute(
            array, "narrow", [(i, (i + turn * side) % narrow) for i in range(narrow)]
        )

    def within(array, turn):
        return lax.ppermute(
            array,
            "narrow",
            [(i, (i // side) * side + (i % side + turn) % side) for i in range(narrow)],
        )

    def gather(array):
        size = array.shape[0]
        whole = jnp.zeros((side * size,) + array.shape[1:], array.dtype)
        whole = lax.dynamic_update_slice(whole, array, (place * size, 0))
        for turn in range(1, side):
            source = lax.rem(place + side - turn, side)
            whole = lax.dynamic_update_slice(whole, within(array, turn), (source * size, 0))
        return whole

    def scatter(parts):
        size = parts.shape[0] // side
        total = lax.dynamic_slice_in_dim(parts, place * size, size).astype(F32)
        for turn in range(1, side):
            target = lax.rem(place + turn, side)
            total += within(
                lax.dynamic_slice_in_dim(parts, target * size, size).astype(BF16), turn
            ).astype(F32)
        return total

    cosine, sine = rope_tables(LEN, HD)
    cosine = jnp.concatenate([cosine] * 4, axis=1)
    sine = jnp.concatenate([-sine, sine, -sine, sine], axis=1)
    qs = jnp.concatenate([query_scale] * 2)[None, :]
    ks = jnp.concatenate([key_scale] * 2)[None, :]
    length = lax.dynamic_slice_in_dim(lengths, mine, 1)

    weights = [(w_query, w_key, w_value, w_out)]
    weights += [tuple(across(w, t) for w in weights[0]) for t in range(1, sequences)]
    joined = w_key.shape[1] % TILE != 0
    if joined:
        weights = [
            tuple(jnp.concatenate(ws, axis=1 if n < 3 else 0) for n, ws in enumerate(zip(*weights)))
        ]

    residual = tokens.astype(F32)
    normed_one, inv_one = row_norm(residual, norm_gain)
    rows_one = gather(normed_one.astype(BF16))
    saved = [run_forward(length, rows_one, *w[:3], qs, ks, cosine, sine) for w in weights]
    mixed = contract(saved[0][0], weights[0][3], 1, 0)
    for s, w in zip(saved[1:], weights[1:]):
        mixed += contract(s[0], w[3], 1, 0)
    middle = residual + scatter(mixed)

    normed_two, inv_two = row_norm(middle, ffn_gain)
    low_two = normed_two.astype(BF16)

    nq, nk = w_query.shape[1], w_key.shape[1]
    if joined:
        order = [0]
        qkv_parts = {
            "own": [(0, nq, 0), (2 * nq, nk, nq), (2 * nq + 2 * nk, nk, nq + nk)],
            "partner": [
                (nq, nq, 0), (2 * nq + nk, nk, nq), (2 * nq + 3 * nk, nk, nq + nk)
            ],
        }
        out_parts = {"own": (0, nq), "partner": (nq, nq)}
    else:
        order = [1, 0]
        qkv_parts = {
            "partner": [(0, nq + 2 * nk, 0)],
            "own": [(nq + 2 * nk, nq + 2 * nk, 0)],
        }
        out_parts = {"partner": (0, nq), "own": (0, nq)}
    plan = {
        "wide": wide, "narrow": narrow, "side": side,
        "qkv_parts": qkv_parts, "out_parts": out_parts,
        "qkv_width": nq + 2 * nk, "out_rows": nq,
    }
    group_arrays = []
    for g in order:
        att, q, k, v, q_raw, k_raw, rinv = saved[g]
        group_arrays.append((q, k, v, att, q_raw, k_raw, rinv, weights[g][3], att.T))
    w_all = jnp.concatenate([w for g in order for w in weights[g][:3]], axis=1)
    sum_gu, sum_down, sum_qkv, sum_out, output, grad_tokens, gains = run_main(
        plan,
        (length, qs, ks, norm_gain[None, :], ffn_gain[None, :]),
        (
            low_two, cotangent, w_gate, w_up, w_down, middle, tokens, cosine, sine,
            rows_one.T, w_all,
        ),
        group_arrays,
    )
    hidden_units = w_gate.shape[1]
    return (
        output,
        grad_tokens,
        gains[0],
        sum_qkv[:, :nq].astype(F32),
        sum_qkv[:, nq : nq + nk].astype(F32),
        sum_qkv[:, nq + nk :].astype(F32),
        gains[2, :HD] + gains[2, HD:TILE],
        gains[3, :HD] + gains[3, HD:TILE],
        sum_out.astype(F32),
        gains[1],
        sum_gu[:, :hidden_units].astype(F32),
        sum_gu[:, hidden_units:].astype(F32),
        sum_down.astype(F32),
    )


def solution(mesh):
    rows = P(("wide", "narrow"), None)
    columns, depth, copied = P(None, "narrow"), P("narrow", None), P()
    return jax.shard_map(
        functools.partial(on_device, mesh.shape["wide"], mesh.shape["narrow"]),
        mesh=mesh,
        in_specs=(
            rows, P("wide"), copied, columns, columns, columns, copied, copied, depth,
            copied, columns, columns, depth, rows,
        ),
        out_specs=(
            rows, rows, copied, columns, columns, columns, copied, copied, depth,
            copied, columns, columns, depth,
        ),
        check_vma=False,
    )
```

```python
import functools
import math

import jax
import jax.numpy as jnp
import numpy as np
from jax import lax
from jax.experimental import pallas as pl
from jax.experimental.pallas import tpu as pltpu
from jax.sharding import PartitionSpec as P

HD = 64
LEN = 1024
BLK = 256
TILE = 2 * HD

EPSILON = 1e-05
ROPE_BASE = 1000000.0
F32 = jnp.float32
BF16 = jnp.bfloat16
BACK_LIMIT = 60 * 1024 * 1024


def rope_tables(length, width):
    half_width = width // 2
    exponents = -(2.0 * np.arange(half_width, dtype=np.float32)) / np.float32(width)
    frequency = np.float32(ROPE_BASE) ** exponents
    angles = np.arange(length, dtype=np.float32)[:, None] * frequency[None, :]
    return (np.cos(angles), np.sin(angles))


def contract(left_side, right_side, left_dim, right_dim):
    return lax.dot_general(
        left_side,
        right_side,
        (((left_dim,), (right_dim,)), ((), ())),
        preferred_element_type=F32,
    )


def lanes(shape):
    return lax.broadcasted_iota(jnp.int32, shape, 1)


def group_ones():
    rows = lax.broadcasted_iota(jnp.int32, (TILE, TILE), 0) // HD
    cols = lax.broadcasted_iota(jnp.int32, (TILE, TILE), 1) // HD
    return jnp.where(rows == cols, 1.0, 0.0).astype(BF16)


def group_sum(values_in, ones):
    high = values_in.astype(BF16)
    rest = (values_in - high.astype(F32)).astype(BF16)
    return contract(high, ones, 1, 0) + contract(rest, ones, 1, 0)


def swap_halves(values_in):
    half = HD // 2
    front = lax.rem(lanes(values_in.shape), HD) < half
    return jnp.where(
        front, pltpu.roll(values_in, TILE - half, 1), pltpu.roll(values_in, half, 1)
    )


class Ring:
    def __init__(self, count, place, target, turn, chunk, first, rows, own, source, out, land, sends, recvs):
        self.count, self.place, self.target, self.turn = count, place, target, turn
        self.chunk, self.first, self.rows = chunk, first, rows
        self.own, self.source, self.out, self.land = own, source, out, land
        self.sends, self.recvs = sends, recvs
        self.done = 0

    def index(self, steps):
        return lax.rem(self.place + self.turn * steps + 2 * self.count, self.count)

    def part(self, ref, steps):
        start = pl.multiple_of(self.index(steps) * self.chunk + self.first, 16)
        return ref.at[pl.ds(start, self.rows), :]

    def copy(self, step, source, target):
        return pltpu.make_async_remote_copy(
            src_ref=source,
            dst_ref=target,
            send_sem=self.sends.at[step],
            recv_sem=self.recvs.at[step],
            device_id={"wide": self.target},
            device_id_type=pl.DeviceIdType.MESH,
        )

    def copy_of(self, step):
        last = self.count - 1
        if step == 0:
            return self.copy(0, self.part(self.source, 0), self.land.at[0])
        if step < last:
            return self.copy(step, self.land.at[step - 1], self.land.at[step])
        steps = last - step + 1
        where = self.part(self.out, steps)
        return self.copy(step, self.land.at[last - 1] if step == last else where, where)

    def begin(self):
        self.copy_of(0).start()

    @property
    def left(self):
        return 2 * (self.count - 1) - self.done

    def tick(self, keep):
        step, last = self.done, self.count - 1
        self.done += 1
        if step < last:
            slot = self.land.at[step]
            self.copy(step, slot, slot).wait_recv()
            start = pl.multiple_of(self.index(-step - 1) * self.chunk + self.first, 16)

            @pl.loop(0, self.rows // 16)
            def _(r):
                at = pl.multiple_of(r * 16, 16)
                mine = self.own[pl.ds(pl.multiple_of(start + at, 16), 16), :].astype(F32)
                slot[pl.ds(at, 16), :] = (slot[pl.ds(at, 16), :].astype(F32) + mine).astype(BF16)

            if step == last - 1:
                kept = pltpu.make_async_copy(slot, self.part(self.out, 1), keep)
                kept.start()
                self.copy_of(last).start()
                kept.wait()
            else:
                self.copy_of(step + 1).start()
        else:
            where = self.part(self.out, last - step)
            self.copy(step, where, where).wait_recv()
            if self.left:
                self.copy_of(step + 1).start()

    def finish(self):
        for step in range(2 * (self.count - 1)):
            self.copy_of(step).wait_send()


def ring_rows(rows, count):
    chunk = -(-rows // (count * 16)) * 16
    forward = -(-chunk // 32) * 16
    return chunk, forward, chunk - forward


def main_kernel(plan, *refs):
    count, narrow, side = plan["wide"], plan["narrow"], plan["side"]
    groups, own_rows = plan["groups"], plan["own"]
    taken = 0

    def take(number):
        nonlocal taken
        taken += number
        return refs[taken - number : taken]

    len_ref, qs_ref, ks_ref, ng_ref, fg_ref = take(5)
    tok_in, cin, wqkv_in, wo_in, wg_in, wu_in, wd_in, cos_in, sin_in = take(9)
    gu_out, gd_out, a1_out, a2_out, out_out, gt_out = take(6)
    mid_in, rows_in, w_all_in, wo_in_all = take(4)
    groups_in = [take(7) for _ in range(groups)]
    (gains_ref,) = take(1)
    x_l, x_r, c_l, c_r = take(4)
    gu_own, gd_own, rx1, rx2 = take(4)
    lands = take(plan["lands"])
    send_b, send_o, got_bl, got_ol, got_br, got_or = take(6)
    got_gn = got_br
    far_b, far_o, own_b, own_o, ownr_b, ownr_o = take(6)
    branch = x_r
    gain_mine, gain_in = take(2)
    load_sems, ring_sends, ring_recvs, keep_sem, sends, recvs, free_sem = take(7)

    w = lax.axis_index("wide")
    n = lax.axis_index("narrow")
    half = count // 2
    place_ring = lax.rem((1 - w % 2) * (count - w // 2) + (w % 2) * (w // 2 + 1), count)

    def at_place(p):
        far = lax.rem(p + count - 1, count) // half
        z = (1 - far) * (p - 1) + far * lax.rem(count - p, count)
        return 2 * z + 1 - far

    onward = at_place(lax.rem(place_ring + 1, count))
    behind = at_place(lax.rem(place_ring + count - 1, count))
    across = lax.rem(n + side, narrow)
    place = lax.rem(n, side)
    turns = range(1, side)

    place_at = [lax.rem(place + turn, side) for turn in range(side)]
    mates_at = [n - place + p for p in place_at]
    block_at = [pl.multiple_of(p * own_rows, BLK) for p in place_at]
    parts = own_rows // BLK
    part_at = [
        [pl.multiple_of(p * own_rows + b * BLK, BLK) for b in range(parts)] for p in place_at
    ]
    far_at = [
        [pl.multiple_of(b * side * BLK + p * BLK, BLK) for b in range(parts)] for p in place_at
    ]

    def mate(turn):
        return mates_at[turn]

    def flip(value, bit):
        return value + bit - 2 * bit * lax.rem(value // bit, 2)

    doubling = [("narrow", 2**e) for e in range(int(math.log2(narrow)))]
    doubling += [("wide", 2**e) for e in range(int(math.log2(count)))]
    partners = [{axis: flip(n if axis == "narrow" else w, bit)} for axis, bit in doubling]
    peers = [{"wide": onward}, {"wide": behind}, {"narrow": across}]
    peers += [{"narrow": mate(t)} for t in turns] + partners

    barrier = pltpu.get_barrier_semaphore()
    for peer in peers:
        pl.semaphore_signal(barrier, inc=1, device_id=peer, device_id_type=pl.DeviceIdType.MESH)
    pl.semaphore_wait(barrier, len(peers))

    numbers = {}
    unsent = []

    def remote(name, source, target, device):
        number = numbers.setdefault(name, len(numbers))
        return pltpu.make_async_remote_copy(
            src_ref=source,
            dst_ref=target,
            send_sem=sends.at[number],
            recv_sem=recvs.at[number],
            device_id=device,
            device_id_type=pl.DeviceIdType.MESH,
        )

    def send(name, source, target, device):
        copy = remote(name, source, target, device)
        copy.start()
        unsent.append((name, source, target, device))

    def sent(name):
        for entry in [e for e in unsent if e[0][: len(name)] == name]:
            remote(*entry).wait_send()
            unsent.remove(entry)

    def received(name, target, device):
        remote(name, target, target, device).wait_recv()

    def block(ref, turn):
        return ref.at[pl.ds(block_at[turn % side], own_rows), :]

    to_across = {"narrow": across}

    def to_mates(name, source, target):
        for t in turns:
            send(f"{name}{t}", source, target, {"narrow": mate(t)})

    def from_mates(name, ref):
        for t in turns:
            received(f"{name}{t}", block(ref, side - t), {"narrow": mate(t)})

    def part(ref, turn, b):
        return ref.at[pl.ds(part_at[turn % side][b], BLK), :]

    def far_part(ref, turn, b):
        return ref.at[pl.ds(far_at[turn % side][b], BLK), :]

    loading = {}

    def load(name, source, target):
        number = len(loading)
        loading[name] = [lambda: pltpu.make_async_copy(source, target, load_sems.at[number])]
        loading[name][0]().start()

    def need(*names):
        for name in names:
            if loading[name]:
                loading[name].pop()().wait()

    rings = []
    used = 0

    def add_ring(own, out, rows):
        nonlocal used
        chunk, forward, backward = ring_rows(rows, count)
        pair = []
        for turn, target, first, size in ((1, onward, 0, forward), (-1, behind, forward, backward)):
            if size:
                pair.append(
                    Ring(
                        count, place_ring, target, turn, chunk, first, size, own, own, out,
                        lands[used], ring_sends.at[used], ring_recvs.at[used],
                    )
                )
                used += 1
        rings.append(pair)

    add_ring(gu_own, gu_out, plan["rows"][0])
    add_ring(gd_own, gd_out, plan["rows"][1])

    def begin(pair):
        for ring in pair:
            ring.begin()

    def tick(pair):
        for ring in pair:
            if ring.left:
                ring.tick(keep_sem)

    depth = x_l.shape[1]
    nq, nk = plan["nq"], plan["nk"]
    joined = groups == 1
    scale_many = 2 if joined else 1
    gq, gk = nq * scale_many, nk * scale_many
    heads = gk // HD
    rows_one = gd_own

    def causal_mask(shape, row_axis):
        rows_id = lax.rem(lax.broadcasted_iota(jnp.int32, shape, row_axis), BLK)
        return lax.broadcasted_iota(jnp.int32, shape, 1 - row_axis) <= rows_id

    def forward(tok, wqkv, wo, cos_ref, sin_ref, mid, vaug_ref, *rest):
        saved = [rest[7 * g : 7 * g + 7] for g in range(groups)]
        send("w1", wqkv_in, rx1, to_across)
        send("w2", wo_in, rx2.at[0:nq, :], to_across)
        for b in range(parts - 1):
            send(f"cy{b}", cin.at[b * BLK : (b + 1) * BLK, :], far_part(c_r, 0, b), to_across)
        load("tok", tok_in, tok)
        load("wqkv", wqkv_in, wqkv)
        load("cos", cos_in, cos_ref)
        load("sin", sin_in, sin_ref)
        load("wo", wo_in, wo)
        load("c", cin, block(c_l, 0))

        length = len_ref[0]
        ones = group_ones()
        lane = lanes((BLK, TILE))
        causal = causal_mask((2 * BLK, BLK), 0)

        need("tok")
        for b in range(parts):
            values = tok[b * BLK : (b + 1) * BLK, :].astype(F32)
            inv = lax.rsqrt(jnp.mean(values * values, axis=1, keepdims=True) + EPSILON)
            mine = part(rows_one, 0, b)
            mine[...] = (values * inv * ng_ref[...]).astype(BF16)
            to_mates(f"r{b}_", mine, mine)
        to_mates("cl", cin, block(c_l, 0))

        def norm_rope(raw, scale, cosine, sine):
            inv = lax.rsqrt(group_sum(raw * raw, ones) * (1.0 / HD) + EPSILON)
            scaled = raw * inv * scale
            return scaled * cosine + swap_halves(scaled) * sine

        def project(g, weight, at):
            q_ref, k_ref, v_ref, _, qraw_ref, kraw_ref, _ = saved[g]
            rows = pl.ds(pl.multiple_of(at, BLK), BLK)
            cosine, sine = cos_ref[rows, :], sin_ref[rows, :]
            real = (lax.broadcasted_iota(jnp.int32, (BLK, TILE), 0) + at) < length
            raw = contract(rows_one[rows, :], weight[...], 1, 0)
            qraw_ref[rows, :] = raw[:, :gq]
            kraw_ref[rows, :] = raw[:, gq : gq + gk]
            for t in range(heads):
                cols = slice(t * TILE, (t + 1) * TILE)
                turned = norm_rope(raw[:, cols], qs_ref[...], cosine, sine)
                q_ref[rows, cols] = (turned * (1.0 / math.sqrt(HD))).astype(BF16)
            for t in range(heads // 2):
                cols = slice(t * TILE, (t + 1) * TILE)
                k_raw = raw[:, gq + t * TILE : gq + (t + 1) * TILE]
                turned = norm_rope(k_raw, ks_ref[...], cosine, sine)
                k_ref[rows, cols] = jnp.where(real, turned, 0.0).astype(BF16)
                v_raw = raw[:, gq + gk + t * TILE : gq + gk + (t + 1) * TILE]
                v_pair = jnp.where(real, v_raw, 0.0)
                v_ref[rows, cols] = v_pair.astype(BF16)
                mark = jnp.where(real & (lane == HD), 1.0, 0.0)
                vaug_ref[2 * t, rows, :] = jnp.where(lane < HD, v_pair, mark).astype(BF16)
                vaug_ref[2 * t + 1, rows, :] = jnp.where(
                    lane < HD, pltpu.roll(v_pair, HD, 1), mark
                ).astype(BF16)

        def attend(g):
            q_ref, k_ref, _, att_ref, _, _, rinv_ref = saved[g]
            for h in range(heads):
                for i in range(LEN // BLK):
                    rows = slice(i * BLK, (i + 1) * BLK)
                    low = h * TILE
                    q_two = jnp.concatenate(
                        [q_ref[rows, low : low + HD], q_ref[rows, low + HD : low + TILE]], axis=0
                    )
                    total = jnp.zeros((2 * BLK, TILE), F32)
                    for j in range(i + 1):
                        keys = slice(j * BLK, (j + 1) * BLK)
                        scores = contract(q_two, k_ref[keys, h * HD : (h + 1) * HD], 1, 1)
                        weight = jnp.exp(scores)
                        if i == j:
                            weight = jnp.where(causal, weight, 0.0)
                        total += contract(weight.astype(BF16), vaug_ref[h, keys, :], 1, 0)
                    inv = 1.0 / total[:, HD : HD + 1]
                    mixed = total[:, :HD] * inv
                    wide_inv = jnp.broadcast_to(inv, (2 * BLK, HD))
                    att_ref[rows, low : low + HD] = mixed[:BLK].astype(BF16)
                    att_ref[rows, low + HD : low + TILE] = mixed[BLK:].astype(BF16)
                    rinv_ref[rows, low : low + HD] = wide_inv[:BLK]
                    rinv_ref[rows, low + HD : low + TILE] = wide_inv[BLK:]
            for i in range(7):
                load(f"save{g}_{i}", saved[g][i], groups_in[g][i])

        def arrive():
            received("w1", rx1, to_across)
            received("w2", rx2.at[0:nq, :], to_across)

        need("wqkv", "cos", "sin")
        if joined:
            wj, woj = rest[7 * groups :]
            arrive()
            need("wo")
            to = 0
            for first, size in ((0, nq), (nq, nk), (nq + nk, nk)):
                for source in (wqkv, rx1):
                    wj[:, to : to + size] = source[:, first : first + size]
                    to += size
            woj[:nq, :] = wo[...]
            woj[nq:, :] = rx2[0:nq, :]
            rounds = [(0, wj)]
            outs = [(0, woj)]
        else:
            rounds = [(1, wqkv), (0, rx1)]
            outs = [(1, wo), (0, rx2.at[0:nq, :])]
        for number, (g, weight) in enumerate(rounds):
            if number:
                received("w1", rx1, to_across)
            for t in range(side):
                for b in range(parts):
                    if t and not number:
                        received(f"r{b}_{t}", part(rows_one, side - t, b), {"narrow": mate(t)})
                    turn = side - t if t else 0
                    project(g, weight, part_at[turn][b])
            if not number:
                load("save_rows", rows_one.at[0:LEN, :], rows_in)
            attend(g)
        if joined:
            load("save_w", wj, w_all_in)
            load("save_wo", woj, wo_in_all)
        else:
            need("wo")
            received("w2", rx2.at[0:nq, :], to_across)
            half_width = wqkv.shape[1]
            load("save_w0", rx1, w_all_in.at[:, 0:half_width])
            load("save_w1", wqkv, w_all_in.at[:, half_width : 2 * half_width])
            load("save_wo0", rx2.at[0:nq, :], wo_in_all.at[0:nq, :])
            load("save_wo1", wo, wo_in_all.at[nq : 2 * nq, :])

        def mix(at):
            rows = pl.ds(pl.multiple_of(at, BLK), BLK)
            total = 0.0
            for g, weight in outs:
                total += contract(saved[g][3][rows, :], weight[...], 1, 0)
            return total

        for b in range(parts):
            here = slice(b * BLK, (b + 1) * BLK)
            for t in turns:
                send_b[t - 1, here, :] = mix(part_at[t][b]).astype(BF16)
                send(
                    f"mx{b}_{t}", send_b.at[t - 1, here, :], got_bl.at[t - 1, here, :],
                    {"narrow": mate(t)},
                )
        for b in range(parts):
            here = slice(b * BLK, (b + 1) * BLK)
            total = tok[here, :].astype(F32) + mix(part_at[0][b])
            for t in turns:
                received(f"mx{b}_{t}", got_bl.at[t - 1, here, :], {"narrow": mate(t)})
                total += got_bl[t - 1, here, :].astype(F32)
            mid[here, :] = total
            inv = lax.rsqrt(jnp.mean(total * total, axis=1, keepdims=True) + EPSILON)
            mine = part(x_l, 0, b)
            mine[...] = (total * inv * fg_ref[...]).astype(BF16)
            send(f"xy{b}", mine, far_part(x_r, 0, b), to_across)
            to_mates(f"xl{b}_", mine, mine)
        last = parts - 1
        send(f"cy{last}", cin.at[last * BLK : own_rows, :], far_part(c_r, 0, last), to_across)
        load("save_mid", mid, mid_in)
        sent("mx")
        sent("r")
        for name in [name for name in loading if name.startswith("save")]:
            need(name)

    own_tile = (own_rows, depth)
    scratch = [
        pltpu.VMEM(own_tile, BF16),
        pltpu.VMEM(wqkv_in.shape, BF16),
        pltpu.VMEM(wo_in.shape, BF16),
        pltpu.VMEM((LEN, TILE), F32),
        pltpu.VMEM((LEN, TILE), F32),
        pltpu.VMEM(own_tile, F32),
        pltpu.VMEM((heads, LEN, TILE), BF16),
    ]
    scratch += [pltpu.VMEM(ref.shape, ref.dtype) for group in groups_in for ref in group]
    if joined:
        scratch += [pltpu.VMEM(w_all_in.shape, BF16), pltpu.VMEM(wo_in_all.shape, BF16)]
    pl.run_scoped(forward, *scratch)

    units = wg_in.shape[1]
    cuts = [0, units // 2 // 128 * 128 + 128, units] if units % 128 == 0 else [0, units]

    def feed_forward(wg, wu, wd, hid, gg, gu):
        load("wg", wg_in, wg)
        load("wu", wu_in, wu)
        load("wd", wd_in, wd)

        def rows_pass(x, c, at, back_to, out_to):
            rows = pl.ds(pl.multiple_of(at, BLK), BLK)
            for first, end in zip(cuts, cuts[1:]):
                cols = slice(first, end)
                gate = contract(x[rows, :], wg[:, cols], 1, 0)
                up = contract(x[rows, :], wu[:, cols], 1, 0)
                grad = contract(c[rows, :], wd[cols, :], 1, 1)
                share = 1.0 / (1.0 + jnp.exp(-gate))
                silu = gate * share
                hid[rows, cols] = (silu * up).astype(BF16)
                gg[rows, cols] = (grad * up * (share + silu * (1.0 - share))).astype(BF16)
                gu[rows, cols] = (grad * silu).astype(BF16)
            back = contract(gg[rows, :], wg[...], 1, 1)
            back += contract(gu[rows, :], wu[...], 1, 1)
            back_to[...] = back.astype(BF16)
            out_to[...] = contract(hid[rows, :], wd[...], 1, 0).astype(BF16)

        def near_pass(turn, back_to, out_to):
            @pl.loop(0, parts)
            def _(b):
                to = pl.ds(pl.multiple_of(b * BLK, BLK), BLK)
                at = block_at[turn] + b * BLK
                rows_pass(x_l, c_l, at, back_to.at[to, :], out_to.at[to, :])

        def weight_pass(x, c, rows, more, last):
            step = 384 if units % 384 == 0 else units
            for start in range(0, units, step):
                cols = slice(start, start + step)
                total = contract(hid[rows, cols], c[rows, :], 0, 0)
                if more:
                    total += gd_own[cols, :].astype(F32)
                gd_own[cols, :] = total.astype(BF16)
            if last:
                begin(rings[1])
            for start in range(0, depth, BLK):
                to = slice(start, start + BLK)
                for first, grad in ((0, gg), (units, gu)):
                    total = contract(x[rows, to], grad[rows, :], 0, 0)
                    cols = slice(first, first + units)
                    if more:
                        total += gu_own[to, cols].astype(F32)
                    gu_own[to, cols] = total.astype(BF16)

        extra = gd_own.shape[0] - units
        if extra:
            gd_own[units:, :] = jnp.zeros((extra, depth), BF16)
        need("wg", "wu", "c", "wd")
        near_pass(0, own_b, own_o)
        for b in range(parts):
            for t in turns:
                received(f"xl{b}_{t}", part(x_l, side - t, b), {"narrow": mate(t)})
        from_mates("cl", c_l)
        for t in turns:
            near_pass(t, send_b.at[t - 1], send_o.at[t - 1])
            send(f"bl{t}", send_b.at[t - 1], got_bl.at[t - 1], {"narrow": mate(t)})
            send(f"ol{t}", send_o.at[t - 1], got_ol.at[t - 1], {"narrow": mate(t)})

        def pass_on(b):
            for name, ref in (("x", x_r), ("c", c_r)):
                mine = far_part(ref, 0, b)
                received(f"{name}y{b}", mine, to_across)
                to_mates(f"{name}r{b}_", mine, mine)

        weight_pass(x_l, c_l, slice(0, LEN), False, False)
        sent("bl")
        sent("ol")
        for b in range(parts):
            here = slice(b * BLK, (b + 1) * BLK)
            pass_on(b)
            for t in turns:
                for name, ref in (("x", x_r), ("c", c_r)):
                    received(f"{name}r{b}_{t}", far_part(ref, side - t, b), {"narrow": mate(t)})
            for t in turns:
                back, out = send_b.at[t - 1, here, :], send_o.at[t - 1, here, :]
                rows_pass(x_r, c_r, far_at[t][b], back, out)
                send(f"br{b}_{t}", back, got_br.at[t - 1, here, :], {"narrow": mate(t)})
                send(f"or{b}_{t}", out, got_or.at[t - 1, here, :], {"narrow": mate(t)})
            rows_pass(x_r, c_r, far_at[0][b], ownr_b.at[here, :], ownr_o.at[here, :])
            for name, mine, got in (("b", ownr_b, got_br), ("o", ownr_o, got_or)):
                for t in turns:
                    received(f"{name}r{b}_{t}", got.at[t - 1, here, :], {"narrow": mate(t)})

                @pl.loop(0, BLK // 32)
                def _(r):
                    rows = pl.ds(pl.multiple_of(b * BLK + r * 32, 32), 32)
                    total = mine[rows, :].astype(F32)
                    for t in turns:
                        total += got[t - 1, rows, :].astype(F32)
                    mine[rows, :] = total.astype(BF16)

                if name == "b":
                    send(f"by{b}", ownr_b.at[here, :], far_b.at[here, :], to_across)
            last = b == parts - 1
            if last:
                send("oy", ownr_o, far_o, to_across)
            weight_pass(x_r, c_r, slice(b * side * BLK, (b + 1) * side * BLK), True, last)
        begin(rings[0])
        for name in ("w", "x", "c", "br", "or"):
            sent(name)

    weights = [pltpu.VMEM(ref.shape, BF16) for ref in (wg_in, wu_in, wd_in)]
    pl.run_scoped(feed_forward, *weights, *[pltpu.VMEM((LEN, units), BF16) for _ in range(3)])

    for t in turns:
        pl.semaphore_signal(
            free_sem, inc=1, device_id={"narrow": mate(t)}, device_id_type=pl.DeviceIdType.MESH
        )

    def attention(mid, gmid, tok, cos_ref, sin_ref, vaug_ref, aug_ref, dk_ref, dv_ref, *rest):
        px1, px2, own1, own2 = rest[:4]
        add_ring(own1, a1_out, plan["rows"][2])
        add_ring(own2, a2_out, plan["rows"][3])
        group = rest[4:12]
        spare = list(rest[12:])
        w_all = c_l if w_all_in.shape == x_r.shape else spare.pop(0)
        all_ref = x_l if w_all_in.shape == x_r.shape else spare.pop(0)
        first_rows = c_r
        q_ref, k_ref, v_ref, att_ref, qraw_ref, kraw_ref, rinv_ref, wo_ref = group

        load("mid_back", mid_in, mid)

        def load_group(g):
            sources = [*groups_in[g], wo_in_all.at[g * gq : (g + 1) * gq, :]]
            for i, (source, target) in enumerate(zip(sources, group)):
                load(f"group{g}_{i}", source, target)

        def need_group(g):
            need(*[f"group{g}_{i}" for i in range(8)])

        load_group(0)
        load("cos_back", cos_in, cos_ref)
        load("sin_back", sin_in, sin_ref)
        load("rows", rows_in, first_rows)
        load("tok_back", tok_in, tok)

        length = len_ref[0]
        ones = group_ones()
        lane = lanes((BLK, TILE))
        width = w_all.shape[1] // groups
        gains = {"q": jnp.zeros((1, TILE), F32), "k": jnp.zeros((1, TILE), F32)}
        causal = causal_mask((BLK, 2 * BLK), 1)

        def turn_back(grad, cosine, sine):
            return grad * cosine - swap_halves(grad) * sine

        def norm_back(raw, turned, scale):
            inv = lax.rsqrt(group_sum(raw * raw, ones) * (1.0 / HD) + EPSILON)
            scaled = turned * scale
            unit = raw * inv
            inner = group_sum(unit * scaled, ones) * (1.0 / HD)
            gain = jnp.sum(turned * unit, axis=0, keepdims=True)
            return inv * (scaled - unit * inner), gain

        def attention_pieces(g):
            base = g * width
            for start in range(0, LEN, BLK):
                rows = slice(start, start + BLK)
                grad = contract(branch[rows, :], wo_ref[...], 1, 1).astype(BF16).astype(F32)
                for t in range(heads):
                    cols = slice(t * TILE, (t + 1) * TILE)
                    part = (grad[:, cols] * rinv_ref[rows, cols]).astype(BF16).astype(F32)
                    inner = group_sum(part * att_ref[rows, cols].astype(F32), ones)
                    for which in range(2):
                        mine = part if which == 0 else pltpu.roll(part, HD, 1)
                        sums = pltpu.roll(inner, HD, 1) if which == 0 else inner
                        high = sums.astype(BF16).astype(F32)
                        tail = jnp.where(
                            lane == HD, -high, jnp.where(lane == HD + 1, high - sums, 0.0)
                        )
                        aug_ref[2 * t + which, rows, :] = jnp.where(lane < HD, mine, tail).astype(
                            BF16
                        )
                for t in range(heads // 2):
                    v_pair = v_ref[rows, t * TILE : (t + 1) * TILE].astype(F32)
                    mark = jnp.where(lane < HD + 2, 1.0, 0.0)
                    vaug_ref[2 * t, rows, :] = jnp.where(lane < HD, v_pair, mark).astype(BF16)
                    vaug_ref[2 * t + 1, rows, :] = jnp.where(
                        lane < HD, pltpu.roll(v_pair, HD, 1), mark
                    ).astype(BF16)
                dk_ref[:, rows, :] = jnp.zeros((heads, BLK, HD), F32)
                dv_ref[:, rows, :] = jnp.zeros((heads, BLK, TILE), F32)
                yield

            for h in range(heads):
                keys_turned = jnp.transpose(
                    k_ref[:, (h // 2) * TILE : (h // 2 + 1) * TILE].astype(F32)
                )[(h % 2) * HD : (h % 2 + 1) * HD].astype(BF16)
                for i in range(LEN // BLK):
                    rows = slice(i * BLK, (i + 1) * BLK)
                    low = h * TILE
                    q_two = jnp.concatenate(
                        [q_ref[rows, low : low + HD], q_ref[rows, low + HD : low + TILE]], axis=0
                    )
                    aug = jnp.concatenate(
                        [aug_ref[2 * h, rows, :], aug_ref[2 * h + 1, rows, :]], axis=0
                    )
                    dq = jnp.zeros((HD, 2 * BLK), F32)
                    for j in range(i + 1):
                        keys = slice(j * BLK, (j + 1) * BLK)
                        weight = jnp.exp(
                            contract(k_ref[keys, h * HD : (h + 1) * HD], q_two, 1, 1)
                        )
                        if i == j:
                            weight = jnp.where(causal, weight, 0.0)
                        slope = (weight * contract(vaug_ref[h, keys, :], aug, 1, 1)).astype(BF16)
                        dv_ref[h, keys, :] += contract(weight.astype(BF16), aug, 1, 0)
                        dk_ref[h, keys, :] += contract(slope, q_two, 1, 0)
                        dq += contract(keys_turned[:, keys], slope, 1, 0)
                    both = jnp.concatenate([dq[:, :BLK], dq[:, BLK:]], axis=0)
                    grad = jnp.transpose(both) * (1.0 / math.sqrt(HD))
                    turned = turn_back(grad, cos_ref[rows, :], sin_ref[rows, :])
                    out, gain = norm_back(qraw_ref[rows, low : low + TILE], turned, qs_ref[...])
                    all_ref[rows, base + low : base + low + TILE] = out.astype(BF16)
                    gains["q"] += gain
                    yield

            for start in range(0, LEN, BLK):
                rows = slice(start, start + BLK)
                real = (lax.broadcasted_iota(jnp.int32, (BLK, TILE), 0) + start) < length
                for t in range(heads // 2):
                    low = base + gq + t * TILE
                    grad = jnp.concatenate(
                        [dk_ref[2 * t, rows, :], dk_ref[2 * t + 1, rows, :]], axis=1
                    )
                    grad = jnp.where(real, grad, 0.0)
                    turned = turn_back(grad, cos_ref[rows, :], sin_ref[rows, :])
                    out, gain = norm_back(
                        kraw_ref[rows, t * TILE : (t + 1) * TILE], turned, ks_ref[...]
                    )
                    all_ref[rows, low : low + TILE] = out.astype(BF16)
                    gains["k"] += gain
                    values = jnp.where(
                        lane < HD,
                        dv_ref[2 * t, rows, :],
                        pltpu.roll(dv_ref[2 * t + 1, rows, :], HD, 1),
                    )
                    all_ref[rows, low + gk : low + gk + TILE] = jnp.where(
                        real, values, 0.0
                    ).astype(BF16)
                yield

        def out_grads(which, target):
            first, size = plan["out_parts"][which]
            target[:size, :] = contract(
                att_ref[:, first : first + size], branch[...], 0, 0
            ).astype(BF16)
            if target.shape[0] > size:
                target[size:, :] = jnp.zeros((target.shape[0] - size, target.shape[1]), BF16)

        def qkv_grads(which, target):
            for start in range(0, depth, BLK):
                rows = slice(start, start + BLK)
                for source, size, to in plan["qkv_parts"][which]:
                    target[rows, to : to + size] = contract(
                        first_rows[:, rows], all_ref[:, source : source + size], 0, 0
                    ).astype(BF16)
                yield

        def gain_copy(step):
            return (f"gain{step}", gain_mine.at[step], gain_in.at[step], partners[step])

        def compute():
            need("mid_back")
            for t in turns:
                received(f"bl{t}", got_bl.at[t - 1], {"narrow": mate(t)})
            tick(rings[1])
            gain_two = jnp.zeros((1, fg_ref.shape[1]), F32)
            own_branch, own_cot = block(branch, 0), block(c_l, 0)
            for start in range(0, own_rows, 64):
                rows = slice(start, start + 64)
                if start % BLK == 0:
                    received(f"by{start // BLK}", far_b.at[start : start + BLK, :], to_across)
                grad = own_b[rows, :].astype(F32) + far_b[rows, :].astype(F32)
                for t in turns:
                    grad += got_bl[t - 1, rows, :].astype(F32)
                values = mid[rows, :]
                inv = lax.rsqrt(jnp.mean(values * values, axis=1, keepdims=True) + EPSILON)
                unit = values * inv
                scaled = grad * fg_ref[...]
                inner = jnp.mean(unit * scaled, axis=1, keepdims=True)
                total = own_cot[rows, :].astype(F32) + inv * (scaled - unit * inner)
                gmid[rows, :] = total
                own_branch[rows, :] = total.astype(BF16)
                gain_two += jnp.sum(grad * unit, axis=0, keepdims=True)
            load("w_all", w_all_in, w_all)
            gain_mine[0, 1:2, :] = gain_two
            pl.semaphore_wait(free_sem, side - 1)
            to_mates("gb", own_branch, own_branch)
            need_group(0)
            need("cos_back", "sin_back")
            from_mates("gb", branch)
            yield
            out_grads("partner", px2)
            send("o2", px2, rx2, to_across)
            if groups == 1:
                out_grads("own", own2)
            yield
            yield from attention_pieces(0)
            need("rows")
            yield from qkv_grads("partner", px1)
            send("o1", px1, rx1, to_across)
            if groups > 1:
                load_group(1)
            for t in turns:
                received(f"ol{t}", got_ol.at[t - 1], {"narrow": mate(t)})
            received("oy", far_o, to_across)
            for start in range(0, own_rows, 64):
                rows = slice(start, start + 64)
                total = mid[rows, :] + own_o[rows, :].astype(F32) + far_o[rows, :].astype(F32)
                for t in turns:
                    total += got_ol[t - 1, rows, :].astype(F32)
                own_o[rows, :] = total.astype(BF16)
            load("output", own_o, out_out)
            yield
            if groups > 1:
                need_group(1)
                out_grads("own", own2)
                yield
                yield from attention_pieces(1)
            yield from qkv_grads("own", own1)
            need("w_all", "tok_back")
            sent("by")
            for turn in [*turns, 0]:
                for start in range(0, own_rows, BLK):
                    at = pl.multiple_of(lax.rem(place + turn, side) * own_rows + start, BLK)
                    grad = contract(all_ref[pl.ds(at, BLK), :], w_all[...], 1, 1).astype(BF16)
                    if turn:
                        send_b[turn - 1, start : start + BLK, :] = grad
                    else:
                        own_b[start : start + BLK, :] = grad
                    yield
                if turn:
                    send(
                        f"gn{turn}", send_b.at[turn - 1], got_gn.at[turn - 1], {"narrow": mate(turn)}
                    )
            for t in turns:
                received(f"gn{t}", got_gn.at[t - 1], {"narrow": mate(t)})
            gain_one = jnp.zeros((1, ng_ref.shape[1]), F32)
            for start in range(0, own_rows, 64):
                rows = slice(start, start + 64)
                grad = own_b[rows, :].astype(F32)
                for t in turns:
                    grad += got_gn[t - 1, rows, :].astype(F32)
                values = tok[rows, :].astype(F32)
                inv = lax.rsqrt(jnp.mean(values * values, axis=1, keepdims=True) + EPSILON)
                unit = values * inv
                scaled = grad * ng_ref[...]
                inner = jnp.mean(unit * scaled, axis=1, keepdims=True)
                gmid[rows, :] += inv * (scaled - unit * inner)
                gain_one += jnp.sum(grad * unit, axis=0, keepdims=True)
            load("grad_tokens", gmid, gt_out)
            gain_mine[0, 0:1, :] = gain_one
            spare = jnp.zeros((1, gain_one.shape[1] - TILE), F32)
            gain_mine[0, 2:3, :] = jnp.concatenate([gains["q"], spare], axis=1)
            gain_mine[0, 3:4, :] = jnp.concatenate([gains["k"], spare], axis=1)
            gain_mine[0, 4:8, :] = jnp.zeros((4, gain_one.shape[1]), F32)
            send(*gain_copy(0))
            yield
            received("o2", rx2, to_across)
            received("o1", rx1, to_across)
            for mine, theirs in ((own1, rx1), (own2, rx2)):
                tall = mine.shape[0] // 16

                @pl.loop(0, tall)
                def _(r):
                    at = pl.ds(pl.multiple_of(r * 16, 16), 16)
                    mine[at, :] = (mine[at, :].astype(F32) + theirs[at, :].astype(F32)).astype(
                        BF16
                    )

        turn = 0
        order = [1, 0]
        for number, _ in enumerate(compute()):
            if number % 4 == 3:
                tick(rings[order[turn % 2]])
                turn += 1
        for pair in rings[2:]:
            begin(pair)
        step = 0
        while any(ring.left for pair in rings for ring in pair):
            tick(rings[order[turn % 2]])
            turn += 1
            tick(rings[2])
            tick(rings[3])
            if step < len(doubling):
                name, mine, other, device = gain_copy(step)
                received(name, other, device)
                total = gain_mine[step] + gain_in[step]
                if step + 1 < len(doubling):
                    gain_mine[step + 1] = total
                    send(*gain_copy(step + 1))
                else:
                    gains_ref[...] = total
            step += 1
        for pair in rings:
            for ring in pair:
                ring.finish()
        sent("")
        need("output", "grad_tokens")

    scratch = [
        pltpu.VMEM((own_rows, depth), F32),
        pltpu.VMEM((own_rows, depth), F32),
        pltpu.VMEM((own_rows, depth), BF16),
        pltpu.VMEM((LEN, TILE), F32),
        pltpu.VMEM((LEN, TILE), F32),
        pltpu.VMEM((heads, LEN, TILE), BF16),
        pltpu.VMEM((2 * heads, LEN, TILE), BF16),
        pltpu.VMEM((heads, LEN, HD), F32),
        pltpu.VMEM((heads, LEN, TILE), F32),
    ]
    scratch += [pltpu.VMEM(ref.shape, BF16) for ref in (rx1, rx2, rx1, rx2)]
    scratch += [pltpu.VMEM(ref.shape, ref.dtype) for ref in groups_in[0]]
    scratch += [pltpu.VMEM((gq, depth), BF16)]
    if w_all_in.shape != x_r.shape:
        scratch += [pltpu.VMEM(w_all_in.shape, BF16), pltpu.VMEM((LEN, w_all_in.shape[1]), BF16)]
    pl.run_scoped(attention, *scratch)


VM = pl.BlockSpec(memory_space=pltpu.VMEM)
ANY = pl.BlockSpec(memory_space=pl.ANY)
SM = pl.BlockSpec(memory_space=pltpu.SMEM)


def run_main(plan, small, big):
    count, narrow, side = plan["wide"], plan["narrow"], plan["side"]
    shape = jax.ShapeDtypeStruct
    own, depth = big[0].shape
    units = big[4].shape[1]
    nq, nk, groups = plan["nq"], plan["nk"], plan["groups"]
    sizes = [(depth, 2 * units), (units, depth), (depth, nq + 2 * nk), (nq, depth)]
    plan = dict(plan, rows=[s[0] for s in sizes], own=own)
    full, lands = [], []
    for rows, cols in sizes:
        chunk, forward, backward = ring_rows(rows, count)
        full.append((chunk * count, cols))
        lands += [pltpu.VMEM((count - 1, r, cols), BF16) for r in (forward, backward) if r]
    plan["lands"] = len(lands)
    steps = 2 * (count - 1)
    doubling = int(math.log2(narrow)) + int(math.log2(count))
    dma = pltpu.SemaphoreType.DMA
    rest = (own, depth)
    mates = (side - 1, own, depth)
    scratch = [pltpu.VMEM((LEN, depth), BF16) for _ in range(4)]
    scratch += [pltpu.VMEM(shape, BF16) for shape in full]
    scratch += lands
    scratch += [pltpu.VMEM(mates, BF16) for _ in range(6)]
    scratch += [pltpu.VMEM(rest, BF16) for _ in range(6)]
    scratch += [pltpu.VMEM((doubling, 8, depth), F32) for _ in range(2)]
    parts = own // BLK
    moves = 4 + 4 * parts + (side - 1) * (7 * parts + 5) + doubling
    scratch += [
        dma((80,)),
        dma((len(lands), steps)),
        dma((len(lands), steps)),
        dma,
        dma((moves,)),
        dma((moves,)),
        pltpu.SemaphoreType.REGULAR,
    ]
    gq, gk = 2 * nq // groups, 2 * nk // groups
    kept = [shape(rest, F32), shape((LEN, depth), BF16)]
    kept += [shape((depth, 2 * (nq + 2 * nk)), BF16), shape((2 * nq, depth), BF16)]
    for _ in range(groups):
        kept += [shape((LEN, gq), BF16), shape((LEN, gk), BF16), shape((LEN, gk), BF16)]
        kept += [shape((LEN, gq), BF16), shape((LEN, gq), F32), shape((LEN, gk), F32)]
        kept += [shape((LEN, gq), F32)]
    results = pl.pallas_call(
        functools.partial(main_kernel, plan),
        out_shape=tuple(shape(s, BF16) for s in full)
        + (shape(rest, BF16), shape(rest, F32), *kept, shape((8, depth), F32)),
        in_specs=[SM] + [VM] * 4 + [ANY] * len(big),
        out_specs=[ANY] * (6 + len(kept)) + [VM],
        scratch_shapes=scratch,
        compiler_params=pltpu.CompilerParams(
            vmem_limit_bytes=BACK_LIMIT, collective_id=1, has_side_effects=True
        ),
        cost_estimate=pl.CostEstimate(
            flops=60 * 10**9, bytes_accessed=64 * 1024 * 1024, transcendentals=0
        ),
        name="main",
    )(*small, *big)
    return [r[: s[0]] for r, s in zip(results[:4], sizes)] + [*results[4:6], results[-1]]


def on_device(
    wide, narrow,
    tokens, lengths, norm_gain, w_query, w_key, w_value, query_scale, key_scale, w_out,
    ffn_gain, w_gate, w_up, w_down, cotangent,
):
    sequences = lengths.shape[0]
    side = narrow // sequences
    mine = lax.axis_index("narrow") // side
    cosine, sine = rope_tables(LEN, HD)
    cosine = jnp.asarray(np.concatenate([cosine] * 4, axis=1))
    sine = jnp.asarray(np.concatenate([-sine, sine, -sine, sine], axis=1))
    qs = jnp.concatenate([query_scale] * 2)[None, :]
    ks = jnp.concatenate([key_scale] * 2)[None, :]
    length = lax.dynamic_slice_in_dim(lengths, mine, 1)

    nq, nk = w_query.shape[1], w_key.shape[1]
    if nk % TILE:
        groups = 1
        qkv_parts = {
            "own": [(0, nq, 0), (2 * nq, nk, nq), (2 * nq + 2 * nk, nk, nq + nk)],
            "partner": [
                (nq, nq, 0), (2 * nq + nk, nk, nq), (2 * nq + 3 * nk, nk, nq + nk)
            ],
        }
        out_parts = {"own": (0, nq), "partner": (nq, nq)}
    else:
        groups = 2
        qkv_parts = {
            "partner": [(0, nq + 2 * nk, 0)],
            "own": [(nq + 2 * nk, nq + 2 * nk, 0)],
        }
        out_parts = {"partner": (0, nq), "own": (0, nq)}
    plan = {
        "wide": wide, "narrow": narrow, "side": side, "groups": groups, "nq": nq, "nk": nk,
        "qkv_parts": qkv_parts, "out_parts": out_parts,
    }
    sum_gu, sum_down, sum_qkv, sum_out, output, grad_tokens, gains = run_main(
        plan,
        (length, qs, ks, norm_gain[None, :], ffn_gain[None, :]),
        (
            tokens, cotangent, jnp.concatenate([w_query, w_key, w_value], axis=1), w_out,
            w_gate, w_up, w_down, cosine, sine,
        ),
    )
    hidden_units = w_gate.shape[1]
    return (
        output,
        grad_tokens,
        gains[0],
        sum_qkv[:, :nq].astype(F32),
        sum_qkv[:, nq : nq + nk].astype(F32),
        sum_qkv[:, nq + nk :].astype(F32),
        gains[2, :HD] + gains[2, HD:TILE],
        gains[3, :HD] + gains[3, HD:TILE],
        sum_out.astype(F32),
        gains[1],
        sum_gu[:, :hidden_units].astype(F32),
        sum_gu[:, hidden_units:].astype(F32),
        sum_down.astype(F32),
    )


def solution(mesh):
    rows = P(("wide", "narrow"), None)
    columns, depth, copied = P(None, "narrow"), P("narrow", None), P()
    return jax.shard_map(
        functools.partial(on_device, mesh.shape["wide"], mesh.shape["narrow"]),
        mesh=mesh,
        in_specs=(
            rows, P("wide"), copied, columns, columns, columns, copied, copied, depth,
            copied, columns, columns, depth, rows,
        ),
        out_specs=(
            rows, rows, copied, columns, columns, columns, copied, copied, depth,
            copied, columns, columns, depth,
        ),
        check_vma=False,
    )
```

```python
import functools
import math

import jax
import jax.numpy as jnp
import numpy as np
from jax import lax
from jax.experimental import pallas as pl
from jax.experimental.pallas import tpu as pltpu
from jax.sharding import PartitionSpec as P

HD = 64
LEN = 1024
BLK = 256
TILE = 2 * HD

EPSILON = 1e-05
ROPE_BASE = 1000000.0
F32 = jnp.float32
BF16 = jnp.bfloat16
BACK_LIMIT = 60 * 1024 * 1024
JOIN_AT = 7


def rope_tables(length, width):
    half_width = width // 2
    exponents = -(2.0 * np.arange(half_width, dtype=np.float32)) / np.float32(width)
    frequency = np.float32(ROPE_BASE) ** exponents
    angles = np.arange(length, dtype=np.float32)[:, None] * frequency[None, :]
    return (np.cos(angles), np.sin(angles))


def contract(left_side, right_side, left_dim, right_dim):
    return lax.dot_general(
        left_side,
        right_side,
        (((left_dim,), (right_dim,)), ((), ())),
        preferred_element_type=F32,
    )


def lanes(shape):
    return lax.broadcasted_iota(jnp.int32, shape, 1)


def group_ones():
    rows = lax.broadcasted_iota(jnp.int32, (TILE, TILE), 0) // HD
    cols = lax.broadcasted_iota(jnp.int32, (TILE, TILE), 1) // HD
    return jnp.where(rows == cols, 1.0, 0.0).astype(BF16)


def group_sum(values_in, ones):
    high = values_in.astype(BF16)
    rest = (values_in - high.astype(F32)).astype(BF16)
    return contract(high, ones, 1, 0) + contract(rest, ones, 1, 0)


def swap_halves(values_in):
    half = HD // 2
    front = lax.rem(lanes(values_in.shape), HD) < half
    return jnp.where(
        front, pltpu.roll(values_in, TILE - half, 1), pltpu.roll(values_in, half, 1)
    )


class Ring:
    def __init__(self, count, place, target, turn, chunk, first, rows, own, source, out, land, sends, recvs):
        self.count, self.place, self.target, self.turn = count, place, target, turn
        self.chunk, self.first, self.rows = chunk, first, rows
        self.own, self.source, self.out, self.land = own, source, out, land
        self.sends, self.recvs = sends, recvs
        self.done = 0

    def index(self, steps):
        return lax.rem(self.place + self.turn * steps + 2 * self.count, self.count)

    def part(self, ref, steps):
        start = pl.multiple_of(self.index(steps) * self.chunk + self.first, 16)
        return ref.at[pl.ds(start, self.rows), :]

    def copy(self, step, source, target):
        return pltpu.make_async_remote_copy(
            src_ref=source,
            dst_ref=target,
            send_sem=self.sends.at[step],
            recv_sem=self.recvs.at[step],
            device_id={"wide": self.target},
            device_id_type=pl.DeviceIdType.MESH,
        )

    def copy_of(self, step):
        last = self.count - 1
        if step == 0:
            return self.copy(0, self.part(self.source, 0), self.land.at[0])
        if step < last:
            return self.copy(step, self.land.at[step - 1], self.land.at[step])
        steps = last - step + 1
        where = self.part(self.out, steps)
        return self.copy(step, self.land.at[last - 1] if step == last else where, where)

    def begin(self):
        self.copy_of(0).start()

    @property
    def left(self):
        return 2 * (self.count - 1) - self.done

    def tick(self, keep):
        step, last = self.done, self.count - 1
        self.done += 1
        if step < last:
            slot = self.land.at[step]
            self.copy(step, slot, slot).wait_recv()
            start = pl.multiple_of(self.index(-step - 1) * self.chunk + self.first, 16)

            @pl.loop(0, self.rows // 16)
            def _(r):
                at = pl.multiple_of(r * 16, 16)
                mine = self.own[pl.ds(pl.multiple_of(start + at, 16), 16), :].astype(F32)
                slot[pl.ds(at, 16), :] = (slot[pl.ds(at, 16), :].astype(F32) + mine).astype(BF16)

            if step == last - 1:
                kept = pltpu.make_async_copy(slot, self.part(self.out, 1), keep)
                kept.start()
                self.copy_of(last).start()
                kept.wait()
            else:
                self.copy_of(step + 1).start()
        else:
            where = self.part(self.out, last - step)
            self.copy(step, where, where).wait_recv()
            if self.left:
                self.copy_of(step + 1).start()

    def finish(self):
        for step in range(2 * (self.count - 1)):
            self.copy_of(step).wait_send()


def ring_rows(rows, count, less=0):
    chunk = -(-rows // (count * 16)) * 16
    forward = -(-chunk // 32) * 16
    if less < forward:
        forward -= less
    return chunk, forward, chunk - forward


def main_kernel(plan, *refs):
    count, narrow, side = plan["wide"], plan["narrow"], plan["side"]
    groups, own_rows = plan["groups"], plan["own"]
    taken = 0

    def take(number):
        nonlocal taken
        taken += number
        return refs[taken - number : taken]

    len_ref, qs_half, ks_half, ng_ref, fg_ref = take(5)
    tok_in, cin, wo_in, wg_in, wu_in, wd_in, cos_in, sin_in = take(8)
    qkv_in = take(plan["qkv_sources"])
    qkv_at = [0]
    for source in qkv_in:
        qkv_at.append(qkv_at[-1] + source.shape[1])
    qkv_at = [slice(*ends) for ends in zip(qkv_at, qkv_at[1:])]
    gu_out, gd_out, a1_out, a2_out, out_out, gt_out = take(6)
    mid_in, rows_in, w_all_in, wo_in_all = take(4)
    groups_in = [take(7) for _ in range(groups)]
    (gains_ref,) = take(1)
    x_l, x_r, c_l, c_r = take(4)
    gu_own, gd_own, rx1, rx2 = take(4)
    lands = take(plan["lands"])
    send_b, send_o, got_bl, got_ol, got_br, got_or = take(6)
    got_gn = got_br
    far_b, far_o, own_b, own_o, ownr_b, ownr_o = take(6)
    branch = x_r
    gain_mine, gain_in, qs_ref, ks_ref = take(4)
    load_sems, ring_sends, ring_recvs, keep_sem, sends, recvs, free_sem = take(7)

    w = lax.axis_index("wide")
    n = lax.axis_index("narrow")
    half = count // 2
    place_ring = lax.rem((1 - w % 2) * (count - w // 2) + (w % 2) * (w // 2 + 1), count)

    def at_place(p):
        far = lax.rem(p + count - 1, count) // half
        z = (1 - far) * (p - 1) + far * lax.rem(count - p, count)
        return 2 * z + 1 - far

    onward = at_place(lax.rem(place_ring + 1, count))
    behind = at_place(lax.rem(place_ring + count - 1, count))
    across = lax.rem(n + side, narrow)
    place = lax.rem(n, side)
    turns = range(1, side)

    place_at = [lax.rem(place + turn, side) for turn in range(side)]
    mates_at = [n - place + p for p in place_at]
    block_at = [pl.multiple_of(p * own_rows, BLK) for p in place_at]
    parts = own_rows // BLK
    part_at = [
        [pl.multiple_of(p * own_rows + b * BLK, BLK) for b in range(parts)] for p in place_at
    ]
    far_at = [
        [pl.multiple_of(b * side * BLK + p * BLK, BLK) for b in range(parts)] for p in place_at
    ]

    def mate(turn):
        return mates_at[turn]

    def flip(value, bit):
        return value + bit - 2 * bit * lax.rem(value // bit, 2)

    doubling = [("narrow", 2**e) for e in range(int(math.log2(narrow)))]
    doubling += [("wide", 2**e) for e in range(int(math.log2(count)))]
    partners = [{axis: flip(n if axis == "narrow" else w, bit)} for axis, bit in doubling]
    peers = [{"wide": onward}, {"wide": behind}, {"narrow": across}]
    peers += [{"narrow": mate(t)} for t in turns] + partners

    barrier = pltpu.get_barrier_semaphore()
    for peer in peers:
        pl.semaphore_signal(barrier, inc=1, device_id=peer, device_id_type=pl.DeviceIdType.MESH)
    pl.semaphore_wait(barrier, len(peers))

    numbers = {}
    unsent = []

    def remote(name, source, target, device):
        number = numbers.setdefault(name, len(numbers))
        return pltpu.make_async_remote_copy(
            src_ref=source,
            dst_ref=target,
            send_sem=sends.at[number],
            recv_sem=recvs.at[number],
            device_id=device,
            device_id_type=pl.DeviceIdType.MESH,
        )

    def send(name, source, target, device):
        copy = remote(name, source, target, device)
        copy.start()
        unsent.append((name, source, target, device))

    def sent(name):
        for entry in [e for e in unsent if e[0][: len(name)] == name]:
            remote(*entry).wait_send()
            unsent.remove(entry)

    def received(name, target, device):
        remote(name, target, target, device).wait_recv()

    def block(ref, turn):
        return ref.at[pl.ds(block_at[turn % side], own_rows), :]

    to_across = {"narrow": across}

    def to_mates(name, source, target):
        for t in turns:
            send(f"{name}{t}", source, target, {"narrow": mate(t)})

    def from_mates(name, ref):
        for t in turns:
            received(f"{name}{t}", block(ref, side - t), {"narrow": mate(t)})

    def part(ref, turn, b):
        return ref.at[pl.ds(part_at[turn % side][b], BLK), :]

    def far_part(ref, turn, b):
        return ref.at[pl.ds(far_at[turn % side][b], BLK), :]

    loading = {}

    def load(name, source, target):
        number = len(loading)
        loading[name] = [lambda: pltpu.make_async_copy(source, target, load_sems.at[number])]
        loading[name][0]().start()

    def need(*names):
        for name in names:
            if loading[name]:
                loading[name].pop()().wait()

    rings = []
    used = 0

    def add_ring(own, out, which):
        nonlocal used
        chunk, forward, backward = ring_rows(plan["rows"][which], count, plan["less"][which])
        pair = []
        for turn, target, first, size in ((1, onward, 0, forward), (-1, behind, forward, backward)):
            if size:
                pair.append(
                    Ring(
                        count, place_ring, target, turn, chunk, first, size, own, own, out,
                        lands[used], ring_sends.at[used], ring_recvs.at[used],
                    )
                )
                used += 1
        rings.append(pair)

    add_ring(gu_own, gu_out, 0)
    add_ring(gd_own, gd_out, 1)

    def begin(pair):
        for ring in pair:
            ring.begin()

    def tick(pair):
        for ring in pair:
            if ring.left:
                ring.tick(keep_sem)

    qs_ref[...] = jnp.concatenate([qs_half[...]] * 2, axis=1)
    ks_ref[...] = jnp.concatenate([ks_half[...]] * 2, axis=1)
    depth = x_l.shape[1]
    nq, nk = plan["nq"], plan["nk"]
    joined = groups == 1
    scale_many = 2 if joined else 1
    gq, gk = nq * scale_many, nk * scale_many
    heads = gk // HD
    rows_one = gd_own

    def causal_mask(shape, row_axis):
        rows_id = lax.rem(lax.broadcasted_iota(jnp.int32, shape, row_axis), BLK)
        return lax.broadcasted_iota(jnp.int32, shape, 1 - row_axis) <= rows_id

    def forward(wg, wu, wd, tok, wqkv, wo, cos_ref, sin_ref, mid, vaug_ref, *rest):
        saved = [rest[7 * g : 7 * g + 7] for g in range(groups)]
        for i, (source, cols) in enumerate(zip(qkv_in, qkv_at)):
            send(f"w1{i}", source, rx1.at[:, cols], to_across)
        send("w2", wo_in, rx2.at[0:nq, :], to_across)
        for b in range(parts - 1):
            send(f"cy{b}", cin.at[b * BLK : (b + 1) * BLK, :], far_part(c_r, 0, b), to_across)
        load("tok", tok_in, tok)
        for i, (source, cols) in enumerate(zip(qkv_in, qkv_at)):
            load(f"wqkv{i}", source, wqkv.at[:, cols])
        load("cos", cos_in, cos_ref)
        load("sin", sin_in, sin_ref)
        load("wo", wo_in, wo)
        load("c", cin, block(c_l, 0))
        load("wg", wg_in, wg)
        load("wu", wu_in, wu)
        load("wd", wd_in, wd)

        length = len_ref[n // side]
        ones = group_ones()
        lane = lanes((BLK, TILE))
        causal = causal_mask((2 * BLK, BLK), 0)

        need("tok")
        for b in range(parts):
            values = tok[b * BLK : (b + 1) * BLK, :].astype(F32)
            inv = lax.rsqrt(jnp.mean(values * values, axis=1, keepdims=True) + EPSILON)
            mine = part(rows_one, 0, b)
            mine[...] = (values * inv * ng_ref[...]).astype(BF16)
            to_mates(f"r{b}_", mine, mine)
        to_mates("cl", cin, block(c_l, 0))

        def norm_rope(raw, scale, cosine, sine):
            inv = lax.rsqrt(group_sum(raw * raw, ones) * (1.0 / HD) + EPSILON)
            scaled = raw * inv * scale
            return scaled * cosine + swap_halves(scaled) * sine

        def project(g, weight, at):
            q_ref, k_ref, v_ref, _, qraw_ref, kraw_ref, _ = saved[g]
            rows = pl.ds(pl.multiple_of(at, BLK), BLK)
            cosine, sine = cos_ref[rows, :], sin_ref[rows, :]
            real = (lax.broadcasted_iota(jnp.int32, (BLK, TILE), 0) + at) < length
            raw = contract(rows_one[rows, :], weight[...], 1, 0)
            qraw_ref[rows, :] = raw[:, :gq]
            kraw_ref[rows, :] = raw[:, gq : gq + gk]
            for t in range(heads):
                cols = slice(t * TILE, (t + 1) * TILE)
                turned = norm_rope(raw[:, cols], qs_ref[...], cosine, sine)
                q_ref[rows, cols] = (turned * (1.0 / math.sqrt(HD))).astype(BF16)
            for t in range(heads // 2):
                cols = slice(t * TILE, (t + 1) * TILE)
                k_raw = raw[:, gq + t * TILE : gq + (t + 1) * TILE]
                turned = norm_rope(k_raw, ks_ref[...], cosine, sine)
                k_ref[rows, cols] = jnp.where(real, turned, 0.0).astype(BF16)
                v_raw = raw[:, gq + gk + t * TILE : gq + gk + (t + 1) * TILE]
                v_pair = jnp.where(real, v_raw, 0.0)
                v_ref[rows, cols] = v_pair.astype(BF16)
                mark = jnp.where(real & (lane == HD), 1.0, 0.0)
                vaug_ref[2 * t, rows, :] = jnp.where(lane < HD, v_pair, mark).astype(BF16)
                vaug_ref[2 * t + 1, rows, :] = jnp.where(
                    lane < HD, pltpu.roll(v_pair, HD, 1), mark
                ).astype(BF16)

        def attend(g):
            q_ref, k_ref, _, att_ref, _, _, rinv_ref = saved[g]
            for h in range(heads):
                for i in range(LEN // BLK):
                    rows = slice(i * BLK, (i + 1) * BLK)
                    low = h * TILE
                    q_two = jnp.concatenate(
                        [q_ref[rows, low : low + HD], q_ref[rows, low + HD : low + TILE]], axis=0
                    )
                    total = jnp.zeros((2 * BLK, TILE), F32)
                    for j in range(i + 1):
                        keys = slice(j * BLK, (j + 1) * BLK)
                        scores = contract(q_two, k_ref[keys, h * HD : (h + 1) * HD], 1, 1)
                        weight = jnp.exp(scores)
                        if i == j:
                            weight = jnp.where(causal, weight, 0.0)
                        total += contract(weight.astype(BF16), vaug_ref[h, keys, :], 1, 0)
                    inv = 1.0 / total[:, HD : HD + 1]
                    mixed = total[:, :HD] * inv
                    wide_inv = jnp.broadcast_to(inv, (2 * BLK, HD))
                    att_ref[rows, low : low + HD] = mixed[:BLK].astype(BF16)
                    att_ref[rows, low + HD : low + TILE] = mixed[BLK:].astype(BF16)
                    rinv_ref[rows, low : low + HD] = wide_inv[:BLK]
                    rinv_ref[rows, low + HD : low + TILE] = wide_inv[BLK:]
            for i in range(7):
                load(f"save{g}_{i}", saved[g][i], groups_in[g][i])

        def arrive():
            for i, cols in enumerate(qkv_at):
                received(f"w1{i}", rx1.at[:, cols], to_across)

        need("cos", "sin", *[f"wqkv{i}" for i in range(len(qkv_in))])
        if joined:
            wj, woj = rest[7 * groups :]
            arrive()
            received("w2", rx2.at[0:nq, :], to_across)
            need("wo")
            to = 0
            for first, size in ((0, nq), (nq, nk), (nq + nk, nk)):
                for source in (wqkv, rx1):
                    wj[:, to : to + size] = source[:, first : first + size]
                    to += size
            woj[:nq, :] = wo[...]
            woj[nq:, :] = rx2[0:nq, :]
            rounds = [(0, wj)]
            outs = [(0, woj)]
        else:
            rounds = [(1, wqkv), (0, rx1)]
            outs = [(1, wo), (0, rx2.at[0:nq, :])]
        for number, (g, weight) in enumerate(rounds):
            if number:
                arrive()
            for t in range(side):
                for b in range(parts):
                    if t and not number:
                        received(f"r{b}_{t}", part(rows_one, side - t, b), {"narrow": mate(t)})
                    turn = side - t if t else 0
                    project(g, weight, part_at[turn][b])
            if not number:
                load("save_rows", rows_one.at[0:LEN, :], rows_in)
            attend(g)
        if joined:
            load("save_w", wj, w_all_in)
            load("save_wo", woj, wo_in_all)
        else:
            need("wo")
            received("w2", rx2.at[0:nq, :], to_across)
            half_width = wqkv.shape[1]
            load("save_w0", rx1, w_all_in.at[:, 0:half_width])
            load("save_w1", wqkv, w_all_in.at[:, half_width : 2 * half_width])
            load("save_wo0", rx2.at[0:nq, :], wo_in_all.at[0:nq, :])
            load("save_wo1", wo, wo_in_all.at[nq : 2 * nq, :])

        def mix(at):
            rows = pl.ds(pl.multiple_of(at, BLK), BLK)
            total = 0.0
            for g, weight in outs:
                total += contract(saved[g][3][rows, :], weight[...], 1, 0)
            return total

        for b in range(parts):
            here = slice(b * BLK, (b + 1) * BLK)
            for t in turns:
                send_b[t - 1, here, :] = mix(part_at[t][b]).astype(BF16)
                send(
                    f"mx{b}_{t}", send_b.at[t - 1, here, :], got_bl.at[t - 1, here, :],
                    {"narrow": mate(t)},
                )
        for b in range(parts):
            here = slice(b * BLK, (b + 1) * BLK)
            total = tok[here, :].astype(F32) + mix(part_at[0][b])
            for t in turns:
                received(f"mx{b}_{t}", got_bl.at[t - 1, here, :], {"narrow": mate(t)})
                total += got_bl[t - 1, here, :].astype(F32)
            mid[here, :] = total
            inv = lax.rsqrt(jnp.mean(total * total, axis=1, keepdims=True) + EPSILON)
            mine = part(x_l, 0, b)
            mine[...] = (total * inv * fg_ref[...]).astype(BF16)
            send(f"xy{b}", mine, far_part(x_r, 0, b), to_across)
            to_mates(f"xl{b}_", mine, mine)
        last = parts - 1
        send(f"cy{last}", cin.at[last * BLK : own_rows, :], far_part(c_r, 0, last), to_across)
        load("save_mid", mid, mid_in)
        sent("mx")
        sent("r")
        for name in [name for name in loading if name.startswith("save")]:
            need(name)

    own_tile = (own_rows, depth)
    scratch = [
        pltpu.VMEM(own_tile, BF16),
        pltpu.VMEM(rx1.shape, BF16),
        pltpu.VMEM(wo_in.shape, BF16),
        pltpu.VMEM((LEN, TILE), F32),
        pltpu.VMEM((LEN, TILE), F32),
        pltpu.VMEM(own_tile, F32),
        pltpu.VMEM((heads, LEN, TILE), BF16),
    ]
    scratch += [pltpu.VMEM(ref.shape, ref.dtype) for group in groups_in for ref in group]
    if joined:
        scratch += [pltpu.VMEM(w_all_in.shape, BF16), pltpu.VMEM(wo_in_all.shape, BF16)]
    forward_scratch = scratch

    units = wg_in.shape[1]
    cuts = [0, units // 2 // 128 * 128 + 128, units] if units % 128 == 0 else [0, units]

    def feed_forward(wg, wu, wd, hid, gg, gu):
        def rows_pass(x, c, at, back_to, out_to):
            rows = pl.ds(pl.multiple_of(at, BLK), BLK)
            for first, end in zip(cuts, cuts[1:]):
                cols = slice(first, end)
                gate = contract(x[rows, :], wg[:, cols], 1, 0)
                up = contract(x[rows, :], wu[:, cols], 1, 0)
                grad = contract(c[rows, :], wd[cols, :], 1, 1)
                share = 1.0 / (1.0 + jnp.exp(-gate))
                silu = gate * share
                hid[rows, cols] = (silu * up).astype(BF16)
                gg[rows, cols] = (grad * up * (share + silu * (1.0 - share))).astype(BF16)
                gu[rows, cols] = (grad * silu).astype(BF16)
            back = contract(gg[rows, :], wg[...], 1, 1)
            back += contract(gu[rows, :], wu[...], 1, 1)
            back_to[...] = back.astype(BF16)
            out_to[...] = contract(hid[rows, :], wd[...], 1, 0).astype(BF16)

        def near_pass(turn, back_to, out_to):
            @pl.loop(0, parts)
            def _(b):
                to = pl.ds(pl.multiple_of(b * BLK, BLK), BLK)
                at = block_at[turn] + b * BLK
                rows_pass(x_l, c_l, at, back_to.at[to, :], out_to.at[to, :])

        def weight_pass(x, c, rows, more, last, between=None):
            step = 384 if units % 384 == 0 else units
            for start in range(0, units, step):
                cols = slice(start, start + step)
                total = contract(hid[rows, cols], c[rows, :], 0, 0)
                if more:
                    total += gd_own[cols, :].astype(F32)
                gd_own[cols, :] = total.astype(BF16)
            if last:
                begin(rings[1])
            if between:
                between()
            for start in range(0, depth, BLK):
                to = slice(start, start + BLK)
                for first, grad in ((0, gg), (units, gu)):
                    total = contract(x[rows, to], grad[rows, :], 0, 0)
                    cols = slice(first, first + units)
                    if more:
                        total += gu_own[to, cols].astype(F32)
                    gu_own[to, cols] = total.astype(BF16)

        extra = gd_own.shape[0] - units
        if extra:
            gd_own[units:, :] = jnp.zeros((extra, depth), BF16)
        need("wg", "wu", "c", "wd")
        near_pass(0, own_b, own_o)
        for b in range(parts):
            for t in turns:
                received(f"xl{b}_{t}", part(x_l, side - t, b), {"narrow": mate(t)})
        from_mates("cl", c_l)
        for t in turns:
            near_pass(t, send_b.at[t - 1], send_o.at[t - 1])
            send(f"bl{t}", send_b.at[t - 1], got_bl.at[t - 1], {"narrow": mate(t)})
            send(f"ol{t}", send_o.at[t - 1], got_ol.at[t - 1], {"narrow": mate(t)})

        def pass_on(b):
            for name, ref in (("x", x_r), ("c", c_r)):
                mine = far_part(ref, 0, b)
                received(f"{name}y{b}", mine, to_across)
                to_mates(f"{name}r{b}_", mine, mine)

        def share_out(b):
            here = slice(b * BLK, (b + 1) * BLK)
            for name, mine, got in (("b", ownr_b, got_br), ("o", ownr_o, got_or)):
                for t in turns:
                    received(f"{name}r{b}_{t}", got.at[t - 1, here, :], {"narrow": mate(t)})

                @pl.loop(0, BLK // 32)
                def _(r):
                    rows = pl.ds(pl.multiple_of(b * BLK + r * 32, 32), 32)
                    total = mine[rows, :].astype(F32)
                    for t in turns:
                        total += got[t - 1, rows, :].astype(F32)
                    mine[rows, :] = total.astype(BF16)

                if name == "b":
                    send(f"by{b}", ownr_b.at[here, :], far_b.at[here, :], to_across)

        weight_pass(x_l, c_l, slice(0, LEN), False, False)
        sent("bl")
        sent("ol")
        for b in range(parts):
            here = slice(b * BLK, (b + 1) * BLK)
            if b:
                share_out(b - 1)
            pass_on(b)
            rows_pass(x_r, c_r, far_at[0][b], ownr_b.at[here, :], ownr_o.at[here, :])
            for t in turns:
                for name, ref in (("x", x_r), ("c", c_r)):
                    received(f"{name}r{b}_{t}", far_part(ref, side - t, b), {"narrow": mate(t)})
            for t in turns:
                back, out = send_b.at[t - 1, here, :], send_o.at[t - 1, here, :]
                rows_pass(x_r, c_r, far_at[t][b], back, out)
                send(f"br{b}_{t}", back, got_br.at[t - 1, here, :], {"narrow": mate(t)})
                send(f"or{b}_{t}", out, got_or.at[t - 1, here, :], {"narrow": mate(t)})
        weight_pass(x_r, c_r, slice(0, LEN), True, True, lambda: share_out(parts - 1))
        begin(rings[0])
        for name in ("w", "x", "c", "br", "or"):
            sent(name)

    def with_weights(wg, wu, wd):
        pl.run_scoped(functools.partial(forward, wg, wu, wd), *forward_scratch)
        pl.run_scoped(
            functools.partial(feed_forward, wg, wu, wd),
            *[pltpu.VMEM((LEN, units), BF16) for _ in range(3)],
        )

    pl.run_scoped(with_weights, *[pltpu.VMEM(ref.shape, BF16) for ref in (wg_in, wu_in, wd_in)])

    for t in turns:
        pl.semaphore_signal(
            free_sem, inc=1, device_id={"narrow": mate(t)}, device_id_type=pl.DeviceIdType.MESH
        )

    def attention(mid, gmid, tok, cos_ref, sin_ref, vaug_ref, aug_ref, dk_ref, dv_ref, *rest):
        px1, px2, own1, own2 = rest[:4]
        add_ring(own1, a1_out, 2)
        add_ring(own2, a2_out, 3)
        group = rest[4:12]
        spare = list(rest[12:])
        w_all = c_l if w_all_in.shape == x_r.shape else spare.pop(0)
        all_ref = x_l if w_all_in.shape == x_r.shape else spare.pop(0)
        first_rows = c_r
        q_ref, k_ref, v_ref, att_ref, qraw_ref, kraw_ref, rinv_ref, wo_ref = group

        load("mid_back", mid_in, mid)

        def load_group(g):
            sources = [*groups_in[g], wo_in_all.at[g * gq : (g + 1) * gq, :]]
            for i, (source, target) in enumerate(zip(sources, group)):
                load(f"group{g}_{i}", source, target)

        def need_group(g):
            need(*[f"group{g}_{i}" for i in range(8)])

        load_group(0)
        load("cos_back", cos_in, cos_ref)
        load("sin_back", sin_in, sin_ref)
        load("rows", rows_in, first_rows)
        load("tok_back", tok_in, tok)

        length = len_ref[n // side]
        ones = group_ones()
        lane = lanes((BLK, TILE))
        width = w_all.shape[1] // groups
        gains = {"q": jnp.zeros((1, TILE), F32), "k": jnp.zeros((1, TILE), F32)}
        causal = causal_mask((BLK, 2 * BLK), 1)

        def turn_back(grad, cosine, sine):
            return grad * cosine - swap_halves(grad) * sine

        def norm_back(raw, turned, scale):
            inv = lax.rsqrt(group_sum(raw * raw, ones) * (1.0 / HD) + EPSILON)
            scaled = turned * scale
            unit = raw * inv
            inner = group_sum(unit * scaled, ones) * (1.0 / HD)
            gain = jnp.sum(turned * unit, axis=0, keepdims=True)
            return inv * (scaled - unit * inner), gain

        def attention_pieces(g):
            base = g * width
            for start in range(0, LEN, BLK):
                rows = slice(start, start + BLK)
                grad = contract(branch[rows, :], wo_ref[...], 1, 1).astype(BF16).astype(F32)
                for t in range(heads):
                    cols = slice(t * TILE, (t + 1) * TILE)
                    part = (grad[:, cols] * rinv_ref[rows, cols]).astype(BF16).astype(F32)
                    inner = group_sum(part * att_ref[rows, cols].astype(F32), ones)
                    for which in range(2):
                        mine = part if which == 0 else pltpu.roll(part, HD, 1)
                        sums = pltpu.roll(inner, HD, 1) if which == 0 else inner
                        high = sums.astype(BF16).astype(F32)
                        tail = jnp.where(
                            lane == HD, -high, jnp.where(lane == HD + 1, high - sums, 0.0)
                        )
                        aug_ref[2 * t + which, rows, :] = jnp.where(lane < HD, mine, tail).astype(
                            BF16
                        )
                for t in range(heads // 2):
                    v_pair = v_ref[rows, t * TILE : (t + 1) * TILE].astype(F32)
                    mark = jnp.where(lane < HD + 2, 1.0, 0.0)
                    vaug_ref[2 * t, rows, :] = jnp.where(lane < HD, v_pair, mark).astype(BF16)
                    vaug_ref[2 * t + 1, rows, :] = jnp.where(
                        lane < HD, pltpu.roll(v_pair, HD, 1), mark
                    ).astype(BF16)
                dk_ref[:, rows, :] = jnp.zeros((heads, BLK, HD), F32)
                dv_ref[:, rows, :] = jnp.zeros((heads, BLK, TILE), F32)
                yield

            for h in range(heads):
                keys_turned = jnp.transpose(
                    k_ref[:, (h // 2) * TILE : (h // 2 + 1) * TILE].astype(F32)
                )[(h % 2) * HD : (h % 2 + 1) * HD].astype(BF16)
                for i in range(LEN // BLK):
                    rows = slice(i * BLK, (i + 1) * BLK)
                    low = h * TILE
                    q_two = jnp.concatenate(
                        [q_ref[rows, low : low + HD], q_ref[rows, low + HD : low + TILE]], axis=0
                    )
                    aug = jnp.concatenate(
                        [aug_ref[2 * h, rows, :], aug_ref[2 * h + 1, rows, :]], axis=0
                    )
                    dq = jnp.zeros((HD, 2 * BLK), F32)
                    for j in range(i + 1):
                        keys = slice(j * BLK, (j + 1) * BLK)
                        weight = jnp.exp(
                            contract(k_ref[keys, h * HD : (h + 1) * HD], q_two, 1, 1)
                        )
                        if i == j:
                            weight = jnp.where(causal, weight, 0.0)
                        slope = (weight * contract(vaug_ref[h, keys, :], aug, 1, 1)).astype(BF16)
                        dv_ref[h, keys, :] += contract(weight.astype(BF16), aug, 1, 0)
                        dk_ref[h, keys, :] += contract(slope, q_two, 1, 0)
                        dq += contract(keys_turned[:, keys], slope, 1, 0)
                    both = jnp.concatenate([dq[:, :BLK], dq[:, BLK:]], axis=0)
                    grad = jnp.transpose(both) * (1.0 / math.sqrt(HD))
                    turned = turn_back(grad, cos_ref[rows, :], sin_ref[rows, :])
                    out, gain = norm_back(qraw_ref[rows, low : low + TILE], turned, qs_ref[...])
                    all_ref[rows, base + low : base + low + TILE] = out.astype(BF16)
                    gains["q"] += gain
                    yield

            for start in range(0, LEN, BLK):
                rows = slice(start, start + BLK)
                real = (lax.broadcasted_iota(jnp.int32, (BLK, TILE), 0) + start) < length
                for t in range(heads // 2):
                    low = base + gq + t * TILE
                    grad = jnp.concatenate(
                        [dk_ref[2 * t, rows, :], dk_ref[2 * t + 1, rows, :]], axis=1
                    )
                    grad = jnp.where(real, grad, 0.0)
                    turned = turn_back(grad, cos_ref[rows, :], sin_ref[rows, :])
                    out, gain = norm_back(
                        kraw_ref[rows, t * TILE : (t + 1) * TILE], turned, ks_ref[...]
                    )
                    all_ref[rows, low : low + TILE] = out.astype(BF16)
                    gains["k"] += gain
                    values = jnp.where(
                        lane < HD,
                        dv_ref[2 * t, rows, :],
                        pltpu.roll(dv_ref[2 * t + 1, rows, :], HD, 1),
                    )
                    all_ref[rows, low + gk : low + gk + TILE] = jnp.where(
                        real, values, 0.0
                    ).astype(BF16)
                yield

        def out_grads(which, target):
            first, size = plan["out_parts"][which]
            target[:size, :] = contract(
                att_ref[:, first : first + size], branch[...], 0, 0
            ).astype(BF16)
            if target.shape[0] > size:
                target[size:, :] = jnp.zeros((target.shape[0] - size, target.shape[1]), BF16)

        def qkv_grads(which, target):
            for start in range(0, depth, BLK):
                rows = slice(start, start + BLK)
                for source, size, to in plan["qkv_parts"][which]:
                    target[rows, to : to + size] = contract(
                        first_rows[:, rows], all_ref[:, source : source + size], 0, 0
                    ).astype(BF16)
                yield

        def gain_copy(step):
            return (f"gain{step}", gain_mine.at[step], gain_in.at[step], partners[step])

        def compute():
            need("mid_back")
            for t in turns:
                received(f"bl{t}", got_bl.at[t - 1], {"narrow": mate(t)})
            tick(rings[1])
            gain_two = jnp.zeros((1, fg_ref.shape[1]), F32)
            own_branch, own_cot = block(branch, 0), block(c_l, 0)
            for start in range(0, own_rows, 64):
                rows = slice(start, start + 64)
                if start % BLK == 0:
                    received(f"by{start // BLK}", far_b.at[start : start + BLK, :], to_across)
                grad = own_b[rows, :].astype(F32) + far_b[rows, :].astype(F32)
                for t in turns:
                    grad += got_bl[t - 1, rows, :].astype(F32)
                values = mid[rows, :]
                inv = lax.rsqrt(jnp.mean(values * values, axis=1, keepdims=True) + EPSILON)
                unit = values * inv
                scaled = grad * fg_ref[...]
                inner = jnp.mean(unit * scaled, axis=1, keepdims=True)
                total = own_cot[rows, :].astype(F32) + inv * (scaled - unit * inner)
                gmid[rows, :] = total
                own_branch[rows, :] = total.astype(BF16)
                gain_two += jnp.sum(grad * unit, axis=0, keepdims=True)
            load("w_all", w_all_in, w_all)
            gain_mine[0, 1:2, :] = gain_two
            pl.semaphore_wait(free_sem, side - 1)
            to_mates("gb", own_branch, own_branch)
            need_group(0)
            need("cos_back", "sin_back")
            from_mates("gb", branch)
            yield
            out_grads("partner", px2)
            send("o2", px2, rx2, to_across)
            if groups == 1:
                out_grads("own", own2)
            yield
            yield from attention_pieces(0)
            need("rows")
            yield from qkv_grads("partner", px1)
            send("o1", px1, rx1, to_across)
            send("oy", ownr_o, far_o, to_across)
            if groups > 1:
                load_group(1)
            if groups > 1:
                need_group(1)
                out_grads("own", own2)
                yield
                yield from attention_pieces(1)
            yield from qkv_grads("own", own1)
            need("w_all", "tok_back")
            sent("by")
            for turn in [*turns, 0]:
                for start in range(0, own_rows, BLK):
                    at = pl.multiple_of(lax.rem(place + turn, side) * own_rows + start, BLK)
                    grad = contract(all_ref[pl.ds(at, BLK), :], w_all[...], 1, 1).astype(BF16)
                    if turn:
                        send_b[turn - 1, start : start + BLK, :] = grad
                    else:
                        own_b[start : start + BLK, :] = grad
                    yield
                if turn:
                    send(
                        f"gn{turn}", send_b.at[turn - 1], got_gn.at[turn - 1], {"narrow": mate(turn)}
                    )
            for t in turns:
                received(f"gn{t}", got_gn.at[t - 1], {"narrow": mate(t)})
            gain_one = jnp.zeros((1, ng_ref.shape[1]), F32)
            for start in range(0, own_rows, 64):
                rows = slice(start, start + 64)
                grad = own_b[rows, :].astype(F32)
                for t in turns:
                    grad += got_gn[t - 1, rows, :].astype(F32)
                values = tok[rows, :].astype(F32)
                inv = lax.rsqrt(jnp.mean(values * values, axis=1, keepdims=True) + EPSILON)
                unit = values * inv
                scaled = grad * ng_ref[...]
                inner = jnp.mean(unit * scaled, axis=1, keepdims=True)
                gmid[rows, :] += inv * (scaled - unit * inner)
                gain_one += jnp.sum(grad * unit, axis=0, keepdims=True)
            load("grad_tokens", gmid, gt_out)
            gain_mine[0, 0:1, :] = gain_one
            spare = jnp.zeros((1, gain_one.shape[1] - TILE), F32)
            gain_mine[0, 2:3, :] = jnp.concatenate([gains["q"], spare], axis=1)
            gain_mine[0, 3:4, :] = jnp.concatenate([gains["k"], spare], axis=1)
            gain_mine[0, 4:8, :] = jnp.zeros((4, gain_one.shape[1]), F32)
            send(*gain_copy(0))
            yield

        def finish_output():
            for t in turns:
                received(f"ol{t}", got_ol.at[t - 1], {"narrow": mate(t)})
            received("oy", far_o, to_across)
            for start in range(0, own_rows, 64):
                rows = slice(start, start + 64)
                total = mid[rows, :] + own_o[rows, :].astype(F32) + far_o[rows, :].astype(F32)
                for t in turns:
                    total += got_ol[t - 1, rows, :].astype(F32)
                own_o[rows, :] = total.astype(BF16)
            load("output", own_o, out_out)

        def join_partner():
            received("o2", rx2, to_across)
            received("o1", rx1, to_across)
            for mine, theirs in ((own1, rx1), (own2, rx2)):
                tall = mine.shape[0] // 16

                @pl.loop(0, tall)
                def _(r):
                    at = pl.ds(pl.multiple_of(r * 16, 16), 16)
                    mine[at, :] = (mine[at, :].astype(F32) + theirs[at, :].astype(F32)).astype(
                        BF16
                    )

        turn = 0
        order = [1, 0]
        for number, _ in enumerate(compute()):
            if number % 4 == 3:
                tick(rings[order[turn % 2]])
                turn += 1
        early = JOIN_AT * (count - 1) // 7
        while min(ring.done for ring in rings[order[turn % 2]]) < early:
            tick(rings[order[turn % 2]])
            turn += 1
        join_partner()
        for pair in rings[2:]:
            begin(pair)
        step = 0
        while any(ring.left for pair in rings for ring in pair):
            tick(rings[order[turn % 2]])
            turn += 1
            tick(rings[2])
            tick(rings[3])
            if step < len(doubling):
                name, mine, other, device = gain_copy(step)
                received(name, other, device)
                total = gain_mine[step] + gain_in[step]
                if step + 1 < len(doubling):
                    gain_mine[step + 1] = total
                    send(*gain_copy(step + 1))
                else:
                    gains_ref[...] = total
            if step == len(doubling):
                finish_output()
            step += 1
        for pair in rings:
            for ring in pair:
                ring.finish()
        sent("")
        need("output", "grad_tokens")

    scratch = [
        pltpu.VMEM((own_rows, depth), F32),
        pltpu.VMEM((own_rows, depth), F32),
        pltpu.VMEM((own_rows, depth), BF16),
        pltpu.VMEM((LEN, TILE), F32),
        pltpu.VMEM((LEN, TILE), F32),
        pltpu.VMEM((heads, LEN, TILE), BF16),
        pltpu.VMEM((2 * heads, LEN, TILE), BF16),
        pltpu.VMEM((heads, LEN, HD), F32),
        pltpu.VMEM((heads, LEN, TILE), F32),
    ]
    scratch += [pltpu.VMEM(ref.shape, BF16) for ref in (rx1, rx2, rx1, rx2)]
    scratch += [pltpu.VMEM(ref.shape, ref.dtype) for ref in groups_in[0]]
    scratch += [pltpu.VMEM((gq, depth), BF16)]
    if w_all_in.shape != x_r.shape:
        scratch += [pltpu.VMEM(w_all_in.shape, BF16), pltpu.VMEM((LEN, w_all_in.shape[1]), BF16)]
    pl.run_scoped(attention, *scratch)


VM = pl.BlockSpec(memory_space=pltpu.VMEM)
ANY = pl.BlockSpec(memory_space=pl.ANY)
SM = pl.BlockSpec(memory_space=pltpu.SMEM)


def run_main(plan, small, big):
    count, narrow, side = plan["wide"], plan["narrow"], plan["side"]
    shape = jax.ShapeDtypeStruct
    own, depth = big[0].shape
    units = big[3].shape[1]
    nq, nk, groups = plan["nq"], plan["nk"], plan["groups"]
    sizes = [(depth, 2 * units), (units, depth), (depth, nq + 2 * nk), (nq, depth)]
    _, ahead, back = ring_rows(units, count)
    less = [0, 0, (ahead - back) * depth // (2 * sizes[2][1]) // 16 * 16, 0]
    plan = dict(plan, rows=[s[0] for s in sizes], own=own, less=less)
    full, lands = [], []
    for (rows, cols), fewer in zip(sizes, less):
        chunk, forward, backward = ring_rows(rows, count, fewer)
        full.append((chunk * count, cols))
        lands += [pltpu.VMEM((count - 1, r, cols), BF16) for r in (forward, backward) if r]
    plan["lands"] = len(lands)
    steps = 2 * (count - 1)
    doubling = int(math.log2(narrow)) + int(math.log2(count))
    dma = pltpu.SemaphoreType.DMA
    rest = (own, depth)
    mates = (side - 1, own, depth)
    scratch = [pltpu.VMEM((LEN, depth), BF16) for _ in range(4)]
    scratch += [pltpu.VMEM(shape, BF16) for shape in full]
    scratch += lands
    scratch += [pltpu.VMEM(mates, BF16) for _ in range(6)]
    scratch += [pltpu.VMEM(rest, BF16) for _ in range(6)]
    scratch += [pltpu.VMEM((doubling, 8, depth), F32) for _ in range(2)]
    scratch += [pltpu.VMEM((1, TILE), F32) for _ in range(2)]
    parts = own // BLK
    moves = 6 + 4 * parts + (side - 1) * (7 * parts + 5) + doubling
    scratch += [
        dma((80,)),
        dma((len(lands), steps)),
        dma((len(lands), steps)),
        dma,
        dma((moves,)),
        dma((moves,)),
        pltpu.SemaphoreType.REGULAR,
    ]
    gq, gk = 2 * nq // groups, 2 * nk // groups
    kept = [shape(rest, F32), shape((LEN, depth), BF16)]
    kept += [shape((depth, 2 * (nq + 2 * nk)), BF16), shape((2 * nq, depth), BF16)]
    for _ in range(groups):
        kept += [shape((LEN, gq), BF16), shape((LEN, gk), BF16), shape((LEN, gk), BF16)]
        kept += [shape((LEN, gq), BF16), shape((LEN, gq), F32), shape((LEN, gk), F32)]
        kept += [shape((LEN, gq), F32)]
    results = pl.pallas_call(
        functools.partial(main_kernel, plan),
        out_shape=tuple(shape(s, BF16) for s in full)
        + (shape(rest, BF16), shape(rest, F32), *kept, shape((8, depth), F32)),
        in_specs=[SM] + [VM] * 4 + [ANY] * len(big),
        out_specs=[ANY] * (6 + len(kept)) + [VM],
        scratch_shapes=scratch,
        compiler_params=pltpu.CompilerParams(
            vmem_limit_bytes=BACK_LIMIT, collective_id=1, has_side_effects=True
        ),
        cost_estimate=pl.CostEstimate(
            flops=60 * 10**9, bytes_accessed=64 * 1024 * 1024, transcendentals=0
        ),
        name="main",
    )(*small, *big)
    return [r[: s[0]] for r, s in zip(results[:4], sizes)] + [*results[4:6], results[-1]]


def widen_kernel(nq, nk, units, gu, gd, a1, a2, rows, grads, gains, *outs):
    *outs, rows_out, grads_out = outs
    rows_out[...] = rows[...]
    grads_out[...] = grads[...]
    q_out, k_out, v_out, out_out, gate_out, up_out, down_out, ng_out, fg_out, qs_out, ks_out = outs
    q_out[...] = a1[:, :nq].astype(F32)
    k_out[...] = a1[:, nq : nq + nk].astype(F32)
    v_out[...] = a1[:, nq + nk :].astype(F32)
    out_out[...] = a2[...].astype(F32)
    gate_out[...] = gu[:, :units].astype(F32)
    up_out[...] = gu[:, units:].astype(F32)
    down_out[...] = gd[...].astype(F32)
    ng_out[...] = gains[0:1, :]
    fg_out[...] = gains[1:2, :]
    qs_out[...] = gains[2:3, :HD] + gains[2:3, HD:TILE]
    ks_out[...] = gains[3:4, :HD] + gains[3:4, HD:TILE]


def widen(nq, nk, gu, gd, a1, a2, rows, grads, gains):
    units, depth = gd.shape
    steps = next(n for n in (8, 4, 2, 1) if all(a.shape[0] % (16 * n) == 0 for a in (gu, gd, a1, a2)))

    def tall(rows, cols):
        return pl.BlockSpec((rows // steps, cols), lambda i: (i, 0))

    def whole(rows, cols):
        return pl.BlockSpec((rows, cols), lambda i: (0, 0))

    shapes = [(depth, nq), (depth, nk), (depth, nk), a2.shape, (depth, units), (depth, units)]
    shapes += [gd.shape]
    ends = [(1, depth), (1, depth), (1, HD), (1, HD)]
    kept = [jax.ShapeDtypeStruct(a.shape, a.dtype) for a in (rows, grads)]
    return pl.pallas_call(
        functools.partial(widen_kernel, nq, nk, units),
        grid=(steps,),
        out_shape=tuple(jax.ShapeDtypeStruct(s, F32) for s in shapes + ends) + tuple(kept),
        in_specs=[tall(*a.shape) for a in (gu, gd, a1, a2, rows, grads)] + [whole(*gains.shape)],
        out_specs=[tall(*s) for s in shapes]
        + [whole(*s) for s in ends]
        + [tall(*a.shape) for a in kept],
        compiler_params=pltpu.CompilerParams(vmem_limit_bytes=BACK_LIMIT),
        name="widen",
    )(gu, gd, a1, a2, rows, grads, gains)


def on_device(
    wide, narrow,
    tokens, lengths, norm_gain, w_query, w_key, w_value, query_scale, key_scale, w_out,
    ffn_gain, w_gate, w_up, w_down, cotangent,
):
    sequences = lengths.shape[0]
    side = narrow // sequences
    cosine, sine = rope_tables(LEN, HD)
    cosine = jnp.asarray(np.concatenate([cosine] * 4, axis=1))
    sine = jnp.asarray(np.concatenate([-sine, sine, -sine, sine], axis=1))

    nq, nk = w_query.shape[1], w_key.shape[1]
    sources = (w_query, w_key, w_value)
    if nk % TILE:
        groups = 1
        sources = (jnp.concatenate(sources, axis=1),)
        qkv_parts = {
            "own": [(0, nq, 0), (2 * nq, nk, nq), (2 * nq + 2 * nk, nk, nq + nk)],
            "partner": [
                (nq, nq, 0), (2 * nq + nk, nk, nq), (2 * nq + 3 * nk, nk, nq + nk)
            ],
        }
        out_parts = {"own": (0, nq), "partner": (nq, nq)}
    else:
        groups = 2
        qkv_parts = {
            "partner": [(0, nq + 2 * nk, 0)],
            "own": [(nq + 2 * nk, nq + 2 * nk, 0)],
        }
        out_parts = {"partner": (0, nq), "own": (0, nq)}
    plan = {
        "wide": wide, "narrow": narrow, "side": side, "groups": groups, "nq": nq, "nk": nk,
        "qkv_parts": qkv_parts, "out_parts": out_parts, "qkv_sources": len(sources),
    }
    sum_gu, sum_down, sum_qkv, sum_out, output, grad_tokens, gains = run_main(
        plan,
        (lengths, query_scale[None, :], key_scale[None, :], norm_gain[None, :], ffn_gain[None, :]),
        (tokens, cotangent, w_out, w_gate, w_up, w_down, cosine, sine, *sources),
    )
    query, key, value, out, gate, up, down, norm_g, ffn_g, query_s, key_s, output, grad_tokens = widen(
        nq, nk, sum_gu, sum_down, sum_qkv, sum_out, output, grad_tokens, gains
    )
    return (
        output, grad_tokens, norm_g[0], query, key, value, query_s[0], key_s[0], out, ffn_g[0],
        gate, up, down,
    )


def solution(mesh):
    rows = P(("wide", "narrow"), None)
    columns, depth, copied = P(None, "narrow"), P("narrow", None), P()
    return jax.shard_map(
        functools.partial(on_device, mesh.shape["wide"], mesh.shape["narrow"]),
        mesh=mesh,
        in_specs=(
            rows, P("wide"), copied, columns, columns, columns, copied, copied, depth,
            copied, columns, columns, depth, rows,
        ),
        out_specs=(
            rows, rows, copied, columns, columns, columns, copied, copied, depth,
            copied, columns, columns, depth,
        ),
        check_vma=False,
    )
```

```python
import functools
import math

import jax
import jax.numpy as jnp
import numpy as np
from jax import lax
from jax.experimental import pallas as pl
from jax.experimental.pallas import tpu as pltpu
from jax.sharding import PartitionSpec as P

HD = 64
LEN = 1024
BLK = 256
TILE = 2 * HD

EPSILON = 1e-05
ROPE_BASE = 1000000.0
F32 = jnp.float32
BF16 = jnp.bfloat16
BACK_LIMIT = 60 * 1024 * 1024
JOIN_AT = 6


def rope_tables(length, width):
    half_width = width // 2
    exponents = -(2.0 * np.arange(half_width, dtype=np.float32)) / np.float32(width)
    frequency = np.float32(ROPE_BASE) ** exponents
    angles = np.arange(length, dtype=np.float32)[:, None] * frequency[None, :]
    return (np.cos(angles), np.sin(angles))


def contract(left_side, right_side, left_dim, right_dim):
    return lax.dot_general(
        left_side,
        right_side,
        (((left_dim,), (right_dim,)), ((), ())),
        preferred_element_type=F32,
    )


def lanes(shape):
    return lax.broadcasted_iota(jnp.int32, shape, 1)


def group_ones():
    rows = lax.broadcasted_iota(jnp.int32, (TILE, TILE), 0) // HD
    cols = lax.broadcasted_iota(jnp.int32, (TILE, TILE), 1) // HD
    return jnp.where(rows == cols, 1.0, 0.0).astype(BF16)


def group_sum(values_in, ones):
    high = values_in.astype(BF16)
    rest = (values_in - high.astype(F32)).astype(BF16)
    return contract(high, ones, 1, 0) + contract(rest, ones, 1, 0)


def swap_halves(values_in):
    half = HD // 2
    front = lax.rem(lanes(values_in.shape), HD) < half
    return jnp.where(
        front, pltpu.roll(values_in, TILE - half, 1), pltpu.roll(values_in, half, 1)
    )


class Ring:
    def __init__(self, count, place, target, turn, chunk, first, rows, own, source, out, land, sends, recvs):
        self.count, self.place, self.target, self.turn = count, place, target, turn
        self.chunk, self.first, self.rows = chunk, first, rows
        self.own, self.source, self.out, self.land = own, source, out, land
        self.sends, self.recvs = sends, recvs
        self.done = 0

    def index(self, steps):
        return lax.rem(self.place + self.turn * steps + 2 * self.count, self.count)

    def part(self, ref, steps):
        start = pl.multiple_of(self.index(steps) * self.chunk + self.first, 16)
        return ref.at[pl.ds(start, self.rows), :]

    def copy(self, step, source, target):
        return pltpu.make_async_remote_copy(
            src_ref=source,
            dst_ref=target,
            send_sem=self.sends.at[step],
            recv_sem=self.recvs.at[step],
            device_id={"wide": self.target},
            device_id_type=pl.DeviceIdType.MESH,
        )

    def copy_of(self, step):
        last = self.count - 1
        if step == 0:
            return self.copy(0, self.part(self.source, 0), self.land.at[0])
        if step < last:
            return self.copy(step, self.land.at[step - 1], self.land.at[step])
        steps = last - step + 1
        where = self.part(self.out, steps)
        return self.copy(step, self.land.at[last - 1] if step == last else where, where)

    def begin(self):
        self.copy_of(0).start()

    @property
    def left(self):
        return 2 * (self.count - 1) - self.done

    def tick(self, keep):
        step, last = self.done, self.count - 1
        self.done += 1
        if step < last:
            slot = self.land.at[step]
            self.copy(step, slot, slot).wait_recv()
            start = pl.multiple_of(self.index(-step - 1) * self.chunk + self.first, 16)

            @pl.loop(0, self.rows // 16)
            def _(r):
                at = pl.multiple_of(r * 16, 16)
                mine = self.own[pl.ds(pl.multiple_of(start + at, 16), 16), :].astype(F32)
                slot[pl.ds(at, 16), :] = (slot[pl.ds(at, 16), :].astype(F32) + mine).astype(BF16)

            if step == last - 1:
                kept = pltpu.make_async_copy(slot, self.part(self.out, 1), keep)
                kept.start()
                self.copy_of(last).start()
                kept.wait()
            else:
                self.copy_of(step + 1).start()
        else:
            where = self.part(self.out, last - step)
            self.copy(step, where, where).wait_recv()
            if self.left:
                self.copy_of(step + 1).start()

    def finish(self):
        for step in range(2 * (self.count - 1)):
            self.copy_of(step).wait_send()


def ring_rows(rows, count, less=0):
    chunk = -(-rows // (count * 16)) * 16
    forward = -(-chunk // 32) * 16
    if less < forward:
        forward -= less
    return chunk, forward, chunk - forward


def main_kernel(plan, *refs):
    count, narrow, side = plan["wide"], plan["narrow"], plan["side"]
    groups, own_rows = plan["groups"], plan["own"]
    taken = 0

    def take(number):
        nonlocal taken
        taken += number
        return refs[taken - number : taken]

    len_ref, qs_half, ks_half, ng_ref, fg_ref = take(5)
    tok_in, cin, wo_in, wg_in, wu_in, wd_in, cos_in, sin_in = take(8)
    qkv_in = take(plan["qkv_sources"])
    qkv_at = [0]
    for source in qkv_in:
        qkv_at.append(qkv_at[-1] + source.shape[1])
    qkv_at = [slice(*ends) for ends in zip(qkv_at, qkv_at[1:])]
    gu_out, gd_out, a1_out, a2_out, out_out, gt_out = take(6)
    mid_in, rows_in, w_all_in, wo_in_all = take(4)
    groups_in = [take(7) for _ in range(groups)]
    (gains_ref,) = take(1)
    x_l, x_r, c_l, c_r = take(4)
    gu_own, gd_own, rx1, rx2 = take(4)
    lands = take(plan["lands"])
    send_b, send_o, got_bl, got_ol, got_br, got_or = take(6)
    got_gn = got_br
    far_b, far_o, own_b, own_o, ownr_b, ownr_o = take(6)
    branch = x_r
    gain_mine, gain_in, qs_ref, ks_ref = take(4)
    load_sems, ring_sends, ring_recvs, keep_sem, sends, recvs, free_sem = take(7)

    w = lax.axis_index("wide")
    n = lax.axis_index("narrow")
    half = count // 2
    place_ring = lax.rem((1 - w % 2) * (count - w // 2) + (w % 2) * (w // 2 + 1), count)

    def at_place(p):
        far = lax.rem(p + count - 1, count) // half
        z = (1 - far) * (p - 1) + far * lax.rem(count - p, count)
        return 2 * z + 1 - far

    onward = at_place(lax.rem(place_ring + 1, count))
    behind = at_place(lax.rem(place_ring + count - 1, count))
    across = lax.rem(n + side, narrow)
    place = lax.rem(n, side)
    turns = range(1, side)

    place_at = [lax.rem(place + turn, side) for turn in range(side)]
    mates_at = [n - place + p for p in place_at]
    block_at = [pl.multiple_of(p * own_rows, BLK) for p in place_at]
    parts = own_rows // BLK
    part_at = [
        [pl.multiple_of(p * own_rows + b * BLK, BLK) for b in range(parts)] for p in place_at
    ]
    far_at = [
        [pl.multiple_of(b * side * BLK + p * BLK, BLK) for b in range(parts)] for p in place_at
    ]

    def mate(turn):
        return mates_at[turn]

    def flip(value, bit):
        return value + bit - 2 * bit * lax.rem(value // bit, 2)

    doubling = [("narrow", 2**e) for e in range(int(math.log2(narrow)))]
    doubling += [("wide", 2**e) for e in range(int(math.log2(count)))]
    partners = [{axis: flip(n if axis == "narrow" else w, bit)} for axis, bit in doubling]
    peers = [{"wide": onward}, {"wide": behind}, {"narrow": across}]
    peers += [{"narrow": mate(t)} for t in turns] + partners

    barrier = pltpu.get_barrier_semaphore()
    for peer in peers:
        pl.semaphore_signal(barrier, inc=1, device_id=peer, device_id_type=pl.DeviceIdType.MESH)
    pl.semaphore_wait(barrier, len(peers))

    numbers = {}
    unsent = []

    def remote(name, source, target, device):
        number = numbers.setdefault(name, len(numbers))
        return pltpu.make_async_remote_copy(
            src_ref=source,
            dst_ref=target,
            send_sem=sends.at[number],
            recv_sem=recvs.at[number],
            device_id=device,
            device_id_type=pl.DeviceIdType.MESH,
        )

    def send(name, source, target, device):
        copy = remote(name, source, target, device)
        copy.start()
        unsent.append((name, source, target, device))

    def sent(name):
        for entry in [e for e in unsent if e[0][: len(name)] == name]:
            remote(*entry).wait_send()
            unsent.remove(entry)

    def received(name, target, device):
        remote(name, target, target, device).wait_recv()

    def block(ref, turn):
        return ref.at[pl.ds(block_at[turn % side], own_rows), :]

    to_across = {"narrow": across}

    def to_mates(name, source, target):
        for t in turns:
            send(f"{name}{t}", source, target, {"narrow": mate(t)})

    def from_mates(name, ref):
        for t in turns:
            received(f"{name}{t}", block(ref, side - t), {"narrow": mate(t)})

    def part(ref, turn, b):
        return ref.at[pl.ds(part_at[turn % side][b], BLK), :]

    def far_part(ref, turn, b):
        return ref.at[pl.ds(far_at[turn % side][b], BLK), :]

    loading = {}

    def load(name, source, target):
        number = len(loading)
        loading[name] = [lambda: pltpu.make_async_copy(source, target, load_sems.at[number])]
        loading[name][0]().start()

    def need(*names):
        for name in names:
            if loading[name]:
                loading[name].pop()().wait()

    rings = []
    used = 0

    def add_ring(own, out, which):
        nonlocal used
        chunk, forward, backward = ring_rows(plan["rows"][which], count, plan["less"][which])
        pair = []
        for turn, target, first, size in ((1, onward, 0, forward), (-1, behind, forward, backward)):
            if size:
                pair.append(
                    Ring(
                        count, place_ring, target, turn, chunk, first, size, own, own, out,
                        lands[used], ring_sends.at[used], ring_recvs.at[used],
                    )
                )
                used += 1
        rings.append(pair)

    add_ring(gu_own, gu_out, 0)
    add_ring(gd_own, gd_out, 1)

    def begin(pair):
        for ring in pair:
            ring.begin()

    def tick(pair):
        for ring in pair:
            if ring.left:
                ring.tick(keep_sem)

    qs_ref[...] = jnp.concatenate([qs_half[...]] * 2, axis=1)
    ks_ref[...] = jnp.concatenate([ks_half[...]] * 2, axis=1)
    depth = x_l.shape[1]
    nq, nk = plan["nq"], plan["nk"]
    joined = groups == 1
    scale_many = 2 if joined else 1
    gq, gk = nq * scale_many, nk * scale_many
    heads = gk // HD
    rows_one = gd_own

    def causal_mask(shape, row_axis):
        rows_id = lax.rem(lax.broadcasted_iota(jnp.int32, shape, row_axis), BLK)
        return lax.broadcasted_iota(jnp.int32, shape, 1 - row_axis) <= rows_id

    def forward(wg, wu, wd, tok, wqkv, wo, cos_ref, sin_ref, mid, vaug_ref, *rest):
        saved = [rest[7 * g : 7 * g + 7] for g in range(groups)]
        for i, (source, cols) in enumerate(zip(qkv_in, qkv_at)):
            send(f"w1{i}", source, rx1.at[:, cols], to_across)
        send("w2", wo_in, rx2.at[0:nq, :], to_across)
        for b in range(parts - 1):
            send(f"cy{b}", cin.at[b * BLK : (b + 1) * BLK, :], far_part(c_r, 0, b), to_across)
        load("tok", tok_in, tok)
        for i, (source, cols) in enumerate(zip(qkv_in, qkv_at)):
            load(f"wqkv{i}", source, wqkv.at[:, cols])
        load("cos", cos_in, cos_ref)
        load("sin", sin_in, sin_ref)
        load("wo", wo_in, wo)
        load("c", cin, block(c_l, 0))
        load("wg", wg_in, wg)
        load("wu", wu_in, wu)
        load("wd", wd_in, wd)

        length = len_ref[n // side]
        ones = group_ones()
        lane = lanes((BLK, TILE))
        causal = causal_mask((2 * BLK, BLK), 0)

        need("tok")
        for b in range(parts):
            values = tok[b * BLK : (b + 1) * BLK, :].astype(F32)
            inv = lax.rsqrt(jnp.mean(values * values, axis=1, keepdims=True) + EPSILON)
            mine = part(rows_one, 0, b)
            mine[...] = (values * inv * ng_ref[...]).astype(BF16)
            to_mates(f"r{b}_", mine, mine)
        to_mates("cl", cin, block(c_l, 0))

        def norm_rope(raw, scale, cosine, sine):
            inv = lax.rsqrt(group_sum(raw * raw, ones) * (1.0 / HD) + EPSILON)
            scaled = raw * inv * scale
            return scaled * cosine + swap_halves(scaled) * sine

        def project(g, weight, at):
            q_ref, k_ref, v_ref, _, qraw_ref, kraw_ref, _ = saved[g]
            rows = pl.ds(pl.multiple_of(at, BLK), BLK)
            cosine, sine = cos_ref[rows, :], sin_ref[rows, :]
            real = (lax.broadcasted_iota(jnp.int32, (BLK, TILE), 0) + at) < length
            raw = contract(rows_one[rows, :], weight[...], 1, 0)
            qraw_ref[rows, :] = raw[:, :gq]
            kraw_ref[rows, :] = raw[:, gq : gq + gk]
            for t in range(heads):
                cols = slice(t * TILE, (t + 1) * TILE)
                turned = norm_rope(raw[:, cols], qs_ref[...], cosine, sine)
                q_ref[rows, cols] = (turned * (1.0 / math.sqrt(HD))).astype(BF16)
            for t in range(heads // 2):
                cols = slice(t * TILE, (t + 1) * TILE)
                k_raw = raw[:, gq + t * TILE : gq + (t + 1) * TILE]
                turned = norm_rope(k_raw, ks_ref[...], cosine, sine)
                k_ref[rows, cols] = jnp.where(real, turned, 0.0).astype(BF16)
                v_raw = raw[:, gq + gk + t * TILE : gq + gk + (t + 1) * TILE]
                v_pair = jnp.where(real, v_raw, 0.0)
                v_ref[rows, cols] = v_pair.astype(BF16)
                mark = jnp.where(real & (lane == HD), 1.0, 0.0)
                vaug_ref[2 * t, rows, :] = jnp.where(lane < HD, v_pair, mark).astype(BF16)
                vaug_ref[2 * t + 1, rows, :] = jnp.where(
                    lane < HD, pltpu.roll(v_pair, HD, 1), mark
                ).astype(BF16)

        def attend(g):
            q_ref, k_ref, _, att_ref, _, _, rinv_ref = saved[g]
            for h in range(heads):
                for i in range(LEN // BLK):
                    rows = slice(i * BLK, (i + 1) * BLK)
                    low = h * TILE
                    q_two = jnp.concatenate(
                        [q_ref[rows, low : low + HD], q_ref[rows, low + HD : low + TILE]], axis=0
                    )
                    total = jnp.zeros((2 * BLK, TILE), F32)
                    for j in range(i + 1):
                        keys = slice(j * BLK, (j + 1) * BLK)
                        scores = contract(q_two, k_ref[keys, h * HD : (h + 1) * HD], 1, 1)
                        weight = jnp.exp(scores)
                        if i == j:
                            weight = jnp.where(causal, weight, 0.0)
                        total += contract(weight.astype(BF16), vaug_ref[h, keys, :], 1, 0)
                    inv = 1.0 / total[:, HD : HD + 1]
                    mixed = total[:, :HD] * inv
                    wide_inv = jnp.broadcast_to(inv, (2 * BLK, HD))
                    att_ref[rows, low : low + HD] = mixed[:BLK].astype(BF16)
                    att_ref[rows, low + HD : low + TILE] = mixed[BLK:].astype(BF16)
                    rinv_ref[rows, low : low + HD] = wide_inv[:BLK]
                    rinv_ref[rows, low + HD : low + TILE] = wide_inv[BLK:]
            for i in range(7):
                load(f"save{g}_{i}", saved[g][i], groups_in[g][i])

        def arrive():
            for i, cols in enumerate(qkv_at):
                received(f"w1{i}", rx1.at[:, cols], to_across)

        need("cos", "sin", *[f"wqkv{i}" for i in range(len(qkv_in))])
        if joined:
            wj, woj = rest[7 * groups :]
            arrive()
            received("w2", rx2.at[0:nq, :], to_across)
            need("wo")
            to = 0
            for first, size in ((0, nq), (nq, nk), (nq + nk, nk)):
                for source in (wqkv, rx1):
                    wj[:, to : to + size] = source[:, first : first + size]
                    to += size
            woj[:nq, :] = wo[...]
            woj[nq:, :] = rx2[0:nq, :]
            rounds = [(0, wj)]
            outs = [(0, woj)]
        else:
            rounds = [(1, wqkv), (0, rx1)]
            outs = [(1, wo), (0, rx2.at[0:nq, :])]
        for number, (g, weight) in enumerate(rounds):
            if number:
                arrive()
            for t in range(side):
                for b in range(parts):
                    if t and not number:
                        received(f"r{b}_{t}", part(rows_one, side - t, b), {"narrow": mate(t)})
                    turn = side - t if t else 0
                    project(g, weight, part_at[turn][b])
            if not number:
                load("save_rows", rows_one.at[0:LEN, :], rows_in)
            attend(g)
        if joined:
            load("save_w", wj, w_all_in)
            load("save_wo", woj, wo_in_all)
        else:
            need("wo")
            received("w2", rx2.at[0:nq, :], to_across)
            half_width = wqkv.shape[1]
            load("save_w0", rx1, w_all_in.at[:, 0:half_width])
            load("save_w1", wqkv, w_all_in.at[:, half_width : 2 * half_width])
            load("save_wo0", rx2.at[0:nq, :], wo_in_all.at[0:nq, :])
            load("save_wo1", wo, wo_in_all.at[nq : 2 * nq, :])

        def mix(at):
            rows = pl.ds(pl.multiple_of(at, BLK), BLK)
            total = 0.0
            for g, weight in outs:
                total += contract(saved[g][3][rows, :], weight[...], 1, 0)
            return total

        for b in range(parts):
            here = slice(b * BLK, (b + 1) * BLK)
            for t in turns:
                send_b[t - 1, here, :] = mix(part_at[t][b]).astype(BF16)
                send(
                    f"mx{b}_{t}", send_b.at[t - 1, here, :], got_bl.at[t - 1, here, :],
                    {"narrow": mate(t)},
                )
        for b in range(parts):
            here = slice(b * BLK, (b + 1) * BLK)
            total = tok[here, :].astype(F32) + mix(part_at[0][b])
            for t in turns:
                received(f"mx{b}_{t}", got_bl.at[t - 1, here, :], {"narrow": mate(t)})
                total += got_bl[t - 1, here, :].astype(F32)
            mid[here, :] = total
            inv = lax.rsqrt(jnp.mean(total * total, axis=1, keepdims=True) + EPSILON)
            mine = part(x_l, 0, b)
            mine[...] = (total * inv * fg_ref[...]).astype(BF16)
            send(f"xy{b}", mine, far_part(x_r, 0, b), to_across)
            to_mates(f"xl{b}_", mine, mine)
        last = parts - 1
        send(f"cy{last}", cin.at[last * BLK : own_rows, :], far_part(c_r, 0, last), to_across)
        load("save_mid", mid, mid_in)
        sent("mx")
        sent("r")
        for name in [name for name in loading if name.startswith("save")]:
            need(name)

    own_tile = (own_rows, depth)
    scratch = [
        pltpu.VMEM(own_tile, BF16),
        pltpu.VMEM(rx1.shape, BF16),
        pltpu.VMEM(wo_in.shape, BF16),
        pltpu.VMEM((LEN, TILE), F32),
        pltpu.VMEM((LEN, TILE), F32),
        pltpu.VMEM(own_tile, F32),
        pltpu.VMEM((heads, LEN, TILE), BF16),
    ]
    scratch += [pltpu.VMEM(ref.shape, ref.dtype) for group in groups_in for ref in group]
    if joined:
        scratch += [pltpu.VMEM(w_all_in.shape, BF16), pltpu.VMEM(wo_in_all.shape, BF16)]
    forward_scratch = scratch

    units = wg_in.shape[1]
    cuts = [0, units // 2 // 128 * 128 + 128, units] if units % 128 == 0 else [0, units]

    def feed_forward(wg, wu, wd, hid, gg, gu):
        def front_pass(x, c, at):
            rows = pl.ds(pl.multiple_of(at, BLK), BLK)
            for first, end in zip(cuts, cuts[1:]):
                cols = slice(first, end)
                gate = contract(x[rows, :], wg[:, cols], 1, 0)
                up = contract(x[rows, :], wu[:, cols], 1, 0)
                grad = contract(c[rows, :], wd[cols, :], 1, 1)
                share = 1.0 / (1.0 + jnp.exp(-gate))
                silu = gate * share
                hid[rows, cols] = (silu * up).astype(BF16)
                gg[rows, cols] = (grad * up * (share + silu * (1.0 - share))).astype(BF16)
                gu[rows, cols] = (grad * silu).astype(BF16)

        def back_pass(at, back_to, out_to):
            rows = pl.ds(pl.multiple_of(at, BLK), BLK)
            back = contract(gg[rows, :], wg[...], 1, 1)
            back += contract(gu[rows, :], wu[...], 1, 1)
            back_to[...] = back.astype(BF16)
            out_to[...] = contract(hid[rows, :], wd[...], 1, 0).astype(BF16)

        def near_pass(turn, back_to, out_to):
            @pl.loop(0, parts)
            def _(b):
                to = pl.ds(pl.multiple_of(b * BLK, BLK), BLK)
                at = block_at[turn] + b * BLK
                front_pass(x_l, c_l, at)
                back_pass(at, back_to.at[to, :], out_to.at[to, :])

        def down_pass(c, more):
            step = 384 if units % 384 == 0 else units
            for start in range(0, units, step):
                cols = slice(start, start + step)
                total = contract(hid[:, cols], c[...], 0, 0)
                if more:
                    total += gd_own[cols, :].astype(F32)
                gd_own[cols, :] = total.astype(BF16)

        def gate_up_pass(x, number, more):
            to = pl.ds(pl.multiple_of(number * BLK, BLK), BLK)
            for first, grad in ((0, gg), (units, gu)):
                total = contract(x[:, to], grad[...], 0, 0)
                cols = slice(first, first + units)
                if more:
                    total += gu_own[to, cols].astype(F32)
                gu_own[to, cols] = total.astype(BF16)

        extra = gd_own.shape[0] - units
        if extra:
            gd_own[units:, :] = jnp.zeros((extra, depth), BF16)
        need("wg", "wu", "c", "wd")
        near_pass(0, own_b, own_o)
        for b in range(parts):
            for t in turns:
                received(f"xl{b}_{t}", part(x_l, side - t, b), {"narrow": mate(t)})
        from_mates("cl", c_l)
        for t in turns:
            near_pass(t, send_b.at[t - 1], send_o.at[t - 1])
            send(f"bl{t}", send_b.at[t - 1], got_bl.at[t - 1], {"narrow": mate(t)})
            send(f"ol{t}", send_o.at[t - 1], got_ol.at[t - 1], {"narrow": mate(t)})

        def pass_on(b):
            for name, ref in (("x", x_r), ("c", c_r)):
                mine = far_part(ref, 0, b)
                received(f"{name}y{b}", mine, to_across)
                to_mates(f"{name}r{b}_", mine, mine)

        def share_out(b):
            here = slice(b * BLK, (b + 1) * BLK)
            for name, mine, got in (("b", ownr_b, got_br), ("o", ownr_o, got_or)):
                for t in turns:
                    received(f"{name}r{b}_{t}", got.at[t - 1, here, :], {"narrow": mate(t)})

                @pl.loop(0, BLK // 32)
                def _(r):
                    rows = pl.ds(pl.multiple_of(b * BLK + r * 32, 32), 32)
                    total = mine[rows, :].astype(F32)
                    for t in turns:
                        total += got[t - 1, rows, :].astype(F32)
                    mine[rows, :] = total.astype(BF16)

                if name == "b":
                    send(f"by{b}", ownr_b.at[here, :], far_b.at[here, :], to_across)

        down_pass(c_l, False)
        for number in range(depth // BLK):
            gate_up_pass(x_l, number, False)
        sent("bl")
        sent("ol")
        for b in range(parts):
            here = slice(b * BLK, (b + 1) * BLK)
            if b:
                share_out(b - 1)
            pass_on(b)
            front_pass(x_r, c_r, far_at[0][b])
            for t in turns:
                for name, ref in (("x", x_r), ("c", c_r)):
                    received(f"{name}r{b}_{t}", far_part(ref, side - t, b), {"narrow": mate(t)})
            for t in turns:
                front_pass(x_r, c_r, far_at[t][b])
            if b == parts - 1:
                chunk = ring_rows(plan["rows"][0], count)[0]
                blocks = depth // BLK
                first = (place_ring * chunk) // BLK if BLK % chunk == 0 else 0
                for number in range(blocks):
                    gate_up_pass(x_r, lax.rem(first + number, blocks), True)
                    if number == (0 if BLK % chunk == 0 else blocks - 1):
                        begin(rings[0])
                        down_pass(c_r, True)
                        begin(rings[1])
            for t in turns:
                back, out = send_b.at[t - 1, here, :], send_o.at[t - 1, here, :]
                back_pass(far_at[t][b], back, out)
                send(f"br{b}_{t}", back, got_br.at[t - 1, here, :], {"narrow": mate(t)})
                send(f"or{b}_{t}", out, got_or.at[t - 1, here, :], {"narrow": mate(t)})
            if b == parts - 1:
                tick(rings[0])
            back_pass(far_at[0][b], ownr_b.at[here, :], ownr_o.at[here, :])
        share_out(parts - 1)
        tick(rings[1])
        for name in ("w", "x", "c", "br", "or"):
            sent(name)

    def with_weights(wg, wu, wd):
        pl.run_scoped(functools.partial(forward, wg, wu, wd), *forward_scratch)
        pl.run_scoped(
            functools.partial(feed_forward, wg, wu, wd),
            *[pltpu.VMEM((LEN, units), BF16) for _ in range(3)],
        )

    pl.run_scoped(with_weights, *[pltpu.VMEM(ref.shape, BF16) for ref in (wg_in, wu_in, wd_in)])

    for t in turns:
        pl.semaphore_signal(
            free_sem, inc=1, device_id={"narrow": mate(t)}, device_id_type=pl.DeviceIdType.MESH
        )

    def attention(mid, gmid, tok, cos_ref, sin_ref, vaug_ref, aug_ref, dk_ref, dv_ref, *rest):
        px1, px2, own1, own2 = rest[:4]
        add_ring(own1, a1_out, 2)
        add_ring(own2, a2_out, 3)
        group = rest[4:12]
        spare = list(rest[12:])
        w_all = c_l if w_all_in.shape == x_r.shape else spare.pop(0)
        all_ref = x_l if w_all_in.shape == x_r.shape else spare.pop(0)
        first_rows = c_r
        q_ref, k_ref, v_ref, att_ref, qraw_ref, kraw_ref, rinv_ref, wo_ref = group

        load("mid_back", mid_in, mid)

        def load_group(g):
            sources = [*groups_in[g], wo_in_all.at[g * gq : (g + 1) * gq, :]]
            for i, (source, target) in enumerate(zip(sources, group)):
                load(f"group{g}_{i}", source, target)

        def need_group(g):
            need(*[f"group{g}_{i}" for i in range(8)])

        load_group(0)
        load("cos_back", cos_in, cos_ref)
        load("sin_back", sin_in, sin_ref)
        load("rows", rows_in, first_rows)
        load("tok_back", tok_in, tok)

        length = len_ref[n // side]
        ones = group_ones()
        lane = lanes((BLK, TILE))
        width = w_all.shape[1] // groups
        gains = {"q": jnp.zeros((1, TILE), F32), "k": jnp.zeros((1, TILE), F32)}
        causal = causal_mask((BLK, 2 * BLK), 1)

        def turn_back(grad, cosine, sine):
            return grad * cosine - swap_halves(grad) * sine

        def norm_back(raw, turned, scale):
            inv = lax.rsqrt(group_sum(raw * raw, ones) * (1.0 / HD) + EPSILON)
            scaled = turned * scale
            unit = raw * inv
            inner = group_sum(unit * scaled, ones) * (1.0 / HD)
            gain = jnp.sum(turned * unit, axis=0, keepdims=True)
            return inv * (scaled - unit * inner), gain

        def attention_pieces(g):
            base = g * width
            for start in range(0, LEN, BLK):
                rows = slice(start, start + BLK)
                grad = contract(branch[rows, :], wo_ref[...], 1, 1).astype(BF16).astype(F32)
                for t in range(heads):
                    cols = slice(t * TILE, (t + 1) * TILE)
                    part = (grad[:, cols] * rinv_ref[rows, cols]).astype(BF16).astype(F32)
                    inner = group_sum(part * att_ref[rows, cols].astype(F32), ones)
                    for which in range(2):
                        mine = part if which == 0 else pltpu.roll(part, HD, 1)
                        sums = pltpu.roll(inner, HD, 1) if which == 0 else inner
                        high = sums.astype(BF16).astype(F32)
                        tail = jnp.where(
                            lane == HD, -high, jnp.where(lane == HD + 1, high - sums, 0.0)
                        )
                        aug_ref[2 * t + which, rows, :] = jnp.where(lane < HD, mine, tail).astype(
                            BF16
                        )
                for t in range(heads // 2):
                    v_pair = v_ref[rows, t * TILE : (t + 1) * TILE].astype(F32)
                    mark = jnp.where(lane < HD + 2, 1.0, 0.0)
                    vaug_ref[2 * t, rows, :] = jnp.where(lane < HD, v_pair, mark).astype(BF16)
                    vaug_ref[2 * t + 1, rows, :] = jnp.where(
                        lane < HD, pltpu.roll(v_pair, HD, 1), mark
                    ).astype(BF16)
                dk_ref[:, rows, :] = jnp.zeros((heads, BLK, HD), F32)
                dv_ref[:, rows, :] = jnp.zeros((heads, BLK, TILE), F32)
                yield

            for h in range(heads):
                keys_turned = jnp.transpose(
                    k_ref[:, (h // 2) * TILE : (h // 2 + 1) * TILE].astype(F32)
                )[(h % 2) * HD : (h % 2 + 1) * HD].astype(BF16)
                for i in range(LEN // BLK):
                    rows = slice(i * BLK, (i + 1) * BLK)
                    low = h * TILE
                    q_two = jnp.concatenate(
                        [q_ref[rows, low : low + HD], q_ref[rows, low + HD : low + TILE]], axis=0
                    )
                    aug = jnp.concatenate(
                        [aug_ref[2 * h, rows, :], aug_ref[2 * h + 1, rows, :]], axis=0
                    )
                    dq = jnp.zeros((HD, 2 * BLK), F32)
                    for j in range(i + 1):
                        keys = slice(j * BLK, (j + 1) * BLK)
                        weight = jnp.exp(
                            contract(k_ref[keys, h * HD : (h + 1) * HD], q_two, 1, 1)
                        )
                        if i == j:
                            weight = jnp.where(causal, weight, 0.0)
                        slope = (weight * contract(vaug_ref[h, keys, :], aug, 1, 1)).astype(BF16)
                        dv_ref[h, keys, :] += contract(weight.astype(BF16), aug, 1, 0)
                        dk_ref[h, keys, :] += contract(slope, q_two, 1, 0)
                        dq += contract(keys_turned[:, keys], slope, 1, 0)
                    both = jnp.concatenate([dq[:, :BLK], dq[:, BLK:]], axis=0)
                    grad = jnp.transpose(both) * (1.0 / math.sqrt(HD))
                    turned = turn_back(grad, cos_ref[rows, :], sin_ref[rows, :])
                    out, gain = norm_back(qraw_ref[rows, low : low + TILE], turned, qs_ref[...])
                    all_ref[rows, base + low : base + low + TILE] = out.astype(BF16)
                    gains["q"] += gain
                    yield

            for start in range(0, LEN, BLK):
                rows = slice(start, start + BLK)
                real = (lax.broadcasted_iota(jnp.int32, (BLK, TILE), 0) + start) < length
                for t in range(heads // 2):
                    low = base + gq + t * TILE
                    grad = jnp.concatenate(
                        [dk_ref[2 * t, rows, :], dk_ref[2 * t + 1, rows, :]], axis=1
                    )
                    grad = jnp.where(real, grad, 0.0)
                    turned = turn_back(grad, cos_ref[rows, :], sin_ref[rows, :])
                    out, gain = norm_back(
                        kraw_ref[rows, t * TILE : (t + 1) * TILE], turned, ks_ref[...]
                    )
                    all_ref[rows, low : low + TILE] = out.astype(BF16)
                    gains["k"] += gain
                    values = jnp.where(
                        lane < HD,
                        dv_ref[2 * t, rows, :],
                        pltpu.roll(dv_ref[2 * t + 1, rows, :], HD, 1),
                    )
                    all_ref[rows, low + gk : low + gk + TILE] = jnp.where(
                        real, values, 0.0
                    ).astype(BF16)
                yield

        def out_grads(which, target):
            first, size = plan["out_parts"][which]
            target[:size, :] = contract(
                att_ref[:, first : first + size], branch[...], 0, 0
            ).astype(BF16)
            if target.shape[0] > size:
                target[size:, :] = jnp.zeros((target.shape[0] - size, target.shape[1]), BF16)

        def qkv_grads(which, target):
            for start in range(0, depth, BLK):
                rows = slice(start, start + BLK)
                for source, size, to in plan["qkv_parts"][which]:
                    target[rows, to : to + size] = contract(
                        first_rows[:, rows], all_ref[:, source : source + size], 0, 0
                    ).astype(BF16)
                yield

        def gain_copy(step):
            return (f"gain{step}", gain_mine.at[step], gain_in.at[step], partners[step])

        def compute():
            need("mid_back")
            for t in turns:
                received(f"bl{t}", got_bl.at[t - 1], {"narrow": mate(t)})
            tick(rings[0])
            tick(rings[1])
            gain_two = jnp.zeros((1, fg_ref.shape[1]), F32)
            own_branch, own_cot = block(branch, 0), block(c_l, 0)
            for start in range(0, own_rows, 64):
                rows = slice(start, start + 64)
                if start % BLK == 0:
                    received(f"by{start // BLK}", far_b.at[start : start + BLK, :], to_across)
                grad = own_b[rows, :].astype(F32) + far_b[rows, :].astype(F32)
                for t in turns:
                    grad += got_bl[t - 1, rows, :].astype(F32)
                values = mid[rows, :]
                inv = lax.rsqrt(jnp.mean(values * values, axis=1, keepdims=True) + EPSILON)
                unit = values * inv
                scaled = grad * fg_ref[...]
                inner = jnp.mean(unit * scaled, axis=1, keepdims=True)
                total = own_cot[rows, :].astype(F32) + inv * (scaled - unit * inner)
                gmid[rows, :] = total
                own_branch[rows, :] = total.astype(BF16)
                gain_two += jnp.sum(grad * unit, axis=0, keepdims=True)
            load("w_all", w_all_in, w_all)
            gain_mine[0, 1:2, :] = gain_two
            pl.semaphore_wait(free_sem, side - 1)
            to_mates("gb", own_branch, own_branch)
            need_group(0)
            need("cos_back", "sin_back")
            from_mates("gb", branch)
            yield
            out_grads("partner", px2)
            send("o2", px2, rx2, to_across)
            if groups == 1:
                out_grads("own", own2)
            yield
            yield from attention_pieces(0)
            need("rows")
            yield from qkv_grads("partner", px1)
            send("o1", px1, rx1, to_across)
            send("oy", ownr_o, far_o, to_across)
            if groups > 1:
                load_group(1)
            if groups > 1:
                need_group(1)
                out_grads("own", own2)
                yield
                yield from attention_pieces(1)
            yield from qkv_grads("own", own1)
            need("w_all", "tok_back")
            sent("by")
            for turn in [*turns, 0]:
                for start in range(0, own_rows, BLK):
                    at = pl.multiple_of(lax.rem(place + turn, side) * own_rows + start, BLK)
                    grad = contract(all_ref[pl.ds(at, BLK), :], w_all[...], 1, 1).astype(BF16)
                    if turn:
                        send_b[turn - 1, start : start + BLK, :] = grad
                    else:
                        own_b[start : start + BLK, :] = grad
                    yield
                if turn:
                    send(
                        f"gn{turn}", send_b.at[turn - 1], got_gn.at[turn - 1], {"narrow": mate(turn)}
                    )
            for t in turns:
                received(f"gn{t}", got_gn.at[t - 1], {"narrow": mate(t)})
            gain_one = jnp.zeros((1, ng_ref.shape[1]), F32)
            for start in range(0, own_rows, 64):
                rows = slice(start, start + 64)
                grad = own_b[rows, :].astype(F32)
                for t in turns:
                    grad += got_gn[t - 1, rows, :].astype(F32)
                values = tok[rows, :].astype(F32)
                inv = lax.rsqrt(jnp.mean(values * values, axis=1, keepdims=True) + EPSILON)
                unit = values * inv
                scaled = grad * ng_ref[...]
                inner = jnp.mean(unit * scaled, axis=1, keepdims=True)
                gmid[rows, :] += inv * (scaled - unit * inner)
                gain_one += jnp.sum(grad * unit, axis=0, keepdims=True)
            load("grad_tokens", gmid, gt_out)
            gain_mine[0, 0:1, :] = gain_one
            spare = jnp.zeros((1, gain_one.shape[1] - TILE), F32)
            gain_mine[0, 2:3, :] = jnp.concatenate([gains["q"], spare], axis=1)
            gain_mine[0, 3:4, :] = jnp.concatenate([gains["k"], spare], axis=1)
            gain_mine[0, 4:8, :] = jnp.zeros((4, gain_one.shape[1]), F32)
            send(*gain_copy(0))
            yield

        def finish_output():
            for t in turns:
                received(f"ol{t}", got_ol.at[t - 1], {"narrow": mate(t)})
            received("oy", far_o, to_across)
            for start in range(0, own_rows, 64):
                rows = slice(start, start + 64)
                total = mid[rows, :] + own_o[rows, :].astype(F32) + far_o[rows, :].astype(F32)
                for t in turns:
                    total += got_ol[t - 1, rows, :].astype(F32)
                own_o[rows, :] = total.astype(BF16)
            load("output", own_o, out_out)

        def join_partner():
            received("o2", rx2, to_across)
            received("o1", rx1, to_across)
            for mine, theirs in ((own1, rx1), (own2, rx2)):
                tall = mine.shape[0] // 16

                @pl.loop(0, tall)
                def _(r):
                    at = pl.ds(pl.multiple_of(r * 16, 16), 16)
                    mine[at, :] = (mine[at, :].astype(F32) + theirs[at, :].astype(F32)).astype(
                        BF16
                    )

        turn = 0
        order = [1, 0]
        for number, _ in enumerate(compute()):
            if number % 6 == 5:
                tick(rings[order[turn % 2]])
                turn += 1
        early = JOIN_AT * (count - 1) // 7
        while min(ring.done for ring in rings[order[turn % 2]]) < early:
            tick(rings[order[turn % 2]])
            turn += 1
        join_partner()
        for pair in rings[2:]:
            begin(pair)
        step = 0
        while any(ring.left for pair in rings for ring in pair):
            tick(rings[order[turn % 2]])
            turn += 1
            tick(rings[2])
            tick(rings[3])
            if step < len(doubling):
                name, mine, other, device = gain_copy(step)
                received(name, other, device)
                total = gain_mine[step] + gain_in[step]
                if step + 1 < len(doubling):
                    gain_mine[step + 1] = total
                    send(*gain_copy(step + 1))
                else:
                    gains_ref[...] = total
            if step == len(doubling):
                finish_output()
            step += 1
        for pair in rings:
            for ring in pair:
                ring.finish()
        sent("")
        need("output", "grad_tokens")

    scratch = [
        pltpu.VMEM((own_rows, depth), F32),
        pltpu.VMEM((own_rows, depth), F32),
        pltpu.VMEM((own_rows, depth), BF16),
        pltpu.VMEM((LEN, TILE), F32),
        pltpu.VMEM((LEN, TILE), F32),
        pltpu.VMEM((heads, LEN, TILE), BF16),
        pltpu.VMEM((2 * heads, LEN, TILE), BF16),
        pltpu.VMEM((heads, LEN, HD), F32),
        pltpu.VMEM((heads, LEN, TILE), F32),
    ]
    scratch += [pltpu.VMEM(ref.shape, BF16) for ref in (rx1, rx2, rx1, rx2)]
    scratch += [pltpu.VMEM(ref.shape, ref.dtype) for ref in groups_in[0]]
    scratch += [pltpu.VMEM((gq, depth), BF16)]
    if w_all_in.shape != x_r.shape:
        scratch += [pltpu.VMEM(w_all_in.shape, BF16), pltpu.VMEM((LEN, w_all_in.shape[1]), BF16)]
    pl.run_scoped(attention, *scratch)


VM = pl.BlockSpec(memory_space=pltpu.VMEM)
ANY = pl.BlockSpec(memory_space=pl.ANY)
SM = pl.BlockSpec(memory_space=pltpu.SMEM)


def run_main(plan, small, big):
    count, narrow, side = plan["wide"], plan["narrow"], plan["side"]
    shape = jax.ShapeDtypeStruct
    own, depth = big[0].shape
    units = big[3].shape[1]
    nq, nk, groups = plan["nq"], plan["nk"], plan["groups"]
    sizes = [(depth, 2 * units), (units, depth), (depth, nq + 2 * nk), (nq, depth)]
    _, ahead, back = ring_rows(units, count)
    less = [0, 0, (ahead - back) * depth // (2 * sizes[2][1]) // 16 * 16, 0]
    plan = dict(plan, rows=[s[0] for s in sizes], own=own, less=less)
    full, lands = [], []
    for (rows, cols), fewer in zip(sizes, less):
        chunk, forward, backward = ring_rows(rows, count, fewer)
        full.append((chunk * count, cols))
        lands += [pltpu.VMEM((count - 1, r, cols), BF16) for r in (forward, backward) if r]
    plan["lands"] = len(lands)
    steps = 2 * (count - 1)
    doubling = int(math.log2(narrow)) + int(math.log2(count))
    dma = pltpu.SemaphoreType.DMA
    rest = (own, depth)
    mates = (side - 1, own, depth)
    scratch = [pltpu.VMEM((LEN, depth), BF16) for _ in range(4)]
    scratch += [pltpu.VMEM(shape, BF16) for shape in full]
    scratch += lands
    scratch += [pltpu.VMEM(mates, BF16) for _ in range(6)]
    scratch += [pltpu.VMEM(rest, BF16) for _ in range(6)]
    scratch += [pltpu.VMEM((doubling, 8, depth), F32) for _ in range(2)]
    scratch += [pltpu.VMEM((1, TILE), F32) for _ in range(2)]
    parts = own // BLK
    moves = 6 + 4 * parts + (side - 1) * (7 * parts + 5) + doubling
    scratch += [
        dma((80,)),
        dma((len(lands), steps)),
        dma((len(lands), steps)),
        dma,
        dma((moves,)),
        dma((moves,)),
        pltpu.SemaphoreType.REGULAR,
    ]
    gq, gk = 2 * nq // groups, 2 * nk // groups
    kept = [shape(rest, F32), shape((LEN, depth), BF16)]
    kept += [shape((depth, 2 * (nq + 2 * nk)), BF16), shape((2 * nq, depth), BF16)]
    for _ in range(groups):
        kept += [shape((LEN, gq), BF16), shape((LEN, gk), BF16), shape((LEN, gk), BF16)]
        kept += [shape((LEN, gq), BF16), shape((LEN, gq), F32), shape((LEN, gk), F32)]
        kept += [shape((LEN, gq), F32)]
    results = pl.pallas_call(
        functools.partial(main_kernel, plan),
        out_shape=tuple(shape(s, BF16) for s in full)
        + (shape(rest, BF16), shape(rest, F32), *kept, shape((8, depth), F32)),
        in_specs=[SM] + [VM] * 4 + [ANY] * len(big),
        out_specs=[ANY] * (6 + len(kept)) + [VM],
        scratch_shapes=scratch,
        compiler_params=pltpu.CompilerParams(
            vmem_limit_bytes=BACK_LIMIT, collective_id=1, has_side_effects=True
        ),
        cost_estimate=pl.CostEstimate(
            flops=60 * 10**9, bytes_accessed=64 * 1024 * 1024, transcendentals=0
        ),
        name="main",
    )(*small, *big)
    return [r[: s[0]] for r, s in zip(results[:4], sizes)] + [*results[4:6], results[-1]]


def widen_kernel(nq, nk, units, gu, gd, a1, a2, rows, grads, gains, *outs):
    *outs, rows_out, grads_out = outs
    rows_out[...] = rows[...]
    grads_out[...] = grads[...]
    q_out, k_out, v_out, out_out, gate_out, up_out, down_out, ng_out, fg_out, qs_out, ks_out = outs
    q_out[...] = a1[:, :nq].astype(F32)
    k_out[...] = a1[:, nq : nq + nk].astype(F32)
    v_out[...] = a1[:, nq + nk :].astype(F32)
    out_out[...] = a2[...].astype(F32)
    gate_out[...] = gu[:, :units].astype(F32)
    up_out[...] = gu[:, units:].astype(F32)
    down_out[...] = gd[...].astype(F32)
    ng_out[...] = gains[0:1, :]
    fg_out[...] = gains[1:2, :]
    qs_out[...] = gains[2:3, :HD] + gains[2:3, HD:TILE]
    ks_out[...] = gains[3:4, :HD] + gains[3:4, HD:TILE]


def widen(nq, nk, gu, gd, a1, a2, rows, grads, gains):
    units, depth = gd.shape
    steps = next(n for n in (8, 4, 2, 1) if all(a.shape[0] % (16 * n) == 0 for a in (gu, gd, a1, a2)))

    def tall(rows, cols):
        return pl.BlockSpec((rows // steps, cols), lambda i: (i, 0))

    def whole(rows, cols):
        return pl.BlockSpec((rows, cols), lambda i: (0, 0))

    shapes = [(depth, nq), (depth, nk), (depth, nk), a2.shape, (depth, units), (depth, units)]
    shapes += [gd.shape]
    ends = [(1, depth), (1, depth), (1, HD), (1, HD)]
    kept = [jax.ShapeDtypeStruct(a.shape, a.dtype) for a in (rows, grads)]
    return pl.pallas_call(
        functools.partial(widen_kernel, nq, nk, units),
        grid=(steps,),
        out_shape=tuple(jax.ShapeDtypeStruct(s, F32) for s in shapes + ends) + tuple(kept),
        in_specs=[tall(*a.shape) for a in (gu, gd, a1, a2, rows, grads)] + [whole(*gains.shape)],
        out_specs=[tall(*s) for s in shapes]
        + [whole(*s) for s in ends]
        + [tall(*a.shape) for a in kept],
        compiler_params=pltpu.CompilerParams(vmem_limit_bytes=BACK_LIMIT),
        name="widen",
    )(gu, gd, a1, a2, rows, grads, gains)


def on_device(
    wide, narrow,
    tokens, lengths, norm_gain, w_query, w_key, w_value, query_scale, key_scale, w_out,
    ffn_gain, w_gate, w_up, w_down, cotangent,
):
    sequences = lengths.shape[0]
    side = narrow // sequences
    cosine, sine = rope_tables(LEN, HD)
    cosine = jnp.asarray(np.concatenate([cosine] * 4, axis=1))
    sine = jnp.asarray(np.concatenate([-sine, sine, -sine, sine], axis=1))

    nq, nk = w_query.shape[1], w_key.shape[1]
    sources = (w_query, w_key, w_value)
    if nk % TILE:
        groups = 1
        sources = (jnp.concatenate(sources, axis=1),)
        qkv_parts = {
            "own": [(0, nq, 0), (2 * nq, nk, nq), (2 * nq + 2 * nk, nk, nq + nk)],
            "partner": [
                (nq, nq, 0), (2 * nq + nk, nk, nq), (2 * nq + 3 * nk, nk, nq + nk)
            ],
        }
        out_parts = {"own": (0, nq), "partner": (nq, nq)}
    else:
        groups = 2
        qkv_parts = {
            "partner": [(0, nq + 2 * nk, 0)],
            "own": [(nq + 2 * nk, nq + 2 * nk, 0)],
        }
        out_parts = {"partner": (0, nq), "own": (0, nq)}
    plan = {
        "wide": wide, "narrow": narrow, "side": side, "groups": groups, "nq": nq, "nk": nk,
        "qkv_parts": qkv_parts, "out_parts": out_parts, "qkv_sources": len(sources),
    }
    sum_gu, sum_down, sum_qkv, sum_out, output, grad_tokens, gains = run_main(
        plan,
        (lengths, query_scale[None, :], key_scale[None, :], norm_gain[None, :], ffn_gain[None, :]),
        (tokens, cotangent, w_out, w_gate, w_up, w_down, cosine, sine, *sources),
    )
    query, key, value, out, gate, up, down, norm_g, ffn_g, query_s, key_s, output, grad_tokens = widen(
        nq, nk, sum_gu, sum_down, sum_qkv, sum_out, output, grad_tokens, gains
    )
    return (
        output, grad_tokens, norm_g[0], query, key, value, query_s[0], key_s[0], out, ffn_g[0],
        gate, up, down,
    )


def solution(mesh):
    rows = P(("wide", "narrow"), None)
    columns, depth, copied = P(None, "narrow"), P("narrow", None), P()
    return jax.shard_map(
        functools.partial(on_device, mesh.shape["wide"], mesh.shape["narrow"]),
        mesh=mesh,
        in_specs=(
            rows, P("wide"), copied, columns, columns, columns, copied, copied, depth,
            copied, columns, columns, depth, rows,
        ),
        out_specs=(
            rows, rows, copied, columns, columns, columns, copied, copied, depth,
            copied, columns, columns, depth,
        ),
        check_vma=False,
    )
```
